32 devices in a mesh: fsdp: 32 (over z, y, x, core).
Axes of the slice: x: 2, y: 2, z: 4, core: 2. Of those that a mesh axis runs over, the one named last changes fastest.
Arguments:
- tokens: bfloat16 [32768, 768], P('fsdp'), may hold values from -6 to 6
- mask_bits: int32 [32768], P('fsdp'), may hold values from 0 to 1, as said below
- pad_flags: int32 [128], P('fsdp'), may hold values from 0 to 1, as said below
- ln1_gain: bfloat16 [768], P('fsdp'), may hold values from 0.5 to 1.5
- ln1_bias: bfloat16 [768], P('fsdp'), may hold values from -3 to 3
- qkv_weight: bfloat16 [768, 2304], P('fsdp'), may hold values from -0.21875 to 0.21875
- qkv_bias: bfloat16 [2304], P('fsdp'), may hold values from -3 to 3
- proj_weight: bfloat16 [768, 768], P('fsdp'), may hold values from -0.875 to 0.875
- proj_bias: bfloat16 [768], P('fsdp'), may hold values from -3 to 3
- ln2_gain: bfloat16 [768], P('fsdp'), may hold values from 0.5 to 1.5
- ln2_bias: bfloat16 [768], P('fsdp'), may hold values from -3 to 3
- fc1_weight: bfloat16 [768, 3072], P('fsdp'), may hold values from -0.21875 to 0.21875
- fc1_bias: bfloat16 [3072], P('fsdp'), may hold values from -3 to 3
- fc2_weight: bfloat16 [3072, 768], P('fsdp'), may hold values from -0.21875 to 0.21875
- fc2_bias: bfloat16 [768], P('fsdp'), may hold values from -3 to 3
- mask_embed: bfloat16 [768], P('fsdp'), may hold values from -4 to 4
- out_grad: bfloat16 [32768, 768], P('fsdp'), may hold values from -6 to 6
Outputs:
- block_out: bfloat16 [32768, 768], P('fsdp')
- input_grad: float32 [32768, 768], P('fsdp')
- grad_ln1_gain: float32 [768], P('fsdp')
- grad_ln1_bias: float32 [768], P('fsdp')
- grad_qkv_weight: float32 [768, 2304], P('fsdp')
- grad_qkv_bias: float32 [2304], P('fsdp')
- grad_proj_weight: float32 [768, 768], P('fsdp')
- grad_proj_bias: float32 [768], P('fsdp')
- grad_ln2_gain: float32 [768], P('fsdp')
- grad_ln2_bias: float32 [768], P('fsdp')
- grad_fc1_weight: float32 [768, 3072], P('fsdp')
- grad_fc1_bias: float32 [3072], P('fsdp')
- grad_fc2_weight: float32 [3072, 768], P('fsdp')
- grad_fc2_bias: float32 [768], P('fsdp')
- grad_mask_embed: float32 [768], P('fsdp')
The draws below stay inside these ranges and needn't reach their ends.
Inputs may be any that keep to these rules, and one draw needn't show every extreme that they name: `mask_bits`: each clip of 16 frames masks its tokens independently with one rate of its own between one half and one. `pad_flags`: in each clip of 16 frames the flagged frames are its last ones, at least one and at most half of the clip, a count of its own.
All inputs are finite; a program needn't handle non-finite values.
Results may differ from the reference program's by a relative error of at most 0.012.
Values may be sent and summed in bfloat16 or wider, within the bound.
A program may use at most 192 MiB of HBM per device.

```python
import jax
import jax.numpy as jnp
from jax import lax

D = 768
HEADS = 12
HEAD_DIM = 64
FF = 3072
WIN = 256
CLIP_FRAMES = 16
FRAMES = 128
TOKENS = 32768


def draw_mask_bits(key, part):
    key = jax.random.fold_in(key, 11)
    clips = FRAMES // CLIP_FRAMES
    ratio = jax.random.randint(jax.random.fold_in(key, 1), (clips, 1), 512, 1025)
    picks = jax.random.randint(jax.random.fold_in(key, 2), (clips, CLIP_FRAMES * WIN), 0, 1024)
    return (picks < ratio).astype(jnp.int32).reshape(FRAMES * WIN)


def draw_pad_flags(key, part):
    key = jax.random.fold_in(key, 23)
    clips = FRAMES // CLIP_FRAMES
    padding = jax.random.randint(key, (clips, 1), 1, CLIP_FRAMES // 2 + 1)
    places = jnp.arange(CLIP_FRAMES, dtype=jnp.int32)[None, :]
    return (places >= CLIP_FRAMES - padding).astype(jnp.int32).reshape(FRAMES)


def levels(rng, dims, pieces, smallest, largest):
    gain = 1.0
    for axis_at, parts in pieces:
        steps = jax.random.uniform(jax.random.fold_in(jax.random.fold_in(rng, 6), axis_at), (parts,), jnp.float32, smallest / len(pieces), largest / len(pieces))
        gain = gain * jnp.repeat(jnp.exp(steps), dims[axis_at] // parts).reshape((-1,) + (1,) * (len(dims) - 1 - axis_at))
    return gain


def bell_draw(stream_key, extent, deviation, most, split=(), held_as=jnp.bfloat16):
    factor_of = levels(stream_key, extent, split, -0.22, 0.18) if split else 1.0
    array = jax.random.normal(stream_key, extent, jnp.float32) * deviation * factor_of
    return jnp.minimum(jnp.maximum(array, -most), most).astype(held_as)


def setup_inputs(seed: int = 0) -> dict:
    seeds = jax.random.split(jax.random.key(seed), 18)
    tokens = bell_draw(seeds[0], (TOKENS, D), 1.0, 6.0, ((0, 32),))
    mask_bits = draw_mask_bits(jax.random.fold_in(seeds[17], 71), 0)
    pad_flags = draw_pad_flags(jax.random.fold_in(seeds[17], 71), 0)
    ln1_gain = jnp.clip(1.0 + 0.1 * jax.random.normal(seeds[3], (D,), jnp.float32), 0.5, 1.5).astype(jnp.bfloat16)
    ln1_bias = bell_draw(seeds[4], (D,), 0.3, 3.0, ((0, 32),))
    qkv_weight = bell_draw(seeds[5], (D, 3 * D), D ** -0.5, 0.21875, ((0, 32),))
    qkv_bias = bell_draw(seeds[6], (3 * D,), 0.3, 3.0, ((0, 32),))
    proj_weight = bell_draw(seeds[7], (D, D), (D // 16) ** -0.5, 0.875, ((0, 32),))
    proj_bias = bell_draw(seeds[8], (D,), 0.3, 3.0, ((0, 32),))
    ln2_gain = jnp.clip(1.0 + 0.1 * jax.random.normal(seeds[9], (D,), jnp.float32), 0.5, 1.5).astype(jnp.bfloat16)
    ln2_bias = bell_draw(seeds[10], (D,), 0.3, 3.0, ((0, 32),))
    fc1_weight = bell_draw(seeds[11], (D, FF), D ** -0.5, 0.21875, ((0, 32),))
    fc1_bias = bell_draw(seeds[12], (FF,), 0.3, 3.0, ((0, 32),))
    fc2_weight = bell_draw(seeds[13], (FF, D), (FF // 4) ** -0.5, 0.21875, ((0, 32),))
    fc2_bias = bell_draw(seeds[14], (D,), 0.3, 3.0, ((0, 32),))
    mask_embed = bell_draw(seeds[15], (D,), 1.0, 4.0, ((0, 32),))
    out_grad = bell_draw(seeds[16], (TOKENS, D), 1.0, 6.0, ((0, 32),))
    return dict(tokens=tokens, mask_bits=mask_bits, pad_flags=pad_flags, ln1_gain=ln1_gain, ln1_bias=ln1_bias, qkv_weight=qkv_weight, qkv_bias=qkv_bias, proj_weight=proj_weight, proj_bias=proj_bias, ln2_gain=ln2_gain, ln2_bias=ln2_bias, fc1_weight=fc1_weight, fc1_bias=fc1_bias, fc2_weight=fc2_weight, fc2_bias=fc2_bias, mask_embed=mask_embed, out_grad=out_grad)


@jax.custom_vjp
def low(v):
    return lax.optimization_barrier(v.astype(jnp.bfloat16)).astype(jnp.float32)

@jax.custom_vjp
def low_back(v):
    return v

def low_keep(v):
    return (low(v), None)

def low_pass(kept, grad):
    return (grad,)

def back_keep(v):
    return (v, None)

def back_low(kept, grad):
    return (low(grad),)
low.defvjp(low_keep, low_pass)
low_back.defvjp(back_keep, back_low)
epsilon = 1e-06

def norm_rows(values, gain_vec, shift_vec):
    row_mean = lax.optimization_barrier(jnp.mean(values, axis=-1, keepdims=True))
    centered = values - row_mean
    variance = lax.optimization_barrier(jnp.mean(centered * centered, axis=-1, keepdims=True))
    return centered * lax.rsqrt(variance + epsilon) * gain_vec + shift_vec

def gelu_exact(values):
    return jax.nn.gelu(values, approximate=False)

def block_forward(params, tok_rows, masked):
    gain_one, shift_one, qkv_w, qkv_b, proj_w, proj_b, gain_two, shift_two, up_w, up_b, down_w, down_b, mask_vec = params
    highest = lax.Precision.HIGHEST
    row_count = tok_rows.shape[0]
    frames = row_count // WIN
    mixed_in = jnp.where(masked[:, None] > 0, mask_vec[None, :], tok_rows)
    normed = low(norm_rows(mixed_in, gain_one, shift_one))
    packed = low_back(low(jnp.dot(normed, qkv_w, precision=highest) + qkv_b))
    heads_view = packed.reshape(frames, WIN, 3, HEADS, HEAD_DIM)
    query_part = heads_view[:, :, 0]
    key_part = heads_view[:, :, 1]
    value_part = heads_view[:, :, 2]
    scores = low_back(jnp.einsum('fqhd,fkhd->fhqk', query_part, key_part, precision=highest) * HEAD_DIM ** (-0.5))
    row_max = lax.optimization_barrier(jnp.max(scores, axis=-1, keepdims=True))
    exp_terms = jnp.exp(scores - row_max)
    probs_low = low(exp_terms / lax.optimization_barrier(jnp.sum(exp_terms, axis=-1, keepdims=True)))
    attended = jnp.einsum('fhqk,fkhd->fqhd', probs_low, value_part, precision=highest).reshape(row_count, HEADS * HEAD_DIM)
    attended = low_back(low(attended))
    branch = low_back(jnp.dot(attended, proj_w, precision=highest) + proj_b)
    middle = mixed_in + branch
    normed_two = low(norm_rows(middle, gain_two, shift_two))
    hidden_pre = low_back(jnp.dot(normed_two, up_w, precision=highest) + up_b)
    hidden_act = low(gelu_exact(hidden_pre))
    branch_two = low_back(jnp.dot(hidden_act, down_w, precision=highest) + down_b)
    return middle + branch_two

def reference(tokens, mask_bits, pad_flags, ln1_gain, ln1_bias, qkv_weight, qkv_bias, proj_weight, proj_bias, ln2_gain, ln2_bias, fc1_weight, fc1_bias, fc2_weight, fc2_bias, mask_embed, out_grad):
    params = tuple((item.astype(jnp.float32) for item in (ln1_gain, ln1_bias, qkv_weight, qkv_bias, proj_weight, proj_bias, ln2_gain, ln2_bias, fc1_weight, fc1_bias, fc2_weight, fc2_bias, mask_embed)))
    frames_group = 16
    groups = FRAMES // frames_group
    row_count = frames_group * WIN
    frame_keep = (1 - pad_flags).astype(jnp.float32)
    tok_weight = (mask_bits.astype(jnp.float32).reshape(FRAMES, WIN) * frame_keep[:, None]).reshape(FRAMES * WIN)
    cotangent = out_grad.astype(jnp.float32) * tok_weight[:, None]
    group_inputs = (tokens.astype(jnp.float32).reshape(groups, row_count, D), mask_bits.reshape(groups, row_count), cotangent.reshape(groups, row_count, D))

    def group_step(totals, group_data):
        tok_rows, masked, group_cot = group_data
        result, pullback = jax.vjp(lambda prm, rows_in: block_forward(prm, rows_in, masked), params, tok_rows)
        param_grads, tok_grad = pullback(group_cot)
        return (jax.tree.map(jnp.add, totals, param_grads), (result.astype(jnp.bfloat16), tok_grad))
    zero_grads = jax.tree.map(jnp.zeros_like, params)
    totals, (results, tok_grads) = lax.scan(group_step, zero_grads, group_inputs)
    block_out = results.reshape(FRAMES * WIN, D)
    input_grad = tok_grads.reshape(FRAMES * WIN, D)
    return (block_out, input_grad, totals[0], totals[1], totals[2], totals[3], totals[4], totals[5], totals[6], totals[7], totals[8], totals[9], totals[10], totals[11], totals[12])
```

```python
import functools

import jax
import jax.numpy as jnp
from jax import lax
from jax.experimental import pallas as pl
from jax.experimental.pallas import tpu as pltpu
from jax.sharding import PartitionSpec as P

HEADS = 12
HEAD_DIM = 64
WIN = 256


epsilon = 1e-06


def norm_rows(values, gain_vec, shift_vec):
    row_mean = jnp.mean(values, axis=-1, keepdims=True)
    centered = values - row_mean
    variance = jnp.mean(centered * centered, axis=-1, keepdims=True)
    return centered * lax.rsqrt(variance + epsilon) * gain_vec + shift_vec


def gelu_exact(values):
    return jax.nn.gelu(values, approximate=False)


def forward_pass(full, tok_rows, masked):
    (
        gain_one,
        shift_one,
        qkv_w,
        qkv_b,
        proj_w,
        proj_b,
        gain_two,
        shift_two,
        up_w,
        up_b,
        down_w,
        down_b,
        mask_vec,
    ) = full
    row_count = tok_rows.shape[0]
    width = tok_rows.shape[1]
    frames = row_count // WIN
    mixed_in = jnp.where(
        masked[:, None] > 0, mask_vec.astype(jnp.float32)[None, :], tok_rows.astype(jnp.float32)
    )
    normed = norm_rows(
        mixed_in, gain_one.astype(jnp.float32), shift_one.astype(jnp.float32)
    ).astype(jnp.bfloat16)
    packed = (
        jnp.dot(normed, qkv_w, preferred_element_type=jnp.float32) + qkv_b.astype(jnp.float32)
    ).astype(jnp.bfloat16)
    heads_view = packed.reshape(frames, WIN, 3, HEADS, HEAD_DIM)
    scores = jnp.einsum(
        "fqhd,fkhd->fhqk",
        heads_view[:, :, 0],
        heads_view[:, :, 1],
        preferred_element_type=jnp.float32,
    ) * HEAD_DIM ** (-0.5)
    row_max = jnp.max(scores, axis=-1, keepdims=True)
    exp_terms = jnp.exp(scores - row_max)
    row_total = jnp.sum(exp_terms, axis=-1, keepdims=True)
    probs_low = (exp_terms / row_total).astype(jnp.bfloat16)
    log_total = row_max + jnp.log(row_total)
    attended = jnp.einsum(
        "fhqk,fkhd->fqhd", probs_low, heads_view[:, :, 2], preferred_element_type=jnp.float32
    )
    attended = attended.reshape(row_count, width).astype(jnp.bfloat16)
    middle = (
        mixed_in
        + jnp.dot(attended, proj_w, preferred_element_type=jnp.float32)
        + proj_b.astype(jnp.float32)
    )
    normed_two = norm_rows(
        middle, gain_two.astype(jnp.float32), shift_two.astype(jnp.float32)
    ).astype(jnp.bfloat16)
    hidden_pre = jnp.dot(normed_two, up_w, preferred_element_type=jnp.float32) + up_b.astype(
        jnp.float32
    )
    hidden_act = gelu_exact(hidden_pre).astype(jnp.bfloat16)
    result = (
        middle
        + jnp.dot(hidden_act, down_w, preferred_element_type=jnp.float32)
        + down_b.astype(jnp.float32)
    )
    saved = (
        mixed_in,
        normed,
        packed,
        log_total,
        attended,
        middle,
        normed_two,
        hidden_pre,
        hidden_act,
    )
    return (result, saved)


def mlp_backward(full, saved, cotangent):
    (
        gain_one,
        shift_one,
        qkv_w,
        qkv_b,
        proj_w,
        proj_b,
        gain_two,
        shift_two,
        up_w,
        up_b,
        down_w,
        down_b,
        mask_vec,
    ) = full
    mixed_in, normed, packed, log_total, attended, middle, normed_two, hidden_pre, hidden_act = (
        saved
    )
    down_in = cotangent.astype(jnp.bfloat16)
    grad_down = jnp.einsum("tf,td->fd", hidden_act, down_in, preferred_element_type=jnp.float32)
    grad_down_b = jnp.sum(down_in.astype(jnp.float32), axis=0)
    grad_act = jnp.einsum("td,fd->tf", down_in, down_w, preferred_element_type=jnp.float32)
    gelu_value, gelu_pull = jax.vjp(gelu_exact, hidden_pre)
    grad_pre = gelu_pull(grad_act)[0].astype(jnp.bfloat16)
    grad_up = jnp.einsum("td,tf->df", normed_two, grad_pre, preferred_element_type=jnp.float32)
    grad_up_b = jnp.sum(grad_pre.astype(jnp.float32), axis=0)
    grad_norm_two = jnp.einsum("tf,df->td", grad_pre, up_w, preferred_element_type=jnp.float32)
    norm_value, norm_pull = jax.vjp(
        norm_rows, middle, gain_two.astype(jnp.float32), shift_two.astype(jnp.float32)
    )
    grad_middle, grad_gain_two, grad_shift_two = norm_pull(grad_norm_two)
    grad_middle = grad_middle + cotangent
    return (
        grad_middle,
        (grad_gain_two, grad_shift_two, grad_up, grad_up_b, grad_down, grad_down_b),
    )


def attn_backward(full, saved, grad_middle, masked):
    (
        gain_one,
        shift_one,
        qkv_w,
        qkv_b,
        proj_w,
        proj_b,
        gain_two,
        shift_two,
        up_w,
        up_b,
        down_w,
        down_b,
        mask_vec,
    ) = full
    mixed_in, normed, packed, log_total, attended, middle, normed_two, hidden_pre, hidden_act = (
        saved
    )
    row_count = grad_middle.shape[0]
    width = grad_middle.shape[1]
    frames = row_count // WIN
    proj_in = grad_middle.astype(jnp.bfloat16)
    grad_proj = jnp.einsum("td,te->de", attended, proj_in, preferred_element_type=jnp.float32)
    grad_proj_b = jnp.sum(proj_in.astype(jnp.float32), axis=0)
    grad_att = jnp.einsum("te,de->td", proj_in, proj_w, preferred_element_type=jnp.float32).astype(
        jnp.bfloat16
    )
    grad_att = grad_att.reshape(frames, WIN, HEADS, HEAD_DIM)
    heads_view = packed.reshape(frames, WIN, 3, HEADS, HEAD_DIM)
    query_part = heads_view[:, :, 0]
    key_part = heads_view[:, :, 1]
    value_part = heads_view[:, :, 2]
    score_scale = HEAD_DIM ** (-0.5)
    scores = (
        jnp.einsum("fqhd,fkhd->fhqk", query_part, key_part, preferred_element_type=jnp.float32)
        * score_scale
    )
    probs_full = jnp.exp(scores - log_total)
    probs_low = probs_full.astype(jnp.bfloat16)
    grad_value = jnp.einsum(
        "fhqk,fqhd->fkhd", probs_low, grad_att, preferred_element_type=jnp.float32
    )
    grad_probs = jnp.einsum(
        "fqhd,fkhd->fhqk", grad_att, value_part, preferred_element_type=jnp.float32
    )
    row_dot = jnp.sum(grad_probs * probs_full, axis=-1, keepdims=True)
    grad_scores = (probs_full * (grad_probs - row_dot)).astype(jnp.bfloat16)
    grad_query = (
        jnp.einsum("fhqk,fkhd->fqhd", grad_scores, key_part, preferred_element_type=jnp.float32)
        * score_scale
    )
    grad_key = (
        jnp.einsum("fhqk,fqhd->fkhd", grad_scores, query_part, preferred_element_type=jnp.float32)
        * score_scale
    )
    grad_packed = (
        jnp.stack([grad_query, grad_key, grad_value], axis=2)
        .reshape(row_count, 3 * width)
        .astype(jnp.bfloat16)
    )
    grad_qkv = jnp.einsum("td,te->de", normed, grad_packed, preferred_element_type=jnp.float32)
    grad_qkv_b = jnp.sum(grad_packed.astype(jnp.float32), axis=0)
    grad_normed = jnp.einsum("te,de->td", grad_packed, qkv_w, preferred_element_type=jnp.float32)
    first_value, first_pull = jax.vjp(
        norm_rows, mixed_in, gain_one.astype(jnp.float32), shift_one.astype(jnp.float32)
    )
    grad_mixed, grad_gain_one, grad_shift_one = first_pull(grad_normed)
    grad_mixed = grad_mixed + grad_middle
    chosen = masked[:, None] > 0
    tok_grad = jnp.where(chosen, 0.0, grad_mixed)
    grad_mask = jnp.sum(jnp.where(chosen, grad_mixed, 0.0), axis=0)
    return (
        tok_grad,
        (grad_gain_one, grad_shift_one, grad_qkv, grad_qkv_b, grad_proj, grad_proj_b, grad_mask),
    )


def per_device(
    tokens,
    mask_bits,
    pad_flags,
    ln1_gain,
    ln1_bias,
    qkv_weight,
    qkv_bias,
    proj_weight,
    proj_bias,
    ln2_gain,
    ln2_bias,
    fc1_weight,
    fc1_bias,
    fc2_weight,
    fc2_bias,
    mask_embed,
    out_grad,
):
    full = (
        lax.all_gather(ln1_gain, "fsdp", axis=0, tiled=True),
        lax.all_gather(ln1_bias, "fsdp", axis=0, tiled=True),
        lax.all_gather(qkv_weight, "fsdp", axis=0, tiled=True),
        lax.all_gather(qkv_bias, "fsdp", axis=0, tiled=True),
        lax.all_gather(proj_weight, "fsdp", axis=0, tiled=True),
        lax.all_gather(proj_bias, "fsdp", axis=0, tiled=True),
        lax.all_gather(ln2_gain, "fsdp", axis=0, tiled=True),
        lax.all_gather(ln2_bias, "fsdp", axis=0, tiled=True),
        lax.all_gather(fc1_weight, "fsdp", axis=0, tiled=True),
        lax.all_gather(fc1_bias, "fsdp", axis=0, tiled=True),
        lax.all_gather(fc2_weight, "fsdp", axis=0, tiled=True),
        lax.all_gather(fc2_bias, "fsdp", axis=0, tiled=True),
        lax.all_gather(mask_embed, "fsdp", axis=0, tiled=True),
    )
    result, saved = forward_pass(full, tokens, mask_bits)
    full_back = (
        lax.all_gather(ln1_gain, "fsdp", axis=0, tiled=True),
        lax.all_gather(ln1_bias, "fsdp", axis=0, tiled=True),
        lax.all_gather(qkv_weight, "fsdp", axis=0, tiled=True),
        lax.all_gather(qkv_bias, "fsdp", axis=0, tiled=True),
        lax.all_gather(proj_weight, "fsdp", axis=0, tiled=True),
        lax.all_gather(proj_bias, "fsdp", axis=0, tiled=True),
        lax.all_gather(ln2_gain, "fsdp", axis=0, tiled=True),
        lax.all_gather(ln2_bias, "fsdp", axis=0, tiled=True),
        lax.all_gather(fc1_weight, "fsdp", axis=0, tiled=True),
        lax.all_gather(fc1_bias, "fsdp", axis=0, tiled=True),
        lax.all_gather(fc2_weight, "fsdp", axis=0, tiled=True),
        lax.all_gather(fc2_bias, "fsdp", axis=0, tiled=True),
        lax.all_gather(mask_embed, "fsdp", axis=0, tiled=True),
    )
    kept_acts = forward_pass(full_back, tokens, mask_bits)[1]
    row_count = tokens.shape[0]
    frames = row_count // WIN
    frame_keep = (1 - pad_flags).astype(jnp.float32)
    tok_weight = (mask_bits.astype(jnp.float32).reshape(frames, WIN) * frame_keep[:, None]).reshape(
        row_count
    )
    cotangent = out_grad.astype(jnp.float32) * tok_weight[:, None]
    grad_middle, mlp_grads = mlp_backward(full_back, kept_acts, cotangent)
    tok_grad, attn_grads = attn_backward(full_back, kept_acts, grad_middle, mask_bits)
    shares = (
        lax.psum_scatter(attn_grads[0], "fsdp", scatter_dimension=0, tiled=True),
        lax.psum_scatter(attn_grads[1], "fsdp", scatter_dimension=0, tiled=True),
        lax.psum_scatter(attn_grads[2], "fsdp", scatter_dimension=0, tiled=True),
        lax.psum_scatter(attn_grads[3], "fsdp", scatter_dimension=0, tiled=True),
        lax.psum_scatter(attn_grads[4], "fsdp", scatter_dimension=0, tiled=True),
        lax.psum_scatter(attn_grads[5], "fsdp", scatter_dimension=0, tiled=True),
        lax.psum_scatter(mlp_grads[0], "fsdp", scatter_dimension=0, tiled=True),
        lax.psum_scatter(mlp_grads[1], "fsdp", scatter_dimension=0, tiled=True),
        lax.psum_scatter(mlp_grads[2], "fsdp", scatter_dimension=0, tiled=True),
        lax.psum_scatter(mlp_grads[3], "fsdp", scatter_dimension=0, tiled=True),
        lax.psum_scatter(mlp_grads[4], "fsdp", scatter_dimension=0, tiled=True),
        lax.psum_scatter(mlp_grads[5], "fsdp", scatter_dimension=0, tiled=True),
        lax.psum_scatter(attn_grads[6], "fsdp", scatter_dimension=0, tiled=True),
    )
    return (
        result.astype(jnp.bfloat16),
        tok_grad,
        shares[0],
        shares[1],
        shares[2],
        shares[3],
        shares[4],
        shares[5],
        shares[6],
        shares[7],
        shares[8],
        shares[9],
        shares[10],
        shares[11],
        shares[12],
    )


F32 = jnp.float32
BF16 = jnp.bfloat16
LANES = 128
ROWS = 48
COLS = 384
PIECES = 12
RING = 4
MESH_ID = pl.DeviceIdType.MESH


def dot_nn(a, b):
    return lax.dot_general(a, b, (((1,), (0,)), ((), ())), preferred_element_type=F32)


def dot_nt(a, b):
    return lax.dot_general(a, b, (((1,), (1,)), ((), ())), preferred_element_type=F32)


def dot_tn(a, b):
    return lax.dot_general(a, b, (((0,), (0,)), ((), ())), preferred_element_type=F32)


def row_stats(values):
    row_mean = jnp.mean(values, axis=-1, keepdims=True)
    centered = values - row_mean
    return row_mean, lax.rsqrt(jnp.mean(centered * centered, axis=-1, keepdims=True) + epsilon)


def gelu_and_slope(x):
    phi = 0.5 + 0.5 * lax.erf(x * 0.7071067811865476)
    return x * phi, phi + x * jnp.exp(x * x * -0.5) * 0.3989422804014327


def norm_backward(x, row_mean, row_scale, grad, gain):
    x_hat = (x - row_mean) * row_scale
    prod = grad * x_hat
    grad_gain = jnp.sum(prod, axis=0, keepdims=True)
    grad_shift = jnp.sum(grad, axis=0, keepdims=True)
    dx = grad * gain
    mean_one = jnp.mean(dx, axis=-1, keepdims=True)
    mean_two = jnp.mean(dx * x_hat, axis=-1, keepdims=True)
    return row_scale * (dx - mean_one - x_hat * mean_two), grad_gain, grad_shift


SMALL_ROWS = (
    ("ln1_gain", 0, 0, 24),
    ("ln1_bias", 0, 24, 24),
    ("proj_bias", 0, 48, 24),
    ("ln2_gain", 0, 72, 24),
    ("ln2_bias", 0, 96, 24),
    ("fc2_bias", 1, 0, 24),
    ("mask_embed", 1, 24, 24),
    ("qkv_bias", 1, 48, 72),
    ("fc1_bias", 2, 0, 96),
)


def spread_tables(lane0, width):
    count = 32 * width
    k = lax.broadcasted_iota(jnp.int32, (1, count), 1)
    pick = lax.broadcasted_iota(jnp.int32, (LANES, count), 0) == lax.rem(k, width) + lane0
    owner = lax.broadcasted_iota(jnp.int32, (32, count), 0) == lax.div(k, width)
    return jnp.where(pick, 1.0, 0.0).astype(BF16), owner


SCRATCH = dict(
    tok=((1024, 768), BF16),
    dm=((1024, 768), BF16),
    st=((1024, 8), F32),
    v24=((8, 768), F32),
    bqkv=((1, 2304), F32),
    bfc1=((1, 3072), F32),
    gv=((8, 768), F32),
    gbqkv=((1, 2304), F32),
    gbfc1=((1, 3072), F32),
    normed=((1024, 768), BF16),
    n2=((1024, 768), BF16),
    tr=((768, 1024), BF16),
    packed=((1024, 2304), BF16),
    att=((1024, 768), BF16),
    mid=((1024, 768), F32),
    hact=((1024, 3072), BF16),
    gp=((11, 768, COLS), BF16),
    dn=((1024, 768), F32),
    lse=((24, 8, 256), F32),
    wa=((8, 768, COLS), BF16),
    w1=((8, 768, COLS), BF16),
    w2=((8, 768, COLS), BF16),
    g2=((8, 768, COLS), BF16),
    sv=((4, 4, 2, 16, LANES), BF16),
    sg=((4, 4, 2, 8, LANES), F32),
    tx=((8, 32, COLS), BF16),
    rx=((8, 32, COLS), BF16),
    fs=((8, ROWS, COLS), F32),
    fr=((8, ROWS // 2, COLS), F32),
    l0=((RING, 4, 4, ROWS, COLS), BF16),
    l1=((RING, 2, 2, ROWS, COLS), BF16),
    l2=((RING, 2, 4, ROWS, COLS), BF16),
    l3=((RING, 3, ROWS, COLS), BF16),
    s0=((4, 4, 8, LANES), F32),
    s1=((2, 2, 8, LANES), F32),
    s2=((2, 4, 8, LANES), F32),
    s3=((3, 8, LANES), F32),
)
SEMS = dict(
    ld=pltpu.SemaphoreType.DMA((8,)),
    prep=pltpu.SemaphoreType.DMA((2,)),
    ags=pltpu.SemaphoreType.DMA((PIECES + 1, 8)),
    agr=pltpu.SemaphoreType.DMA((PIECES + 1, 8)),
    rss=pltpu.SemaphoreType.DMA((PIECES + 1, 9)),
    rsr=pltpu.SemaphoreType.DMA((PIECES + 1, 9)),
    credit=pltpu.SemaphoreType.REGULAR((8,)),
)


class Refs:
    pass


def fused_kernel(*refs):
    r = Refs()
    names = ["tok_in", "og_in", "mask", "pad", "small", "sq", "sp", "s1w", "s2w"]
    names += ["bo", "ig", "oq", "op", "o1", "o2", "osm"]
    names += list(SCRATCH) + list(SEMS)
    for name, ref in zip(names, refs):
        setattr(r, name, ref)

    me = lax.axis_index("fsdp")
    core = lax.rem(me, 2)
    other = 1 - core
    chip = lax.div(me, 2)
    xpos = lax.rem(chip, 2)
    ypos = lax.rem(lax.div(chip, 2), 2)
    zpos = lax.div(chip, 4)
    xy = lax.rem(chip, 4)
    xy_x = xy + 1 - 2 * xpos
    xy_y = xy + 2 - 4 * ypos
    xy_d = xy_x + 2 - 4 * ypos
    sib = me + 1 - 2 * core
    x_dev = me + 2 - 4 * xpos
    y_dev = me + 4 - 8 * ypos

    def z_of(k):
        return lax.rem(zpos + k, 4)

    def z_dev(k):
        return me + 8 * (z_of(k) - zpos)

    def remote(src, dst, ssem, rsem, dev):
        return pltpu.make_async_remote_copy(
            src_ref=src,
            dst_ref=dst,
            send_sem=ssem,
            recv_sem=rsem,
            device_id=(dev,),
            device_id_type=MESH_ID,
        )

    wa_v = r.wa.reshape(2, 4, 4, 4, ROWS, COLS)
    w1_v = r.w1.reshape(2, 4, 4, 4, ROWS, COLS)
    w2_v = r.w2.reshape(2, 4, 4, 2, 2, ROWS, COLS)
    w2_shard = r.w2.reshape(2, 4, 4, 2, 2 * ROWS, COLS)
    w2_m = r.w2.reshape(2, 3072, COLS)
    wa_m = r.wa.reshape(2, 4, 768, COLS)
    w1_m = r.w1.reshape(2, 4, 768, COLS)
    g2_v = r.g2.reshape(2, 4, 4, 2, 2, ROWS, COLS)
    g2_m = r.g2.reshape(2, 3072, COLS)
    ga_v = r.gp.reshape(11, 4, 4, ROWS, COLS)
    gp_m = r.gp.reshape(11 * 768, COLS)

    def weight_piece(p, half):
        if p == 0:
            return r.sv.at[:, :, half]
        if p <= 4:
            return wa_v.at[half, p - 1]
        if p <= 8:
            return w1_v.at[half, p - 5]
        return w2_v.at[(p - 9) % 2, :, :, half, (p - 9) // 2]

    def grad_piece(p, half):
        if p == 0:
            return r.sg.at[:, :, half]
        if p <= 4:
            return ga_v.at[half * 4 + p - 1]
        if p <= 8:
            return w1_v.at[half, p - 5]
        return g2_v.at[(p - 9) % 2, :, :, half, (p - 9) // 2]

    def ag_copy(p, i, src, dst, dev):
        return remote(src, dst, r.ags.at[p, i], r.agr.at[p, i], dev)

    def ag_a(p):
        v = weight_piece(p, core)
        for k in (1, 2, 3):
            ag_copy(p, k - 1, v.at[zpos, xy], v.at[zpos, xy], z_dev(k)).start()

    def ag_b(p):
        v = weight_piece(p, core)
        for k in (1, 2, 3):
            came = v.at[z_of(4 - k), xy]
            ag_copy(p, k - 1, came, came, z_dev(k)).wait_recv()
        ag_copy(p, 3, v.at[:, xy], v.at[:, xy], x_dev).start()
        ag_copy(p, 4, v.at[:, xy], v.at[:, xy], y_dev).start()

    def ag_c(p):
        v = weight_piece(p, core)
        ag_copy(p, 3, v.at[:, xy_x], v.at[:, xy_x], x_dev).wait_recv()
        ag_copy(p, 4, v.at[:, xy_y], v.at[:, xy_y], y_dev).wait_recv()
        up, down = pl.ds(0, 2), pl.ds(2, 2)
        ag_copy(p, 5, v.at[down, xy_y], v.at[down, xy_y], x_dev).start()
        ag_copy(p, 6, v.at[up, xy_x], v.at[up, xy_x], y_dev).start()

    def ag_d(p):
        v = weight_piece(p, core)
        up, down = pl.ds(0, 2), pl.ds(2, 2)
        ag_copy(p, 5, v.at[down, xy_d], v.at[down, xy_d], x_dev).wait_recv()
        ag_copy(p, 6, v.at[up, xy_d], v.at[up, xy_d], y_dev).wait_recv()
        ag_copy(p, 7, v, v, sib).start()

    def ag_e(p):
        v = weight_piece(p, other)
        ag_copy(p, 7, v, v, sib).wait_recv()

    def ag_f(p):
        v = weight_piece(p, core)
        up = pl.ds(0, 2)
        for k in (1, 2, 3):
            ag_copy(p, k - 1, v.at[zpos, xy], v.at[zpos, xy], z_dev(k)).wait_send()
        ag_copy(p, 3, v.at[:, xy], v.at[:, xy], x_dev).wait_send()
        ag_copy(p, 4, v.at[:, xy], v.at[:, xy], y_dev).wait_send()
        ag_copy(p, 5, v.at[up, xy_y], v.at[up, xy_y], x_dev).wait_send()
        ag_copy(p, 6, v.at[up, xy_x], v.at[up, xy_x], y_dev).wait_send()
        ag_copy(p, 7, v, v, sib).wait_send()

    ahead = 3

    def ag_step(s):
        if s + ahead <= PIECES:
            ag_a(s + ahead)
        if s <= PIECES:
            ag_b(s)
        if 1 <= s <= PIECES + 1:
            ag_c(s - 1)
        if 2 <= s <= PIECES + 2:
            ag_d(s - 2)

    order = [9, 10, 11, 12, 5, 6, 7, 8, 4, 1, 2, 3, 0]

    def rs_bufs(n):
        if n == PIECES:
            return r.s0, r.s1, r.s2, r.s3
        q = n % RING
        return r.l0.at[q], r.l1.at[q], r.l2.at[q], r.l3.at[q]

    def rs_copy(n, i, src, dst, dev):
        return remote(src, dst, r.rss.at[n, i], r.rsr.at[n, i], dev)

    def credit_wait(n, i):
        if RING <= n < PIECES:
            pl.semaphore_wait(r.credit.at[i], 1)

    def credit_give(n, i, dev):
        if n < PIECES - RING:
            pl.semaphore_signal(r.credit.at[i], inc=1, device_id=(dev,), device_id_type=MESH_ID)

    def add_into(ref, at, landed):
        ref[at] = (ref[at].astype(F32) + landed.astype(F32)).astype(ref.dtype)

    def rs_0(n):
        p = order[n]
        l0 = rs_bufs(n)[0]
        credit_wait(n, 0)
        rs_copy(n, 0, grad_piece(p, other), l0, sib).start()

    def rs_1(n):
        p = order[n]
        l0, l1, l2, l3 = rs_bufs(n)
        g = grad_piece(p, core)
        rs_copy(n, 0, grad_piece(p, other), l0, sib).wait_recv()

        def body(i, carry):
            g[i] = (g[i].astype(F32) + l0[i].astype(F32)).astype(g.dtype)
            return carry

        lax.fori_loop(0, 4, body, 0)
        credit_give(n, 0, sib)
        credit_wait(n, 1)
        rs_copy(n, 1, g.at[pl.ds(2, 2), xy_d], l1.at[0], x_dev).start()
        credit_wait(n, 2)
        rs_copy(n, 2, g.at[pl.ds(0, 2), xy_d], l1.at[1], y_dev).start()

    def rs_2(n):
        p = order[n]
        l0, l1, l2, l3 = rs_bufs(n)
        g = grad_piece(p, core)
        rs_copy(n, 1, g.at[pl.ds(2, 2), xy_d], l1.at[0], x_dev).wait_recv()
        for i in range(2):
            g[2 + i, xy_y] = (g[2 + i, xy_y].astype(F32) + l1[0, i].astype(F32)).astype(g.dtype)
        credit_give(n, 1, x_dev)
        rs_copy(n, 2, g.at[pl.ds(0, 2), xy_d], l1.at[1], y_dev).wait_recv()
        for i in range(2):
            g[i, xy_x] = (g[i, xy_x].astype(F32) + l1[1, i].astype(F32)).astype(g.dtype)
        credit_give(n, 2, y_dev)
        credit_wait(n, 3)
        rs_copy(n, 3, g.at[:, xy_x], l2.at[0], x_dev).start()
        credit_wait(n, 4)
        rs_copy(n, 4, g.at[:, xy_y], l2.at[1], y_dev).start()

    def rs_3(n):
        p = order[n]
        l0, l1, l2, l3 = rs_bufs(n)
        g = grad_piece(p, core)
        rs_copy(n, 3, g.at[:, xy_x], l2.at[0], x_dev).wait_recv()
        rs_copy(n, 4, g.at[:, xy_y], l2.at[1], y_dev).wait_recv()
        for i in range(4):
            g[i, xy] = (
                g[i, xy].astype(F32) + l2[0, i].astype(F32) + l2[1, i].astype(F32)
            ).astype(g.dtype)
        credit_give(n, 3, x_dev)
        credit_give(n, 4, y_dev)
        for k in (1, 2, 3):
            credit_wait(n, 4 + k)
            rs_copy(n, 4 + k, g.at[z_of(k), xy], l3.at[k - 1], z_dev(k)).start()

    def rs_4(n):
        p = order[n]
        l0, l1, l2, l3 = rs_bufs(n)
        g = grad_piece(p, core)
        total = g[zpos, xy].astype(F32)
        for k in (1, 2, 3):
            rs_copy(n, 4 + k, g.at[z_of(k), xy], l3.at[k - 1], z_dev(k)).wait_recv()
            total = total + l3[k - 1].astype(F32)
        for k in (1, 2, 3):
            credit_give(n, 4 + k, z_dev(4 - k))
        if p == 0:
            r.osm[...] = total
        elif p >= 9:
            i, j = (p - 9) // 2, (p - 9) % 2
            r.o2[ROWS * i : ROWS * (i + 1), COLS * j : COLS * (j + 1)] = total
        else:
            r.fs[p - 1] = total
            half = pl.ds(pl.multiple_of(other * 24, 8), 24)
            rs_copy(n, 8, r.fs.at[p - 1, half], r.fr.at[p - 1], sib).start()

    def rs_5(n):
        p = order[n]
        if p == 0 or p >= 9:
            return
        half = pl.ds(pl.multiple_of(other * 24, 8), 24)
        mine = pl.ds(pl.multiple_of(core * 24, 8), 24)
        rs_copy(n, 8, r.fs.at[p - 1, half], r.fr.at[p - 1], sib).wait_recv()
        out, first = (r.oq, p - 1) if p <= 3 else ((r.op, 0) if p == 4 else (r.o1, p - 5))
        for g in range(3):
            lanes = slice(LANES * g, LANES * (g + 1))
            base = 768 * first + 256 * g
            out[:, pl.ds(pl.multiple_of(base + LANES * core, LANES), LANES)] = r.fs[
                p - 1, mine, lanes
            ]
            out[:, pl.ds(pl.multiple_of(base + LANES * other, LANES), LANES)] = r.fr[
                p - 1, :, lanes
            ]

    def rs_6(n):
        p = order[n]
        l0, l1, l2, l3 = rs_bufs(n)
        g = grad_piece(p, core)
        rs_copy(n, 0, grad_piece(p, other), l0, sib).wait_send()
        rs_copy(n, 1, g.at[pl.ds(2, 2), xy_d], l1.at[0], x_dev).wait_send()
        rs_copy(n, 2, g.at[pl.ds(0, 2), xy_d], l1.at[1], y_dev).wait_send()
        rs_copy(n, 3, g.at[:, xy_x], l2.at[0], x_dev).wait_send()
        rs_copy(n, 4, g.at[:, xy_y], l2.at[1], y_dev).wait_send()
        for k in (1, 2, 3):
            rs_copy(n, 4 + k, g.at[z_of(k), xy], l3.at[k - 1], z_dev(k)).wait_send()
        if 1 <= p <= 8:
            half = pl.ds(pl.multiple_of(other * 24, 8), 24)
            rs_copy(n, 8, r.fs.at[p - 1, half], r.fr.at[p - 1], sib).wait_send()

    rs_stages = (rs_0, rs_1, rs_2, rs_3, rs_4, rs_5, rs_6)

    base = [0, 1, 2, 3, 6, 7, 8, 9, 10, 14, 15, 16, 18]

    def rs_step(s):
        for i, stage in enumerate(rs_stages):
            if s - i in base:
                stage(base.index(s - i))

    def rows_of(f):
        return pl.ds(pl.multiple_of(f * WIN, WIN), WIN)

    def loop(count, body, ticks=()):
        def step(i, carry):
            body(i)
            for k, tick in enumerate(ticks):
                if tick is not None:
                    pl.when(i == k)(tick)
            return carry

        lax.fori_loop(0, count, step, 0)

    def steps(fn, *numbers):
        return [functools.partial(fn, s) if s is not None else None for s in numbers]

    def natural(ref, lead, rows):
        parts = []
        for g in range(3):
            for h in range(2):
                parts.append(ref[(h, *lead, rows, pl.ds(LANES * g, LANES))])
        return parts

    def put(ref, lead, rows, value):
        for g in range(3):
            for h in range(2):
                at = 256 * g + LANES * h
                ref[(h, *lead, rows, pl.ds(LANES * g, LANES))] = value[:, at : at + LANES]

    def put_a(piece, rows, value):
        for g in range(3):
            for h in range(2):
                at = 256 * g + LANES * h
                r.gp[4 * h + piece, rows, LANES * g : LANES * (g + 1)] = value[:, at : at + LANES]

    def pre_rows(t, h, s):
        return pl.ds(pl.multiple_of((2 * t + h) * 1024 + s.start, 8), s.stop - s.start)

    def pre_tile(t, s):
        return jnp.concatenate([gp_m[pre_rows(t, h, s), :] for h in range(2)], axis=1)

    def mixed_in(f):
        rw = rows_of(f)
        return jnp.where(r.st[rw, 0:1] > 0, r.v24[6:7, :], r.tok[rw, :].astype(F32))

    def masks():
        bits = jnp.transpose(r.mask[...].astype(F32))
        for j in range(8):
            keep = 1.0 - r.pad[j // 2].astype(F32)
            col = bits[:, j : j + 1]
            r.st[LANES * j : LANES * (j + 1), 0:1] = col
            r.st[LANES * j : LANES * (j + 1), 1:2] = col * keep

    def mask_grad(f):
        rw = rows_of(f)
        r.dm[rw, :] = (r.dm[rw, :].astype(F32) * r.st[rw, 1:2]).astype(BF16)

    def spread_small():
        table = r.sv[...].reshape(32, 16, LANES).astype(F32)
        rows = [table[:, i, :].astype(BF16) for i in range(3)]
        at = 0
        for name, row, lane0, width in SMALL_ROWS:
            pick, owner = spread_tables(lane0, width)
            full = jnp.sum(jnp.where(owner, dot_nn(rows[row], pick), 0.0), axis=0, keepdims=True)
            if name == "qkv_bias":
                r.bqkv[...] = full
            elif name == "fc1_bias":
                r.bfc1[...] = full
            else:
                r.v24[at : at + 1, :] = full
                at += 1
        r.gv[...] = jnp.zeros_like(r.gv)

    def collect_small():
        table = [jnp.zeros((32, LANES), F32) for _ in range(3)]
        at = 0
        for name, row, lane0, width in SMALL_ROWS:
            pick, owner = spread_tables(lane0, width)
            if name == "qkv_bias":
                full = r.gbqkv[...]
            elif name == "fc1_bias":
                full = r.gbfc1[...]
            else:
                full = r.gv[at : at + 1, :]
                at += 1
            parts = jnp.where(owner, full, 0.0)
            for _ in range(3):
                high = parts.astype(BF16)
                table[row] = table[row] + dot_nt(high, pick)
                parts = parts - high.astype(F32)
        flat = r.sg.reshape(256, LANES)
        r.sg[...] = jnp.zeros_like(r.sg)
        for i in range(3):
            flat[pl.ds(i, 32, stride=8), :] = table[i]

    def ln1(f):
        rw = rows_of(f)
        x = mixed_in(f)
        row_mean, row_scale = row_stats(x)
        r.st[rw, 2:3] = row_mean
        r.st[rw, 3:4] = row_scale
        r.normed[rw, :] = ((x - row_mean) * row_scale * r.v24[0:1, :] + r.v24[1:2, :]).astype(BF16)

    def qkv(t):
        w = jnp.concatenate(natural(wa_m, (t,), pl.ds(0, 768)), axis=1)
        cols = slice(768 * t, 768 * (t + 1))
        bias = r.bqkv[:, cols]
        for i in range(4):
            s = slice(WIN * i, WIN * (i + 1))
            r.packed[s, cols] = (dot_nn(r.normed[s, :], w) + bias).astype(BF16)

    low_lanes = lax.broadcasted_iota(jnp.int32, (WIN, LANES), 1) < HEAD_DIM

    def two_heads(a):
        z = jnp.zeros_like(a)
        return jnp.concatenate([jnp.where(low_lanes, a, z), jnp.where(low_lanes, z, a)], axis=0)

    def attention(f):
        rw = rows_of(f)
        for hp in range(HEADS // 2):
            part = lambda i: slice(768 * i + LANES * hp, 768 * i + LANES * (hp + 1))
            q2 = r.packed[rw, part(0)] * jnp.asarray(0.125, BF16)
            k2 = r.packed[rw, part(1)]
            v2 = r.packed[rw, part(2)]
            scores = dot_nt(two_heads(q2), k2)
            row_max = jnp.max(scores, axis=1, keepdims=True)
            e = jnp.exp(scores - row_max)
            total = jnp.sum(e, axis=1, keepdims=True)
            inv = 1.0 / total
            log_total = row_max + jnp.log(total)
            for h in range(2):
                col = jnp.broadcast_to(log_total[WIN * h : WIN * (h + 1)], (WIN, 8))
                r.lse[f * 6 + hp, h : h + 1, :] = jnp.transpose(col)[0:1]
            e = e.astype(BF16)
            out = dot_nn(jnp.concatenate([e[:WIN], e[WIN:]], axis=1), two_heads(v2))
            scale = jnp.where(
                low_lanes,
                jnp.broadcast_to(inv[:WIN], (WIN, LANES)),
                jnp.broadcast_to(inv[WIN:], (WIN, LANES)),
            )
            r.att[rw, part(0)] = (out * scale).astype(BF16)

    def project(f):
        rw = rows_of(f)
        w = jnp.concatenate(natural(wa_m, (3,), pl.ds(0, 768)), axis=1)
        middle = mixed_in(f) + (dot_nn(r.att[rw, :], w) + r.v24[2:3, :])
        r.mid[rw, :] = middle
        row_mean, row_scale = row_stats(middle)
        r.st[rw, 4:5] = row_mean
        r.st[rw, 5:6] = row_scale
        r.n2[rw, :] = ((middle - row_mean) * row_scale * r.v24[3:4, :] + r.v24[4:5, :]).astype(BF16)

    def tile(t):
        return pl.ds(pl.multiple_of(t * 768, 768), 768)

    def fc1(t):
        w = jnp.concatenate(natural(w1_m, (t,), pl.ds(0, 768)), axis=1)
        cols = tile(t)
        bias = r.bfc1[:, cols]
        for i in range(4):
            s = slice(WIN * i, WIN * (i + 1))
            act, slope = gelu_and_slope(dot_nn(r.n2[s, :], w) + bias)
            r.hact[s, cols] = act.astype(BF16)
            slope = slope.astype(BF16)
            gp_m[pre_rows(t, 0, s), :] = slope[:, :COLS]
            gp_m[pre_rows(t, 1, s), :] = slope[:, COLS:]

    def turn(src):
        def body(f):
            rw = rows_of(f)
            r.tr[:, rw] = r.normed[rw, :].T if src == 0 else r.n2[rw, :].T

        return body

    def fc2(n):
        cols = pl.ds(pl.multiple_of(n * 256, 256), 256)
        parts = []
        for i in range(2):
            g = 2 * n + i
            lanes = pl.ds(pl.multiple_of(lax.rem(g, 3) * LANES, LANES), LANES)
            parts.append(w2_m[lax.div(g, 3), :, lanes])
        w = jnp.concatenate(parts, axis=1)
        for i in range(4):
            s = slice(WIN * i, WIN * (i + 1))
            r.n2[s, cols] = (
                dot_nn(r.hact[s, :], w) + (r.mid[s, cols] + r.v24[5:6, cols])
            ).astype(BF16)

    def grad_fc2(t):
        cols = tile(t)
        g = dot_tn(r.hact[:, cols], r.dm[...]).astype(BF16)
        g2_m[0, cols, :] = g[:, :COLS]
        g2_m[1, cols, :] = g[:, COLS:]

    def grad_pre(t):
        cols = tile(t)
        w = jnp.concatenate([w2_m[0, cols, :], w2_m[1, cols, :]], axis=1)
        sums = jnp.zeros((1, 768), F32)
        for i in range(4):
            s = slice(WIN * i, WIN * (i + 1))
            d = (dot_nt(r.dm[s, :], w) * pre_tile(t, s).astype(F32)).astype(BF16)
            gp_m[pre_rows(t, 0, s), :] = d[:, :COLS]
            gp_m[pre_rows(t, 1, s), :] = d[:, COLS:]
            sums = sums + jnp.sum(d.astype(F32), axis=0, keepdims=True)
        r.gbfc1[:, cols] = sums

    def grad_fc1(t):
        put(w1_m, (t,), pl.ds(0, 768), dot_nn(r.tr[...], pre_tile(t, slice(0, 1024))).astype(BF16))

    def grad_norm_two(n):
        rw = rows_of(n)
        parts = []
        for t in range(4):
            parts += natural(w1_m, (t,), rw)
        w = jnp.concatenate(parts, axis=1)
        for i in range(4):
            s = slice(WIN * i, WIN * (i + 1))
            pre = jnp.concatenate([pre_tile(t, s) for t in range(4)], axis=1)
            r.dn[s, rw] = dot_nt(pre, w)

    def grad_middle(f):
        rw = rows_of(f)
        dy = r.dm[rw, :].astype(F32)
        dx, gain, shift = norm_backward(
            r.mid[rw, :], r.st[rw, 4:5], r.st[rw, 5:6], r.dn[rw, :], r.v24[3:4, :]
        )
        d = dy + dx
        low = d.astype(BF16)
        r.mid[rw, :] = d
        r.dm[rw, :] = low
        r.gv[3:4, :] += gain
        r.gv[4:5, :] += shift
        r.gv[5:6, :] += jnp.sum(dy, axis=0, keepdims=True)
        r.gv[2:3, :] += jnp.sum(low.astype(F32), axis=0, keepdims=True)

    def grad_proj(j):
        rw = rows_of(j)
        put_a(3, rw, dot_tn(r.att[:, rw], r.dm[...]).astype(BF16))

    def grad_att(f):
        rw = rows_of(f)
        w = jnp.concatenate(natural(wa_m, (3,), pl.ds(0, 768)), axis=1)
        r.n2[rw, :] = dot_nt(r.dm[rw, :], w).astype(BF16)

    def attention_backward(f):
        rw = rows_of(f)
        for hp in range(HEADS // 2):
            part = lambda i: slice(768 * i + LANES * hp, 768 * i + LANES * (hp + 1))
            q2 = r.packed[rw, part(0)] * jnp.asarray(0.125, BF16)
            k2 = r.packed[rw, part(1)]
            v2 = r.packed[rw, part(2)]
            qs, ds, ks = two_heads(q2), two_heads(r.n2[rw, part(0)]), two_heads(k2)
            log_total = jnp.concatenate(
                [r.lse[f * 6 + hp, 0:1, :], r.lse[f * 6 + hp, 1:2, :]], axis=1
            )
            probs = jnp.exp(dot_nt(k2, qs) - log_total)
            prod = probs * dot_nt(v2, ds)
            row_dot = jnp.sum(prod, axis=0, keepdims=True)
            d_scores = (prod - probs * row_dot).astype(BF16)
            r.packed[rw, part(2)] = dot_nn(probs.astype(BF16), ds).astype(BF16)
            r.packed[rw, part(1)] = dot_nn(d_scores, qs).astype(BF16)
            stacked = jnp.concatenate([d_scores[:, :WIN], d_scores[:, WIN:]], axis=0)
            r.packed[rw, part(0)] = (dot_tn(stacked, ks) * 0.125).astype(BF16)

    def grad_qkv(t):
        cols = slice(768 * t, 768 * (t + 1))
        d = r.packed[:, cols]
        put_a(t, slice(None), dot_nn(r.tr[...], d).astype(BF16))
        r.gbqkv[:, cols] = jnp.sum(d.astype(F32), axis=0, keepdims=True)

    def grad_norm_one(n):
        rw = rows_of(n)
        parts = []
        for t in range(3):
            parts += natural(wa_m, (t,), rw)
        w = jnp.concatenate(parts, axis=1)
        for i in range(4):
            s = slice(WIN * i, WIN * (i + 1))
            r.dn[s, rw] = dot_nt(r.packed[s, :], w)

    def grad_mixed(f):
        rw = rows_of(f)
        dx, gain, shift = norm_backward(
            mixed_in(f), r.st[rw, 2:3], r.st[rw, 3:4], r.dn[rw, :], r.v24[0:1, :]
        )
        d = r.mid[rw, :] + dx
        chosen = r.st[rw, 0:1] > 0
        r.dn[rw, :] = jnp.where(chosen, 0.0, d)
        r.gv[0:1, :] += gain
        r.gv[1:2, :] += shift
        r.gv[6:7, :] += jnp.sum(jnp.where(chosen, d, 0.0), axis=0, keepdims=True)

    loads = [
        pltpu.make_async_copy(r.og_in, r.dm, r.ld.at[0]),
        pltpu.make_async_copy(r.tok_in, r.tok, r.ld.at[1]),
    ]
    for q in range(2):
        loads.append(
            pltpu.make_async_copy(
                r.s2w.at[:, pl.ds(COLS * q, COLS)], w2_shard.at[q, zpos, xy, core], r.ld.at[2 + q]
            )
        )
    loads.append(pltpu.make_async_copy(r.small, r.sv.at[zpos, xy, core], r.ld.at[4]))
    for copy in loads:
        copy.start()

    barrier = pltpu.get_barrier_semaphore()
    peers = [sib, x_dev, y_dev, z_dev(1), z_dev(2), z_dev(3)]
    for dev in peers:
        pl.semaphore_signal(barrier, inc=1, device_id=(dev,), device_id_type=MESH_ID)

    def shard_half(t, half):
        ref, first = (r.sq, t) if t < 3 else ((r.sp, 0) if t == 3 else (r.s1w, t - 4))
        parts = []
        for g in range(3):
            base = 768 * first + 256 * g
            a = ref[:, base : base + LANES].astype(F32)
            b = ref[:, base + LANES : base + 2 * LANES].astype(F32)
            parts.append(jnp.where(half == 0, a, b))
        return jnp.concatenate(parts, axis=1)

    for t in range(8):
        away = jnp.concatenate([shard_half(t, other), jnp.zeros((8, COLS), F32)], axis=0)
        r.tx[t] = away.astype(BF16)
    pl.semaphore_wait(barrier, len(peers))
    swap = remote(r.tx, r.rx, r.prep.at[0], r.prep.at[1], sib)
    swap.start()
    loads[4].wait()
    ag_a(0)
    swap.wait()
    for t in range(8):
        here = shard_half(t, core)
        there = r.rx[t].astype(F32)[:24]
        block = jnp.concatenate(
            [jnp.where(core == 0, here, there), jnp.where(core == 0, there, here)], axis=0
        ).astype(BF16)
        if t < 4:
            wa_v[core, t, zpos, xy] = block
        else:
            w1_v[core, t - 4, zpos, xy] = block
    for p in range(1, ahead):
        ag_a(p)
    loads[2].wait()
    loads[3].wait()
    ag_step(0)
    masks()
    ag_step(1)
    loads[0].wait()
    loop(4, mask_grad)
    ag_step(2)
    ag_e(0)
    loads[1].wait()
    spread_small()
    ag_step(3)
    loop(4, ln1)
    ag_e(1)
    qkv(0)
    ag_step(4)
    ag_e(2)
    qkv(1)
    ag_step(5)
    ag_e(3)
    qkv(2)
    ag_step(6)
    loop(4, attention, steps(ag_step, None, 7, 8, 9))
    ag_e(4)
    loop(4, project)
    keep_middle = pltpu.make_async_copy(r.mid, r.ig, r.ld.at[5])
    keep_middle.start()

    def arrive(p, s=None):
        def go():
            if s is not None:
                ag_step(s)
            ag_e(p)

        return go

    arrive(5)()
    loop(4, fc1, [arrive(6, 10), arrive(7, 11), arrive(8), functools.partial(ag_step, 12)])
    loop(4, turn(1))
    loop(4, grad_fc2, steps(ag_step, None, 13, None, 14))
    rs_step(0)
    for p in range(PIECES + 1):
        if p >= 9:
            ag_e(p)
        ag_f(p)
    rs_step(1)
    loop(4, grad_pre, steps(rs_step, None, 2, None, 3))
    loop(3, grad_norm_two, steps(rs_step, 4, None, 5))
    loop(4, grad_fc1, steps(rs_step, 6, None, None, 7))
    keep_middle.wait()
    loop(4, grad_middle)
    rs_step(8)
    loop(3, grad_proj)
    loop(4, grad_att)
    rs_step(9)
    loop(4, attention_backward, steps(rs_step, 10, 11, 12, 13))
    loop(4, turn(0))
    for t in range(3):
        grad_qkv(t)
        rs_step(14 + t)
    loop(3, grad_norm_one, steps(rs_step, None, 17, None))
    loop(4, grad_mixed)
    collect_small()
    load_middle = pltpu.make_async_copy(r.ig, r.mid, r.ld.at[6])
    load_middle.start()
    rs_step(18)
    load_middle.wait()
    write_grad = pltpu.make_async_copy(r.dn, r.ig, r.ld.at[7])
    write_grad.start()
    loop(3, fc2, steps(rs_step, 19, 20, None))
    write_out = pltpu.make_async_copy(r.n2, r.bo, r.ld.at[0])
    write_out.start()
    rs_step(21)
    rs_step(22)
    rs_step(23)
    rs_step(24)
    write_grad.wait()
    write_out.wait()


def fused_device(
    tokens,
    mask_bits,
    pad_flags,
    ln1_gain,
    ln1_bias,
    qkv_weight,
    qkv_bias,
    proj_weight,
    proj_bias,
    ln2_gain,
    ln2_bias,
    fc1_weight,
    fc1_bias,
    fc2_weight,
    fc2_bias,
    mask_embed,
    out_grad,
):
    pad = jnp.zeros((8,), BF16)
    small = jnp.concatenate(
        [ln1_gain, ln1_bias, proj_bias, ln2_gain, ln2_bias, pad, fc2_bias, mask_embed, qkv_bias]
        + [pad, fc1_bias, jnp.zeros((32 + 13 * LANES,), BF16)]
    ).reshape(16, LANES)
    any_spec = pl.BlockSpec(memory_space=pl.ANY)
    vmem = pl.BlockSpec(memory_space=pltpu.VMEM)
    smem = pl.BlockSpec(memory_space=pltpu.SMEM)
    shape = jax.ShapeDtypeStruct
    outs = pl.pallas_call(
        fused_kernel,
        out_shape=(
            shape((1024, 768), BF16),
            shape((1024, 768), F32),
            shape((24, 2304), F32),
            shape((24, 768), F32),
            shape((24, 3072), F32),
            shape((96, 768), F32),
            shape((8, LANES), F32),
        ),
        in_specs=[any_spec, any_spec, vmem, smem, any_spec, vmem, vmem, vmem, any_spec],
        out_specs=(any_spec, any_spec, vmem, vmem, vmem, vmem, vmem),
        scratch_shapes=[pltpu.VMEM(*spec) for spec in SCRATCH.values()] + list(SEMS.values()),
        compiler_params=pltpu.CompilerParams(
            collective_id=0, has_side_effects=True, vmem_limit_bytes=64 * 2**20
        ),
    )(
        tokens,
        out_grad,
        mask_bits.reshape(8, LANES),
        pad_flags,
        small,
        qkv_weight,
        proj_weight,
        fc1_weight,
        fc2_weight,
    )
    block_out, input_grad, gq, gpj, g1, g2, gsmall = outs
    v = {name: gsmall[row, lane : lane + width] for name, row, lane, width in SMALL_ROWS}
    return (
        block_out,
        input_grad,
        v["ln1_gain"],
        v["ln1_bias"],
        gq,
        v["qkv_bias"],
        gpj,
        v["proj_bias"],
        v["ln2_gain"],
        v["ln2_bias"],
        g1,
        v["fc1_bias"],
        g2,
        v["fc2_bias"],
        v["mask_embed"],
    )


def solution(mesh):
    placed = (
        P("fsdp", None),
        P("fsdp"),
        P("fsdp"),
        P("fsdp"),
        P("fsdp"),
        P("fsdp", None),
        P("fsdp"),
        P("fsdp", None),
        P("fsdp"),
        P("fsdp"),
        P("fsdp"),
        P("fsdp", None),
        P("fsdp"),
        P("fsdp", None),
        P("fsdp"),
        P("fsdp"),
        P("fsdp", None),
    )
    return jax.shard_map(
        fused_device if mesh.shape["fsdp"] == 32 else per_device,
        mesh=mesh,
        in_specs=placed,
        out_specs=(
            P("fsdp", None),
            P("fsdp", None),
            P("fsdp"),
            P("fsdp"),
            P("fsdp", None),
            P("fsdp"),
            P("fsdp", None),
            P("fsdp"),
            P("fsdp"),
            P("fsdp"),
            P("fsdp", None),
            P("fsdp"),
            P("fsdp", None),
            P("fsdp"),
            P("fsdp"),
        ),
        check_vma=False,
    )
```

```python
import functools

import jax
import jax.numpy as jnp
from jax import lax
from jax.experimental import pallas as pl
from jax.experimental.pallas import tpu as pltpu
from jax.sharding import PartitionSpec as P

HEADS = 12
HEAD_DIM = 64
WIN = 256


epsilon = 1e-06


def norm_rows(values, gain_vec, shift_vec):
    row_mean = jnp.mean(values, axis=-1, keepdims=True)
    centered = values - row_mean
    variance = jnp.mean(centered * centered, axis=-1, keepdims=True)
    return centered * lax.rsqrt(variance + epsilon) * gain_vec + shift_vec


def gelu_exact(values):
    return jax.nn.gelu(values, approximate=False)


def forward_pass(full, tok_rows, masked):
    (
        gain_one,
        shift_one,
        qkv_w,
        qkv_b,
        proj_w,
        proj_b,
        gain_two,
        shift_two,
        up_w,
        up_b,
        down_w,
        down_b,
        mask_vec,
    ) = full
    row_count = tok_rows.shape[0]
    width = tok_rows.shape[1]
    frames = row_count // WIN
    mixed_in = jnp.where(
        masked[:, None] > 0, mask_vec.astype(jnp.float32)[None, :], tok_rows.astype(jnp.float32)
    )
    normed = norm_rows(
        mixed_in, gain_one.astype(jnp.float32), shift_one.astype(jnp.float32)
    ).astype(jnp.bfloat16)
    packed = (
        jnp.dot(normed, qkv_w, preferred_element_type=jnp.float32) + qkv_b.astype(jnp.float32)
    ).astype(jnp.bfloat16)
    heads_view = packed.reshape(frames, WIN, 3, HEADS, HEAD_DIM)
    scores = jnp.einsum(
        "fqhd,fkhd->fhqk",
        heads_view[:, :, 0],
        heads_view[:, :, 1],
        preferred_element_type=jnp.float32,
    ) * HEAD_DIM ** (-0.5)
    row_max = jnp.max(scores, axis=-1, keepdims=True)
    exp_terms = jnp.exp(scores - row_max)
    row_total = jnp.sum(exp_terms, axis=-1, keepdims=True)
    probs_low = (exp_terms / row_total).astype(jnp.bfloat16)
    log_total = row_max + jnp.log(row_total)
    attended = jnp.einsum(
        "fhqk,fkhd->fqhd", probs_low, heads_view[:, :, 2], preferred_element_type=jnp.float32
    )
    attended = attended.reshape(row_count, width).astype(jnp.bfloat16)
    middle = (
        mixed_in
        + jnp.dot(attended, proj_w, preferred_element_type=jnp.float32)
        + proj_b.astype(jnp.float32)
    )
    normed_two = norm_rows(
        middle, gain_two.astype(jnp.float32), shift_two.astype(jnp.float32)
    ).astype(jnp.bfloat16)
    hidden_pre = jnp.dot(normed_two, up_w, preferred_element_type=jnp.float32) + up_b.astype(
        jnp.float32
    )
    hidden_act = gelu_exact(hidden_pre).astype(jnp.bfloat16)
    result = (
        middle
        + jnp.dot(hidden_act, down_w, preferred_element_type=jnp.float32)
        + down_b.astype(jnp.float32)
    )
    saved = (
        mixed_in,
        normed,
        packed,
        log_total,
        attended,
        middle,
        normed_two,
        hidden_pre,
        hidden_act,
    )
    return (result, saved)


def mlp_backward(full, saved, cotangent):
    (
        gain_one,
        shift_one,
        qkv_w,
        qkv_b,
        proj_w,
        proj_b,
        gain_two,
        shift_two,
        up_w,
        up_b,
        down_w,
        down_b,
        mask_vec,
    ) = full
    mixed_in, normed, packed, log_total, attended, middle, normed_two, hidden_pre, hidden_act = (
        saved
    )
    down_in = cotangent.astype(jnp.bfloat16)
    grad_down = jnp.einsum("tf,td->fd", hidden_act, down_in, preferred_element_type=jnp.float32)
    grad_down_b = jnp.sum(down_in.astype(jnp.float32), axis=0)
    grad_act = jnp.einsum("td,fd->tf", down_in, down_w, preferred_element_type=jnp.float32)
    gelu_value, gelu_pull = jax.vjp(gelu_exact, hidden_pre)
    grad_pre = gelu_pull(grad_act)[0].astype(jnp.bfloat16)
    grad_up = jnp.einsum("td,tf->df", normed_two, grad_pre, preferred_element_type=jnp.float32)
    grad_up_b = jnp.sum(grad_pre.astype(jnp.float32), axis=0)
    grad_norm_two = jnp.einsum("tf,df->td", grad_pre, up_w, preferred_element_type=jnp.float32)
    norm_value, norm_pull = jax.vjp(
        norm_rows, middle, gain_two.astype(jnp.float32), shift_two.astype(jnp.float32)
    )
    grad_middle, grad_gain_two, grad_shift_two = norm_pull(grad_norm_two)
    grad_middle = grad_middle + cotangent
    return (
        grad_middle,
        (grad_gain_two, grad_shift_two, grad_up, grad_up_b, grad_down, grad_down_b),
    )


def attn_backward(full, saved, grad_middle, masked):
    (
        gain_one,
        shift_one,
        qkv_w,
        qkv_b,
        proj_w,
        proj_b,
        gain_two,
        shift_two,
        up_w,
        up_b,
        down_w,
        down_b,
        mask_vec,
    ) = full
    mixed_in, normed, packed, log_total, attended, middle, normed_two, hidden_pre, hidden_act = (
        saved
    )
    row_count = grad_middle.shape[0]
    width = grad_middle.shape[1]
    frames = row_count // WIN
    proj_in = grad_middle.astype(jnp.bfloat16)
    grad_proj = jnp.einsum("td,te->de", attended, proj_in, preferred_element_type=jnp.float32)
    grad_proj_b = jnp.sum(proj_in.astype(jnp.float32), axis=0)
    grad_att = jnp.einsum("te,de->td", proj_in, proj_w, preferred_element_type=jnp.float32).astype(
        jnp.bfloat16
    )
    grad_att = grad_att.reshape(frames, WIN, HEADS, HEAD_DIM)
    heads_view = packed.reshape(frames, WIN, 3, HEADS, HEAD_DIM)
    query_part = heads_view[:, :, 0]
    key_part = heads_view[:, :, 1]
    value_part = heads_view[:, :, 2]
    score_scale = HEAD_DIM ** (-0.5)
    scores = (
        jnp.einsum("fqhd,fkhd->fhqk", query_part, key_part, preferred_element_type=jnp.float32)
        * score_scale
    )
    probs_full = jnp.exp(scores - log_total)
    probs_low = probs_full.astype(jnp.bfloat16)
    grad_value = jnp.einsum(
        "fhqk,fqhd->fkhd", probs_low, grad_att, preferred_element_type=jnp.float32
    )
    grad_probs = jnp.einsum(
        "fqhd,fkhd->fhqk", grad_att, value_part, preferred_element_type=jnp.float32
    )
    row_dot = jnp.sum(grad_probs * probs_full, axis=-1, keepdims=True)
    grad_scores = (probs_full * (grad_probs - row_dot)).astype(jnp.bfloat16)
    grad_query = (
        jnp.einsum("fhqk,fkhd->fqhd", grad_scores, key_part, preferred_element_type=jnp.float32)
        * score_scale
    )
    grad_key = (
        jnp.einsum("fhqk,fqhd->fkhd", grad_scores, query_part, preferred_element_type=jnp.float32)
        * score_scale
    )
    grad_packed = (
        jnp.stack([grad_query, grad_key, grad_value], axis=2)
        .reshape(row_count, 3 * width)
        .astype(jnp.bfloat16)
    )
    grad_qkv = jnp.einsum("td,te->de", normed, grad_packed, preferred_element_type=jnp.float32)
    grad_qkv_b = jnp.sum(grad_packed.astype(jnp.float32), axis=0)
    grad_normed = jnp.einsum("te,de->td", grad_packed, qkv_w, preferred_element_type=jnp.float32)
    first_value, first_pull = jax.vjp(
        norm_rows, mixed_in, gain_one.astype(jnp.float32), shift_one.astype(jnp.float32)
    )
    grad_mixed, grad_gain_one, grad_shift_one = first_pull(grad_normed)
    grad_mixed = grad_mixed + grad_middle
    chosen = masked[:, None] > 0
    tok_grad = jnp.where(chosen, 0.0, grad_mixed)
    grad_mask = jnp.sum(jnp.where(chosen, grad_mixed, 0.0), axis=0)
    return (
        tok_grad,
        (grad_gain_one, grad_shift_one, grad_qkv, grad_qkv_b, grad_proj, grad_proj_b, grad_mask),
    )


def per_device(
    tokens,
    mask_bits,
    pad_flags,
    ln1_gain,
    ln1_bias,
    qkv_weight,
    qkv_bias,
    proj_weight,
    proj_bias,
    ln2_gain,
    ln2_bias,
    fc1_weight,
    fc1_bias,
    fc2_weight,
    fc2_bias,
    mask_embed,
    out_grad,
):
    full = (
        lax.all_gather(ln1_gain, "fsdp", axis=0, tiled=True),
        lax.all_gather(ln1_bias, "fsdp", axis=0, tiled=True),
        lax.all_gather(qkv_weight, "fsdp", axis=0, tiled=True),
        lax.all_gather(qkv_bias, "fsdp", axis=0, tiled=True),
        lax.all_gather(proj_weight, "fsdp", axis=0, tiled=True),
        lax.all_gather(proj_bias, "fsdp", axis=0, tiled=True),
        lax.all_gather(ln2_gain, "fsdp", axis=0, tiled=True),
        lax.all_gather(ln2_bias, "fsdp", axis=0, tiled=True),
        lax.all_gather(fc1_weight, "fsdp", axis=0, tiled=True),
        lax.all_gather(fc1_bias, "fsdp", axis=0, tiled=True),
        lax.all_gather(fc2_weight, "fsdp", axis=0, tiled=True),
        lax.all_gather(fc2_bias, "fsdp", axis=0, tiled=True),
        lax.all_gather(mask_embed, "fsdp", axis=0, tiled=True),
    )
    result, saved = forward_pass(full, tokens, mask_bits)
    full_back = (
        lax.all_gather(ln1_gain, "fsdp", axis=0, tiled=True),
        lax.all_gather(ln1_bias, "fsdp", axis=0, tiled=True),
        lax.all_gather(qkv_weight, "fsdp", axis=0, tiled=True),
        lax.all_gather(qkv_bias, "fsdp", axis=0, tiled=True),
        lax.all_gather(proj_weight, "fsdp", axis=0, tiled=True),
        lax.all_gather(proj_bias, "fsdp", axis=0, tiled=True),
        lax.all_gather(ln2_gain, "fsdp", axis=0, tiled=True),
        lax.all_gather(ln2_bias, "fsdp", axis=0, tiled=True),
        lax.all_gather(fc1_weight, "fsdp", axis=0, tiled=True),
        lax.all_gather(fc1_bias, "fsdp", axis=0, tiled=True),
        lax.all_gather(fc2_weight, "fsdp", axis=0, tiled=True),
        lax.all_gather(fc2_bias, "fsdp", axis=0, tiled=True),
        lax.all_gather(mask_embed, "fsdp", axis=0, tiled=True),
    )
    kept_acts = forward_pass(full_back, tokens, mask_bits)[1]
    row_count = tokens.shape[0]
    frames = row_count // WIN
    frame_keep = (1 - pad_flags).astype(jnp.float32)
    tok_weight = (mask_bits.astype(jnp.float32).reshape(frames, WIN) * frame_keep[:, None]).reshape(
        row_count
    )
    cotangent = out_grad.astype(jnp.float32) * tok_weight[:, None]
    grad_middle, mlp_grads = mlp_backward(full_back, kept_acts, cotangent)
    tok_grad, attn_grads = attn_backward(full_back, kept_acts, grad_middle, mask_bits)
    shares = (
        lax.psum_scatter(attn_grads[0], "fsdp", scatter_dimension=0, tiled=True),
        lax.psum_scatter(attn_grads[1], "fsdp", scatter_dimension=0, tiled=True),
        lax.psum_scatter(attn_grads[2], "fsdp", scatter_dimension=0, tiled=True),
        lax.psum_scatter(attn_grads[3], "fsdp", scatter_dimension=0, tiled=True),
        lax.psum_scatter(attn_grads[4], "fsdp", scatter_dimension=0, tiled=True),
        lax.psum_scatter(attn_grads[5], "fsdp", scatter_dimension=0, tiled=True),
        lax.psum_scatter(mlp_grads[0], "fsdp", scatter_dimension=0, tiled=True),
        lax.psum_scatter(mlp_grads[1], "fsdp", scatter_dimension=0, tiled=True),
        lax.psum_scatter(mlp_grads[2], "fsdp", scatter_dimension=0, tiled=True),
        lax.psum_scatter(mlp_grads[3], "fsdp", scatter_dimension=0, tiled=True),
        lax.psum_scatter(mlp_grads[4], "fsdp", scatter_dimension=0, tiled=True),
        lax.psum_scatter(mlp_grads[5], "fsdp", scatter_dimension=0, tiled=True),
        lax.psum_scatter(attn_grads[6], "fsdp", scatter_dimension=0, tiled=True),
    )
    return (
        result.astype(jnp.bfloat16),
        tok_grad,
        shares[0],
        shares[1],
        shares[2],
        shares[3],
        shares[4],
        shares[5],
        shares[6],
        shares[7],
        shares[8],
        shares[9],
        shares[10],
        shares[11],
        shares[12],
    )


F32 = jnp.float32
BF16 = jnp.bfloat16
LANES = 128
ROWS = 48
COLS = 384
PIECES = 12
CUT = 16
RINGS = dict(l0=2, l1=4, lz=4, lt=4, l2=4, l3=4)
CREDIT_RINGS = ["l0", "l1", "lt", "l2", "l2"] + ["lz"] * 4 + ["l3"] * 4
SHORT = 11
MESH_ID = pl.DeviceIdType.MESH


def dot_nn(a, b):
    return lax.dot_general(a, b, (((1,), (0,)), ((), ())), preferred_element_type=F32)


def dot_nt(a, b):
    return lax.dot_general(a, b, (((1,), (1,)), ((), ())), preferred_element_type=F32)


def dot_tn(a, b):
    return lax.dot_general(a, b, (((0,), (0,)), ((), ())), preferred_element_type=F32)


def row_stats(values):
    row_mean = jnp.mean(values, axis=-1, keepdims=True)
    centered = values - row_mean
    return row_mean, lax.rsqrt(jnp.mean(centered * centered, axis=-1, keepdims=True) + epsilon)


def gelu_and_slope(x):
    phi = 0.5 + 0.5 * lax.erf(x * 0.7071067811865476)
    return x * phi, phi + x * jnp.exp(x * x * -0.5) * 0.3989422804014327


def norm_backward(x, row_mean, row_scale, grad, gain):
    x_hat = (x - row_mean) * row_scale
    prod = grad * x_hat
    grad_gain = jnp.sum(prod, axis=0, keepdims=True)
    grad_shift = jnp.sum(grad, axis=0, keepdims=True)
    dx = grad * gain
    mean_one = jnp.mean(dx, axis=-1, keepdims=True)
    mean_two = jnp.mean(dx * x_hat, axis=-1, keepdims=True)
    return row_scale * (dx - mean_one - x_hat * mean_two), grad_gain, grad_shift


SMALL_ROWS = (
    ("ln1_gain", 0, 0, 24),
    ("ln1_bias", 0, 24, 24),
    ("proj_bias", 0, 48, 24),
    ("ln2_gain", 0, 72, 24),
    ("ln2_bias", 0, 96, 24),
    ("fc2_bias", 1, 0, 24),
    ("mask_embed", 1, 24, 24),
    ("qkv_bias", 1, 48, 72),
    ("fc1_bias", 2, 0, 96),
)


def spread_tables(lane0, width):
    count = 32 * width
    k = lax.broadcasted_iota(jnp.int32, (1, count), 1)
    pick = lax.broadcasted_iota(jnp.int32, (LANES, count), 0) == lax.rem(k, width) + lane0
    owner = lax.broadcasted_iota(jnp.int32, (32, count), 0) == lax.div(k, width)
    return jnp.where(pick, 1.0, 0.0).astype(BF16), owner


SCRATCH = dict(
    tok=((1024, 768), BF16),
    dm=((1024, 768), BF16),
    st=((1024, 8), F32),
    v24=((8, 768), F32),
    bqkv=((1, 2304), F32),
    bfc1=((1, 3072), F32),
    gv=((8, 768), F32),
    gbqkv=((1, 2304), F32),
    gbfc1=((1, 3072), F32),
    normed=((1024, 768), BF16),
    n2=((1024, 768), BF16),
    tr=((768, 1024), BF16),
    packed=((1024, 2304), BF16),
    att=((1024, 768), BF16),
    mid=((1024, 768), F32),
    hact=((1024, 3072), BF16),
    gp=((11, 768, COLS), BF16),
    dn=((1024, 768), F32),
    lse=((24, 8, 256), F32),
    wa=((8, 768, COLS), BF16),
    w1=((8, 768, COLS), BF16),
    w2=((8, 768, COLS), BF16),
    g2=((8, 768, COLS), BF16),
    sv=((4, 4, 2, 8, LANES), F32),
    sg=((4, 4, 2, 8, LANES), F32),
    fs=((8, ROWS, COLS), F32),
    fr=((8, ROWS // 2, COLS), F32),
    l0=((RINGS["l0"], 4, 4, ROWS, COLS), BF16),
    l1=((RINGS["l1"], 4, CUT, COLS), BF16),
    lz=((RINGS["lz"], 4, ROWS - CUT, COLS), BF16),
    lt=((RINGS["lt"], ROWS - CUT, COLS), BF16),
    l2=((RINGS["l2"], 2, 4, ROWS, COLS), BF16),
    l3=((RINGS["l3"], 4, ROWS, COLS), BF16),
    l1s=((4, ROWS, COLS), BF16),
    l3s=((4, ROWS, COLS), BF16),
    s0=((4, 4, 8, LANES), F32),
    s1=((4, 8, LANES), F32),
    s2=((2, 4, 8, LANES), F32),
    s3=((4, 8, LANES), F32),
)
SEMS = dict(
    ld=pltpu.SemaphoreType.DMA((8,)),
    prep=pltpu.SemaphoreType.DMA((2,)),
    ags=pltpu.SemaphoreType.DMA((PIECES + 1, 17)),
    agr=pltpu.SemaphoreType.DMA((PIECES + 1, 17)),
    rss=pltpu.SemaphoreType.DMA((PIECES + 1, 19)),
    rsr=pltpu.SemaphoreType.DMA((PIECES + 1, 19)),
    credit=pltpu.SemaphoreType.REGULAR((32,)),
)


class Refs:
    pass


def fused_kernel(*refs):
    r = Refs()
    names = ["tok_in", "og_in", "mask", "pad", "small", "sq", "sp", "s1w", "s2w"]
    names += ["bo", "ig", "oq", "op", "o1", "o2", "osm"]
    names += list(SCRATCH) + list(SEMS)
    for name, ref in zip(names, refs):
        setattr(r, name, ref)

    me = lax.axis_index("fsdp")
    core = lax.rem(me, 2)
    other = 1 - core
    chip = lax.div(me, 2)
    xpos = lax.rem(chip, 2)
    ypos = lax.rem(lax.div(chip, 2), 2)
    zpos = lax.div(chip, 4)
    xy = lax.rem(chip, 4)
    xy_x = xy + 1 - 2 * xpos
    xy_y = xy + 2 - 4 * ypos
    xy_d = xy_x + 2 - 4 * ypos
    sib = me + 1 - 2 * core
    x_dev = me + 2 - 4 * xpos
    y_dev = me + 4 - 8 * ypos

    def z_of(k):
        return lax.rem(zpos + k, 4)

    def z_dev(k):
        return me + 8 * (z_of(k) - zpos)

    def remote(src, dst, ssem, rsem, dev):
        return pltpu.make_async_remote_copy(
            src_ref=src,
            dst_ref=dst,
            send_sem=ssem,
            recv_sem=rsem,
            device_id=(dev,),
            device_id_type=MESH_ID,
        )

    wa_v = r.wa.reshape(2, 4, 4, 4, ROWS, COLS)
    w1_v = r.w1.reshape(2, 4, 4, 4, ROWS, COLS)
    w2_v = r.w2.reshape(2, 4, 4, 2, 2, ROWS, COLS)
    w2_shard = r.w2.reshape(2, 4, 4, 2, 2 * ROWS, COLS)
    w2_m = r.w2.reshape(2, 3072, COLS)
    wa_m = r.wa.reshape(2, 4, 768, COLS)
    w1_m = r.w1.reshape(2, 4, 768, COLS)
    g2_v = r.g2.reshape(2, 4, 4, 2, 2, ROWS, COLS)
    g2_m = r.g2.reshape(2, 3072, COLS)
    ga_v = r.gp.reshape(11, 4, 4, ROWS, COLS)
    gp_m = r.gp.reshape(11 * 768, COLS)

    def weight_piece(p, half):
        if p == 0:
            return r.sv.at[:, :, half]
        if p <= 4:
            return wa_v.at[half, p - 1]
        if p <= 8:
            return w1_v.at[half, p - 5]
        return w2_v.at[(p - 9) % 2, :, :, half, (p - 9) // 2]

    def grad_piece(p, half):
        if p == 0:
            return r.sg.at[:, :, half]
        if p <= 4:
            return ga_v.at[half * 4 + p - 1]
        if p <= 8:
            return w1_v.at[half, p - 5]
        return g2_v.at[(p - 9) % 2, :, :, half, (p - 9) // 2]

    def ag_copy(p, i, src, dst, dev):
        return remote(src, dst, r.ags.at[p, i], r.agr.at[p, i], dev)

    def rows_one(p):
        return pl.ds(0, CUT) if p else pl.ds(0, 8)

    def rs_rows_one(n):
        return pl.ds(0, ROWS) if SHORT <= n < PIECES else rows_one(order[n])

    rows_two = pl.ds(CUT, ROWS - CUT)

    def sides(p):
        along_x, along_y = (x_dev, xy_x), (y_dev, xy_y)
        return (along_x, along_y) if p % 2 == 0 else (along_y, along_x)

    at_start, at_end = zpos == 0, zpos == 3
    inside = jnp.logical_and(zpos > 0, zpos < 3)

    def along_z(fn):
        pl.when(jnp.logical_not(at_end))(lambda: fn(1))
        fn(2)
        pl.when(jnp.logical_not(at_start))(lambda: fn(3))

    def pass_to_end(fn):
        pl.when(zpos == 1)(lambda: fn(3, 3))
        pl.when(zpos == 2)(lambda: fn(0, 1))

    def ag_z(p, k, at):
        return ag_copy(p, k - 1, at, at, z_dev(k))

    def ag_z2(p, k, at):
        return ag_copy(p, 12 + k, at, at, z_dev(k))

    def ag_z_from(p, k, at, base=0):
        return ag_copy(p, base + k - 1, at, at, z_dev(k))

    def ag_pass(p, far, k, at, base=0):
        return ag_copy(p, base + (0 if k == 3 else 2), at, at, z_dev(k))

    def ag_x(p, k, v):
        at = v.at[z_of(4 - k), xy] if k else v.at[zpos, xy]
        return ag_copy(p, 3 + k, at, at, x_dev)

    def ag_y(p, k, v):
        at = v.at[z_of(4 - k), xy] if k else v.at[zpos, xy]
        return ag_copy(p, 7 + k, at, at, y_dev)

    def from_x(p, k, v):
        at = v.at[z_of(4 - k), xy_x] if k else v.at[zpos, xy_x]
        return ag_copy(p, 3 + k, at, at, x_dev)

    def from_y(p, k, v):
        at = v.at[z_of(4 - k), xy_y] if k else v.at[zpos, xy_y]
        return ag_copy(p, 7 + k, at, at, y_dev)

    def from_a(p, k, v):
        return from_x(p, k, v) if p % 2 == 0 else from_y(p, k, v)

    def from_b(p, k, v):
        return from_y(p, k, v) if p % 2 == 0 else from_x(p, k, v)

    def ag_one(p, v, col):
        at = v.at[:, col, rows_one(p)]
        return ag_copy(p, 11, at, at, sides(p)[1][0])

    def ag_two(p, v, col):
        at = v.at[zpos, col, rows_two]
        return ag_copy(p, 12, at, at, sides(p)[0][0])

    def ag_a(p):
        v = weight_piece(p, core)
        along_z(lambda k: ag_z(p, k, v.at[zpos, xy]).start())
        ag_x(p, 0, v).start()
        ag_y(p, 0, v).start()

    def ag_b(p):
        v = weight_piece(p, core)
        for k in (1, 3):
            ag_z_from(p, k, v.at[z_of(4 - k), xy]).wait_recv()
            ag_x(p, k, v).start()
            ag_y(p, k, v).start()

    def ag_b2(p):
        v = weight_piece(p, core)
        ag_z_from(p, 2, v.at[z_of(2), xy]).wait_recv()
        pass_to_end(lambda far, k: ag_pass(p, far, k, v.at[far, xy]).start())
        ag_x(p, 2, v).start()
        ag_y(p, 2, v).start()

    def ag_c2(p):
        if p:
            v = weight_piece(p, core)
            from_b(p, 0, v).wait_recv()
            ag_two(p, v, sides(p)[1][1]).start()

    def ag_c3(p):
        if p:
            v = weight_piece(p, core)
            ag_two(p, v, xy_d).wait_recv()
            along_z(lambda k: ag_z2(p, k, v.at[zpos, xy_d, rows_two]).start())

    def ag_c1(p):
        v = weight_piece(p, core)
        for k in range(4):
            from_a(p, k, v).wait_recv()
        ag_one(p, v, sides(p)[0][1]).start()

    def ag_c4(p):
        if p:
            v = weight_piece(p, core)
            ag_z_from(p, 2, v.at[z_of(2), xy_d, rows_two], 13).wait_recv()
            pass_to_end(
                lambda far, k: ag_pass(p, far, k, v.at[far, xy_d, rows_two], 13).start()
            )

    def ag_d(p):
        v = weight_piece(p, core)
        for k in (1, 2, 3) if p else (0, 1, 2, 3):
            from_b(p, k, v).wait_recv()
        ag_one(p, v, xy_d).wait_recv()
        if p:
            for k in (1, 3):
                ag_z_from(p, k, v.at[z_of(4 - k), xy_d, rows_two], 13).wait_recv()
        ag_copy(p, 16, v, v, sib).start()

    def ag_e(p):
        v = weight_piece(p, other)
        ag_copy(p, 16, v, v, sib).wait_recv()

    def ag_f(p):
        v = weight_piece(p, core)
        along_z(lambda k: ag_z(p, k, v.at[zpos, xy]).wait_send())
        pass_to_end(lambda far, k: ag_pass(p, far, k, v.at[far, xy]).wait_send())
        for k in range(4):
            ag_x(p, k, v).wait_send()
            ag_y(p, k, v).wait_send()
        ag_one(p, v, sides(p)[0][1]).wait_send()
        if p:
            ag_two(p, v, sides(p)[1][1]).wait_send()
            along_z(lambda k: ag_z2(p, k, v.at[zpos, xy_d, rows_two]).wait_send())
            pass_to_end(
                lambda far, k: ag_pass(p, far, k, v.at[far, xy_d, rows_two], 13).wait_send()
            )
        ag_copy(p, 16, v, v, sib).wait_send()

    ahead = 3

    def ag_step(s):
        for lag, stage in AG_STAGES:
            if 0 <= s - lag <= PIECES and not (lag < 0 and stage is ag_a and s - lag < ahead):
                stage(s - lag)

    AG_STAGES = (
        (-ahead, ag_a),
        (0, ag_b),
        (-1, ag_b2),
        (-1, ag_c2),
        (0, ag_c3),
        (1, ag_c1),
        (1, ag_c4),
        (2, ag_d),
    )

    order = [9, 10, 11, 12, 5, 6, 7, 8, 4, 1, 2, 3, 0]

    def rs_bufs(n):
        if n == PIECES:
            return r.s0, r.s1, r.s2, r.s3
        ring = [getattr(r, name).at[n % RINGS[name]] for name in ("l0", "l1", "l2", "l3")]
        if n >= SHORT:
            ring[1], ring[3] = r.l1s, r.l3s
        return tuple(ring)

    def rs_copy(n, i, src, dst, dev):
        return remote(src, dst, r.rss.at[n, i], r.rsr.at[n, i], dev)

    def credit_wait(n, i):
        if RINGS[CREDIT_RINGS[i]] <= n < (PIECES if i in (0, 3, 4) else SHORT):
            pl.semaphore_wait(r.credit.at[2 * i + n % 2], 1)

    def credit_give(n, i, dev):
        if n < (PIECES if i in (0, 3, 4) else SHORT) - RINGS[CREDIT_RINGS[i]]:
            at = r.credit.at[2 * i + n % 2]
            pl.semaphore_signal(at, inc=1, device_id=(dev,), device_id_type=MESH_ID)

    def add_to(g, at, landed):
        g[at] = (g[at].astype(F32) + landed.astype(F32)).astype(g.dtype)

    def z_send(n, first, block, land, k):
        return rs_copy(n, first + k - 1, block(z_of(k)), land.at[k - 1], z_dev(k))

    def z_far(n, first, block, land, k):
        return rs_copy(n, first + 3, block(3 if k == 1 else 0), land.at[3], z_dev(k))

    def sum_z_start(n, first, credit, block, land):
        def near(k):
            credit_wait(n, credit + k - 1)
            z_send(n, first, block, land, k).start()

        def far(k):
            near(2)
            credit_wait(n, credit + 3)
            z_far(n, first, block, land, k).start()

        pl.when(jnp.logical_not(at_end))(lambda: near(1))
        pl.when(jnp.logical_not(at_start))(lambda: near(3))
        pl.when(at_start)(lambda: far(1))
        pl.when(at_end)(lambda: far(3))

    def sum_z_pass(n, first, credit, block, land):
        def go():
            z_far(n, first, block, land, 1).wait_recv()
            add_to(block(z_of(2)), Ellipsis, land[3])
            pl.when(zpos == 1)(lambda: credit_give(n, credit + 3, z_dev(3)))
            pl.when(zpos == 2)(lambda: credit_give(n, credit + 3, z_dev(1)))
            credit_wait(n, credit + 1)
            z_send(n, first, block, land, 2).start()

        pl.when(inside)(go)

    def sum_z_end(n, first, credit, block, land):
        z_send(n, first, block, land, 2).wait_recv()
        pl.when(jnp.logical_not(at_start))(lambda: z_send(n, first, block, land, 1).wait_recv())
        pl.when(jnp.logical_not(at_end))(lambda: z_send(n, first, block, land, 3).wait_recv())
        total = land[0].astype(F32) + land[1].astype(F32) + land[2].astype(F32)

        def give():
            credit_give(n, credit + 1, z_dev(2))
            pl.when(jnp.logical_not(at_start))(lambda: credit_give(n, credit, z_dev(3)))
            pl.when(jnp.logical_not(at_end))(lambda: credit_give(n, credit + 2, z_dev(1)))

        return total, give

    def sum_z_sent(n, first, block, land):
        z_send(n, first, block, land, 2).wait_send()
        pl.when(jnp.logical_not(at_end))(lambda: z_send(n, first, block, land, 1).wait_send())
        pl.when(jnp.logical_not(at_start))(lambda: z_send(n, first, block, land, 3).wait_send())
        pl.when(at_start)(lambda: z_far(n, first, block, land, 1).wait_send())
        pl.when(at_end)(lambda: z_far(n, first, block, land, 3).wait_send())

    def diagonal(n):
        g = grad_piece(order[n], core)
        return lambda z: g.at[z, xy_d, rows_two], r.lz.at[n % RINGS["lz"]]

    def own_line(n):
        g = grad_piece(order[n], core)
        return lambda z: g.at[z, xy], rs_bufs(n)[3]

    def rs_main(n):
        p = order[n]
        g, land = grad_piece(p, core), rs_bufs(n)[2]
        (a_dev, a), (b_dev, b) = sides(n)
        one = rs_rows_one(n)
        early, late_one, late_two = [], [], []
        if n < SHORT:
            early.append((7, g.at[:, a, rows_two], land.at[0, :, rows_two], a_dev))
        late_one.append((8, g.at[:, a, one], land.at[0, :, one], a_dev))
        early.append((9, g.at[:, b, one], land.at[1, :, one], b_dev))
        if n < SHORT:
            for k in (1, 2, 3):
                z = z_of(k)
                early.append((9 + k, g.at[z, b, rows_two], land.at[1, z, rows_two], b_dev))
            late_two.append((13, g.at[zpos, b, rows_two], land.at[1, zpos, rows_two], b_dev))
        return [[rs_copy(n, *entry) for entry in group] for group in (early, late_one, late_two)]

    def rs_one(n):
        p = order[n]
        return rs_copy(
            n, 1, grad_piece(p, core).at[:, xy_d, rs_rows_one(n)], rs_bufs(n)[1], sides(n)[1][0]
        )

    def rs_two(n):
        p = order[n]
        return rs_copy(
            n,
            6,
            grad_piece(p, core).at[zpos, xy_d, rows_two],
            r.lt.at[n % RINGS["lt"]],
            sides(n)[0][0],
        )

    def rs_swap(n):
        p = order[n]
        half = pl.ds(pl.multiple_of(other * 24, 8), 24)
        return rs_copy(n, 18, r.fs.at[p - 1, half], r.fr.at[p - 1], sib)

    def rs_0(n):
        credit_wait(n, 0)
        rs_copy(n, 0, grad_piece(order[n], other), rs_bufs(n)[0], sib).start()

    def rs_1(n):
        p = order[n]
        l0 = rs_bufs(n)[0]
        g = grad_piece(p, core)
        rs_copy(n, 0, grad_piece(p, other), l0, sib).wait_recv()

        def body(i, carry):
            g[i] = (g[i].astype(F32) + l0[i].astype(F32)).astype(g.dtype)
            return carry

        lax.fori_loop(0, 4, body, 0)
        credit_give(n, 0, sib)
        credit_wait(n, 1)
        rs_one(n).start()
        if n < SHORT:
            sum_z_start(n, 2, 5, *diagonal(n))
        credit_wait(n, 3)
        credit_wait(n, 4)
        for copy in rs_main(n)[0]:
            copy.start()

    def rs_2(n):
        p = order[n]
        g, l1 = grad_piece(p, core), rs_bufs(n)[1]
        (a_dev, a), (b_dev, b) = sides(n)
        rs_one(n).wait_recv()
        for z in range(4):
            add_to(g, (z, a, rs_rows_one(n)), l1[z])
        credit_give(n, 1, b_dev)
        for copy in rs_main(n)[1]:
            copy.start()
        if n < SHORT:
            sum_z_pass(n, 2, 5, *diagonal(n))

    def rs_3(n):
        p = order[n]
        if p:
            g = grad_piece(p, core)
            total, give = sum_z_end(n, 2, 5, *diagonal(n))
            add_to(g, (zpos, xy_d, rows_two), total)
            give()
            credit_wait(n, 2)
            rs_two(n).start()

    def rs_4(n):
        p = order[n]
        if p:
            g = grad_piece(p, core)
            (a_dev, a), (b_dev, b) = sides(n)
            rs_two(n).wait_recv()
            add_to(g, (zpos, b, rows_two), r.lt[n % RINGS["lt"]])
            credit_give(n, 2, a_dev)
            for copy in rs_main(n)[2]:
                copy.start()

    def rs_5(n):
        p = order[n]
        g, l2 = grad_piece(p, core), rs_bufs(n)[2]
        (a_dev, a), (b_dev, b) = sides(n)
        for group in rs_main(n):
            for copy in group:
                copy.wait_recv()
        for z in range(4):
            add_to(g, (z, xy), l2[0, z].astype(F32) + l2[1, z].astype(F32))
        credit_give(n, 3, a_dev)
        credit_give(n, 4, b_dev)
        if n < SHORT:
            sum_z_start(n, 14, 9, *own_line(n))
        else:
            for k in (1, 2, 3):
                z_send(n, 14, *own_line(n), k).start()

    def rs_6(n):
        sum_z_pass(n, 14, 9, *own_line(n))

    def rs_7(n):
        p = order[n]
        if n < SHORT:
            total, give = sum_z_end(n, 14, 9, *own_line(n))
        else:
            land = rs_bufs(n)[3]
            for k in (1, 2, 3):
                z_send(n, 14, *own_line(n), k).wait_recv()
            total = land[0].astype(F32) + land[1].astype(F32) + land[2].astype(F32)
        total = total + grad_piece(p, core)[zpos, xy].astype(F32)
        if p == 0:
            r.osm[...] = total
        elif p >= 9:
            i, j = (p - 9) // 2, (p - 9) % 2
            r.o2[ROWS * i : ROWS * (i + 1), COLS * j : COLS * (j + 1)] = total
        else:
            r.fs[p - 1] = total
            rs_swap(n).start()
        if n < SHORT:
            give()

    def rs_8(n):
        p = order[n]
        if p == 0 or p >= 9:
            return
        mine = pl.ds(pl.multiple_of(core * 24, 8), 24)
        rs_swap(n).wait_recv()
        out, first = (r.oq, 0) if p <= 3 else ((r.op, 0) if p == 4 else (r.o1, p - 5))
        for g in range(3):
            lanes = slice(LANES * g, LANES * (g + 1))
            base = 768 * g + 256 * (p - 1) if p <= 3 else 768 * first + 256 * g
            out[:, pl.ds(pl.multiple_of(base + LANES * core, LANES), LANES)] = r.fs[
                p - 1, mine, lanes
            ]
            out[:, pl.ds(pl.multiple_of(base + LANES * other, LANES), LANES)] = r.fr[
                p - 1, :, lanes
            ]

    def rs_9(n):
        p = order[n]
        rs_copy(n, 0, grad_piece(p, other), rs_bufs(n)[0], sib).wait_send()
        rs_one(n).wait_send()
        for group in rs_main(n):
            for copy in group:
                copy.wait_send()
        if n < SHORT:
            sum_z_sent(n, 2, *diagonal(n))
            rs_two(n).wait_send()
            sum_z_sent(n, 14, *own_line(n))
        else:
            for k in (1, 2, 3):
                z_send(n, 14, *own_line(n), k).wait_send()
        if 1 <= p <= 8:
            rs_swap(n).wait_send()

    rs_long = (rs_0, rs_1, rs_2, rs_3, rs_4, rs_5, rs_6, rs_7, rs_8, rs_9)
    rs_short = (rs_0, rs_1, rs_2, rs_5, rs_7, rs_8, rs_9)

    base = [0, 1, 2, 3, 4, 5, 6, 7, 8, 9, 10, 12, 14]

    def rs_step(s):
        for n in range(PIECES + 1):
            stages = rs_long if n < SHORT else rs_short
            if 0 <= s - base[n] < len(stages):
                stages[s - base[n]](n)

    def rows_of(f):
        return pl.ds(pl.multiple_of(f * WIN, WIN), WIN)

    def loop(count, body, ticks=()):
        def step(i, carry):
            body(i)
            for k, tick in enumerate(ticks):
                if tick is not None:
                    pl.when(i == k)(tick)
            return carry

        lax.fori_loop(0, count, step, 0)

    def steps(fn, *numbers):
        return [functools.partial(fn, s) if s is not None else None for s in numbers]

    def natural(ref, lead, rows):
        parts = []
        for g in range(3):
            for h in range(2):
                parts.append(ref[(h, *lead, rows, pl.ds(LANES * g, LANES))])
        return parts

    def put(ref, lead, rows, value):
        for g in range(3):
            for h in range(2):
                at = 256 * g + LANES * h
                ref[(h, *lead, rows, pl.ds(LANES * g, LANES))] = value[:, at : at + LANES]

    def put_a(piece, rows, value):
        for g in range(3):
            for h in range(2):
                at = 256 * g + LANES * h
                r.gp[4 * h + piece, rows, LANES * g : LANES * (g + 1)] = value[:, at : at + LANES]

    def pre_rows(t, h, s):
        return pl.ds(pl.multiple_of((2 * t + h) * 1024 + s.start, 8), s.stop - s.start)

    def pre_tile(t, s):
        return jnp.concatenate([gp_m[pre_rows(t, h, s), :] for h in range(2)], axis=1)

    def mixed_in(f):
        rw = rows_of(f)
        return jnp.where(r.st[rw, 0:1] > 0, r.v24[6:7, :], r.tok[rw, :].astype(F32))

    def masks():
        bits = jnp.transpose(r.mask[...].astype(F32))
        for j in range(8):
            keep = 1.0 - r.pad[j // 2].astype(F32)
            col = bits[:, j : j + 1]
            r.st[LANES * j : LANES * (j + 1), 0:1] = col
            r.st[LANES * j : LANES * (j + 1), 1:2] = col * keep

    def mask_grad(f):
        rw = rows_of(f)
        r.dm[rw, :] = (r.dm[rw, :].astype(F32) * r.st[rw, 1:2]).astype(BF16)

    def spread_small():
        table = r.sv[...].reshape(32, 8, LANES)
        rows = [table[:, i, :].astype(BF16) for i in range(3)]
        at = 0
        for name, row, lane0, width in SMALL_ROWS:
            pick, owner = spread_tables(lane0, width)
            full = jnp.sum(jnp.where(owner, dot_nn(rows[row], pick), 0.0), axis=0, keepdims=True)
            if name == "qkv_bias":
                for t in range(3):
                    for g in range(3):
                        at_piece, at_whole = 768 * t + 256 * g, 768 * g + 256 * t
                        r.bqkv[:, at_piece : at_piece + 256] = full[:, at_whole : at_whole + 256]
            elif name == "fc1_bias":
                r.bfc1[...] = full
            else:
                r.v24[at : at + 1, :] = full
                at += 1
        r.gv[...] = jnp.zeros_like(r.gv)

    def collect_small():
        table = [jnp.zeros((32, LANES), F32) for _ in range(3)]
        at = 0
        for name, row, lane0, width in SMALL_ROWS:
            pick, owner = spread_tables(lane0, width)
            if name == "qkv_bias":
                chunks = [768 * t + 256 * g for g in range(3) for t in range(3)]
                full = jnp.concatenate([r.gbqkv[:, c : c + 256] for c in chunks], axis=1)
            elif name == "fc1_bias":
                full = r.gbfc1[...]
            else:
                full = r.gv[at : at + 1, :]
                at += 1
            parts = jnp.where(owner, full, 0.0)
            for _ in range(3):
                high = parts.astype(BF16)
                table[row] = table[row] + dot_nt(high, pick)
                parts = parts - high.astype(F32)
        flat = r.sg.reshape(256, LANES)
        r.sg[...] = jnp.zeros_like(r.sg)
        for i in range(3):
            flat[pl.ds(i, 32, stride=8), :] = table[i]

    def ln1(f):
        rw = rows_of(f)
        x = mixed_in(f)
        row_mean, row_scale = row_stats(x)
        r.st[rw, 2:3] = row_mean
        r.st[rw, 3:4] = row_scale
        r.normed[rw, :] = ((x - row_mean) * row_scale * r.v24[0:1, :] + r.v24[1:2, :]).astype(BF16)

    def qkv(t):
        w = jnp.concatenate(natural(wa_m, (t,), pl.ds(0, 768)), axis=1)
        cols = tile(t)
        bias = r.bqkv[:, cols]
        for i in range(4):
            s = slice(WIN * i, WIN * (i + 1))
            r.packed[s, cols] = (dot_nn(r.normed[s, :], w) + bias).astype(BF16)

    def part(t, i, pair):
        return pl.ds(pl.multiple_of(768 * t + 256 * i + LANES * pair, LANES), LANES)

    def head_cols(t, pair):
        return pl.ds(pl.multiple_of(256 * t + LANES * pair, LANES), LANES)

    low_lanes = lax.broadcasted_iota(jnp.int32, (WIN, LANES), 1) < HEAD_DIM

    def two_heads(a):
        z = jnp.zeros_like(a)
        return jnp.concatenate([jnp.where(low_lanes, a, z), jnp.where(low_lanes, z, a)], axis=0)

    def attention(t, f, pair):
        rw = rows_of(f)
        q2 = r.packed[rw, part(t, 0, pair)] * jnp.asarray(0.125, BF16)
        k2 = r.packed[rw, part(t, 1, pair)]
        v2 = r.packed[rw, part(t, 2, pair)]
        scores = dot_nt(two_heads(q2), k2)
        row_max = jnp.max(scores, axis=1, keepdims=True)
        e = jnp.exp(scores - row_max)
        total = jnp.sum(e, axis=1, keepdims=True)
        inv = 1.0 / total
        log_total = row_max + jnp.log(total)
        for h in range(2):
            col = jnp.broadcast_to(log_total[WIN * h : WIN * (h + 1)], (WIN, 8))
            r.lse[f * 6 + 2 * t + pair, h : h + 1, :] = jnp.transpose(col)[0:1]
        e = e.astype(BF16)
        out = dot_nn(jnp.concatenate([e[:WIN], e[WIN:]], axis=1), two_heads(v2))
        scale = jnp.where(
            low_lanes,
            jnp.broadcast_to(inv[:WIN], (WIN, LANES)),
            jnp.broadcast_to(inv[WIN:], (WIN, LANES)),
        )
        r.att[rw, head_cols(t, pair)] = (out * scale).astype(BF16)

    def heads_forward(t):
        qkv(t)
        for f in range(4):
            for pair in range(2):
                attention(t, f, pair)

    def project(f):
        rw = rows_of(f)
        w = jnp.concatenate(natural(wa_m, (3,), pl.ds(0, 768)), axis=1)
        middle = mixed_in(f) + (dot_nn(r.att[rw, :], w) + r.v24[2:3, :])
        r.mid[rw, :] = middle
        row_mean, row_scale = row_stats(middle)
        r.st[rw, 4:5] = row_mean
        r.st[rw, 5:6] = row_scale
        r.n2[rw, :] = ((middle - row_mean) * row_scale * r.v24[3:4, :] + r.v24[4:5, :]).astype(BF16)

    def tile(t):
        return pl.ds(pl.multiple_of(t * 768, 768), 768)

    def fc1(t):
        w = jnp.concatenate(natural(w1_m, (t,), pl.ds(0, 768)), axis=1)
        cols = tile(t)
        bias = r.bfc1[:, cols]
        for i in range(4):
            s = slice(WIN * i, WIN * (i + 1))
            act, slope = gelu_and_slope(dot_nn(r.n2[s, :], w) + bias)
            r.hact[s, cols] = act.astype(BF16)
            slope = slope.astype(BF16)
            gp_m[pre_rows(t, 0, s), :] = slope[:, :COLS]
            gp_m[pre_rows(t, 1, s), :] = slope[:, COLS:]

    def turn(src):
        def body(f):
            rw = rows_of(f)
            r.tr[:, rw] = r.normed[rw, :].T if src == 0 else r.n2[rw, :].T

        return body

    def fc2(n):
        cols = pl.ds(pl.multiple_of(n * 256, 256), 256)
        parts = []
        for i in range(2):
            g = 2 * n + i
            lanes = pl.ds(pl.multiple_of(lax.rem(g, 3) * LANES, LANES), LANES)
            parts.append(w2_m[lax.div(g, 3), :, lanes])
        w = jnp.concatenate(parts, axis=1)
        for i in range(4):
            s = slice(WIN * i, WIN * (i + 1))
            r.n2[s, cols] = (
                dot_nn(r.hact[s, :], w) + (r.mid[s, cols] + r.v24[5:6, cols])
            ).astype(BF16)

    def grad_fc2(t):
        cols = tile(t)
        g = dot_tn(r.hact[:, cols], r.dm[...]).astype(BF16)
        g2_m[0, cols, :] = g[:, :COLS]
        g2_m[1, cols, :] = g[:, COLS:]

    def grad_pre(t):
        cols = tile(t)
        w = jnp.concatenate([w2_m[0, cols, :], w2_m[1, cols, :]], axis=1)
        sums = jnp.zeros((1, 768), F32)
        for i in range(4):
            s = slice(WIN * i, WIN * (i + 1))
            d = (dot_nt(r.dm[s, :], w) * pre_tile(t, s).astype(F32)).astype(BF16)
            gp_m[pre_rows(t, 0, s), :] = d[:, :COLS]
            gp_m[pre_rows(t, 1, s), :] = d[:, COLS:]
            sums = sums + jnp.sum(d.astype(F32), axis=0, keepdims=True)
        r.gbfc1[:, cols] = sums

    def grad_fc1(t):
        put(w1_m, (t,), pl.ds(0, 768), dot_nn(r.tr[...], pre_tile(t, slice(0, 1024))).astype(BF16))

    def grad_norm_two(n):
        rw = rows_of(n)
        parts = []
        for t in range(4):
            parts += natural(w1_m, (t,), rw)
        w = jnp.concatenate(parts, axis=1)
        for i in range(4):
            s = slice(WIN * i, WIN * (i + 1))
            pre = jnp.concatenate([pre_tile(t, s) for t in range(4)], axis=1)
            r.dn[s, rw] = dot_nt(pre, w)

    def grad_middle(f):
        rw = rows_of(f)
        dy = r.dm[rw, :].astype(F32)
        dx, gain, shift = norm_backward(
            r.mid[rw, :], r.st[rw, 4:5], r.st[rw, 5:6], r.dn[rw, :], r.v24[3:4, :]
        )
        d = dy + dx
        low = d.astype(BF16)
        r.mid[rw, :] = d
        r.dm[rw, :] = low
        r.gv[3:4, :] += gain
        r.gv[4:5, :] += shift
        r.gv[5:6, :] += jnp.sum(dy, axis=0, keepdims=True)
        r.gv[2:3, :] += jnp.sum(low.astype(F32), axis=0, keepdims=True)

    def grad_proj(j):
        rw = rows_of(j)
        put_a(3, rw, dot_tn(r.att[:, rw], r.dm[...]).astype(BF16))

    def grad_att(f):
        rw = rows_of(f)
        w = jnp.concatenate(natural(wa_m, (3,), pl.ds(0, 768)), axis=1)
        r.n2[rw, :] = dot_nt(r.dm[rw, :], w).astype(BF16)

    def attention_backward(t, f, pair):
        rw = rows_of(f)
        q2 = r.packed[rw, part(t, 0, pair)] * jnp.asarray(0.125, BF16)
        k2 = r.packed[rw, part(t, 1, pair)]
        v2 = r.packed[rw, part(t, 2, pair)]
        qs, ds, ks = two_heads(q2), two_heads(r.n2[rw, head_cols(t, pair)]), two_heads(k2)
        at = f * 6 + 2 * t + pair
        log_total = jnp.concatenate([r.lse[at, 0:1, :], r.lse[at, 1:2, :]], axis=1)
        probs = jnp.exp(dot_nt(k2, qs) - log_total)
        prod = probs * dot_nt(v2, ds)
        row_dot = jnp.sum(prod, axis=0, keepdims=True)
        d_scores = (prod - probs * row_dot).astype(BF16)
        r.packed[rw, part(t, 2, pair)] = dot_nn(probs.astype(BF16), ds).astype(BF16)
        r.packed[rw, part(t, 1, pair)] = dot_nn(d_scores, qs).astype(BF16)
        stacked = jnp.concatenate([d_scores[:, :WIN], d_scores[:, WIN:]], axis=0)
        r.packed[rw, part(t, 0, pair)] = (dot_tn(stacked, ks) * 0.125).astype(BF16)

    def heads_backward(t):
        def body(f):
            for pair in range(2):
                attention_backward(t, f, pair)

        return body

    def grad_qkv(t):
        cols = tile(t)
        d = r.packed[:, cols]
        put_a(t, slice(None), dot_nn(r.tr[...], d).astype(BF16))
        r.gbqkv[:, cols] = jnp.sum(d.astype(F32), axis=0, keepdims=True)

    def grad_norm_one(n):
        rw = rows_of(n)
        parts = []
        for t in range(3):
            parts += natural(wa_m, (t,), rw)
        w = jnp.concatenate(parts, axis=1)
        for i in range(4):
            s = slice(WIN * i, WIN * (i + 1))
            r.dn[s, rw] = dot_nt(r.packed[s, :], w)

    def grad_mixed(f):
        rw = rows_of(f)
        dx, gain, shift = norm_backward(
            mixed_in(f), r.st[rw, 2:3], r.st[rw, 3:4], r.dn[rw, :], r.v24[0:1, :]
        )
        d = r.mid[rw, :] + dx
        chosen = r.st[rw, 0:1] > 0
        r.dn[rw, :] = jnp.where(chosen, 0.0, d)
        r.gv[0:1, :] += gain
        r.gv[1:2, :] += shift
        r.gv[6:7, :] += jnp.sum(jnp.where(chosen, d, 0.0), axis=0, keepdims=True)

    loads = [
        pltpu.make_async_copy(r.og_in, r.dm, r.ld.at[0]),
        pltpu.make_async_copy(r.tok_in, r.tok, r.ld.at[1]),
    ]
    for q in range(2):
        loads.append(
            pltpu.make_async_copy(
                r.s2w.at[:, pl.ds(COLS * q, COLS)], w2_shard.at[q, zpos, xy, core], r.ld.at[2 + q]
            )
        )
    loads.append(pltpu.make_async_copy(r.small, r.sv.at[zpos, xy, core], r.ld.at[4]))
    for copy in loads:
        copy.start()

    for land in (r.lz, r.l3):
        for slot in range(land.shape[0]):
            land[slot, 0] = jnp.zeros_like(land[slot, 0])
            land[slot, 2] = jnp.zeros_like(land[slot, 2])

    barrier = pltpu.get_barrier_semaphore()
    peers = [sib, x_dev, y_dev, z_dev(1), z_dev(2), z_dev(3)]
    for dev in peers:
        pl.semaphore_signal(barrier, inc=1, device_id=(dev,), device_id_type=MESH_ID)

    def shard_half(t, half):
        ref, first = (r.sq, 0) if t < 3 else ((r.sp, 0) if t == 3 else (r.s1w, t - 4))
        parts = []
        for g in range(3):
            base = 768 * g + 256 * t if t < 3 else 768 * first + 256 * g
            a = ref[:, base : base + LANES].astype(F32)
            b = ref[:, base + LANES : base + 2 * LANES].astype(F32)
            parts.append(jnp.where(half == 0, a, b))
        return jnp.concatenate(parts, axis=1)

    for t in range(8):
        away = jnp.concatenate([shard_half(t, other), jnp.zeros((8, COLS), F32)], axis=0)
        r.l0[0, t // 4, t % 4, 0:32] = away.astype(BF16)
    pl.semaphore_wait(barrier, len(peers))
    away, came = [r.l0.at[i, pl.ds(0, 2), :, pl.ds(0, 32)] for i in range(2)]
    swap = remote(away, came, r.prep.at[0], r.prep.at[1], sib)
    swap.start()
    loads[4].wait()
    ag_a(0)
    swap.wait()
    for t in range(8):
        here = shard_half(t, core)
        there = r.l0[1, t // 4, t % 4, 0:32].astype(F32)[:24]
        block = jnp.concatenate(
            [jnp.where(core == 0, here, there), jnp.where(core == 0, there, here)], axis=0
        ).astype(BF16)
        if t < 4:
            wa_v[core, t, zpos, xy] = block
        else:
            w1_v[core, t - 4, zpos, xy] = block
        if t + 1 < ahead:
            ag_a(t + 1)
    ag_step(-1)
    loads[2].wait()
    loads[3].wait()
    def ag(*numbers):
        def go():
            for s in numbers:
                ag_step(s)

        return go

    def rs(*numbers):
        def go():
            for s in numbers:
                rs_step(s)

        return go

    def arrive(p, *numbers):
        def go():
            ag(*numbers)()
            ag_e(p)

        return go

    ag_step(0)
    masks()
    ag_step(1)
    loads[0].wait()
    loop(4, mask_grad)
    ag_step(2)
    ag_e(0)
    ag_step(3)
    loads[1].wait()
    spread_small()
    loop(4, ln1)
    ag_e(1)
    loop(3, heads_forward, [arrive(2, 4), arrive(3, 5), ag(6)])
    arrive(4)()
    loop(4, project, [None, ag(7), None, None])
    keep_middle = pltpu.make_async_copy(r.mid, r.ig, r.ld.at[5])
    keep_middle.start()
    arrive(5)()
    loop(4, fc1, [arrive(6, 8), arrive(7, 9), arrive(8, 10), ag(11)])
    loop(4, turn(1))
    loop(4, grad_fc2, [ag(12), None, ag(13), ag(14)])
    rs_step(0)
    for p in range(PIECES + 1):
        if p >= 9:
            ag_e(p)
        ag_f(p)
    rs_step(1)
    loop(4, grad_pre, [None, None, rs(2), None])
    loop(3, grad_norm_two, [rs(3), None, None])
    loop(4, grad_fc1, [rs(4), None, None, rs(5)])
    keep_middle.wait()
    loop(4, grad_middle)
    loop(3, grad_proj)
    rs_step(6)
    loop(4, grad_att)
    loop(4, turn(0))
    loop(4, heads_backward(0), [rs(7), None, None, rs(8)])
    grad_qkv(0)
    loop(4, heads_backward(1), [None, rs(9), None, None])
    grad_qkv(1)
    rs_step(10)
    loop(4, heads_backward(2), [None, None, rs(11), None])
    grad_qkv(2)
    rs_step(12)
    loop(3, grad_norm_one, [None, None, rs(13)])
    loop(4, grad_mixed)
    load_middle = pltpu.make_async_copy(r.ig, r.mid, r.ld.at[6])
    load_middle.start()
    collect_small()
    rs_step(14)
    load_middle.wait()
    write_grad = pltpu.make_async_copy(r.dn, r.ig, r.ld.at[7])
    write_grad.start()
    loop(3, fc2, [rs(15), rs(16), rs(17)])
    write_out = pltpu.make_async_copy(r.n2, r.bo, r.ld.at[0])
    write_out.start()
    for s in range(18, 21):
        rs_step(s)
    write_grad.wait()
    write_out.wait()


HAND_PARTS = 4


def hand_over(*refs):
    arrays, small, outs = refs[:6], refs[6], refs[7:13]
    vectors, held, (in_sems, out_sems) = refs[13:-8], refs[-8:-2], refs[-2:]
    loads, stores = [], []
    for src, buf, dst in zip(arrays, held, outs):
        parts = HAND_PARTS if src.shape[0] == 1024 else 1
        rows = src.shape[0] // parts
        for i in range(parts):
            at, n = pl.ds(rows * i, rows), len(loads)
            loads.append(pltpu.make_async_copy(src.at[at], buf.at[at], in_sems.at[n]))
            stores.append(pltpu.make_async_copy(buf.at[at], dst.at[at], out_sems.at[n]))
    for copy in loads:
        copy.start()
    for ref, (_, row, lane0, width) in zip(vectors, SMALL_ROWS):
        ref[...] = small[row : row + 1, lane0 : lane0 + width]
    for load, store in zip(loads, stores):
        load.wait()
        store.start()
    for copy in stores:
        copy.wait()


def fused_device(
    tokens,
    mask_bits,
    pad_flags,
    ln1_gain,
    ln1_bias,
    qkv_weight,
    qkv_bias,
    proj_weight,
    proj_bias,
    ln2_gain,
    ln2_bias,
    fc1_weight,
    fc1_bias,
    fc2_weight,
    fc2_bias,
    mask_embed,
    out_grad,
):
    held = dict(
        ln1_gain=ln1_gain,
        ln1_bias=ln1_bias,
        proj_bias=proj_bias,
        ln2_gain=ln2_gain,
        ln2_bias=ln2_bias,
        fc2_bias=fc2_bias,
        mask_embed=mask_embed,
        qkv_bias=qkv_bias,
        fc1_bias=fc1_bias,
    )
    small = jnp.zeros((8 * LANES,), F32)
    for name, row, lane0, width in SMALL_ROWS:
        first = row * LANES + lane0
        small = small + jnp.pad(held[name].astype(F32), (first, 8 * LANES - first - width))
    small = small.reshape(8, LANES)
    any_spec = pl.BlockSpec(memory_space=pl.ANY)
    vmem = pl.BlockSpec(memory_space=pltpu.VMEM)
    smem = pl.BlockSpec(memory_space=pltpu.SMEM)
    shape = jax.ShapeDtypeStruct
    outs = pl.pallas_call(
        fused_kernel,
        out_shape=(
            shape((1024, 768), BF16),
            shape((1024, 768), F32),
            shape((24, 2304), F32),
            shape((24, 768), F32),
            shape((24, 3072), F32),
            shape((96, 768), F32),
            shape((8, LANES), F32),
        ),
        in_specs=[any_spec, any_spec, vmem, smem, any_spec, vmem, vmem, vmem, any_spec],
        out_specs=(any_spec, any_spec, vmem, vmem, vmem, vmem, vmem),
        scratch_shapes=[pltpu.VMEM(*spec) for spec in SCRATCH.values()] + list(SEMS.values()),
        compiler_params=pltpu.CompilerParams(
            collective_id=0, has_side_effects=True, vmem_limit_bytes=64 * 2**20
        ),
    )(
        tokens,
        out_grad,
        mask_bits.reshape(8, LANES),
        pad_flags,
        small,
        qkv_weight,
        proj_weight,
        fc1_weight,
        fc2_weight,
    )
    held = pl.pallas_call(
        hand_over,
        out_shape=tuple(shape(o.shape, o.dtype) for o in outs[:6])
        + tuple(shape((1, width), F32) for _, _, _, width in SMALL_ROWS),
        in_specs=[any_spec] * 6 + [vmem],
        out_specs=(any_spec,) * 6 + (vmem,) * len(SMALL_ROWS),
        scratch_shapes=[pltpu.VMEM(o.shape, o.dtype) for o in outs[:6]]
        + [pltpu.SemaphoreType.DMA((6 * HAND_PARTS,)), pltpu.SemaphoreType.DMA((6 * HAND_PARTS,))],
        compiler_params=pltpu.CompilerParams(vmem_limit_bytes=63 * 2**20),
    )(*outs)
    block_out, input_grad, gq, gpj, g1, g2 = held[:6]
    v = {entry[0]: vec.reshape(entry[3]) for entry, vec in zip(SMALL_ROWS, held[6:])}
    return (
        block_out,
        input_grad,
        v["ln1_gain"],
        v["ln1_bias"],
        gq,
        v["qkv_bias"],
        gpj,
        v["proj_bias"],
        v["ln2_gain"],
        v["ln2_bias"],
        g1,
        v["fc1_bias"],
        g2,
        v["fc2_bias"],
        v["mask_embed"],
    )


def solution(mesh):
    placed = (
        P("fsdp", None),
        P("fsdp"),
        P("fsdp"),
        P("fsdp"),
        P("fsdp"),
        P("fsdp", None),
        P("fsdp"),
        P("fsdp", None),
        P("fsdp"),
        P("fsdp"),
        P("fsdp"),
        P("fsdp", None),
        P("fsdp"),
        P("fsdp", None),
        P("fsdp"),
        P("fsdp"),
        P("fsdp", None),
    )
    return jax.shard_map(
        fused_device if mesh.shape["fsdp"] == 32 else per_device,
        mesh=mesh,
        in_specs=placed,
        out_specs=(
            P("fsdp", None),
            P("fsdp", None),
            P("fsdp"),
            P("fsdp"),
            P("fsdp", None),
            P("fsdp"),
            P("fsdp", None),
            P("fsdp"),
            P("fsdp"),
            P("fsdp"),
            P("fsdp", None),
            P("fsdp"),
            P("fsdp", None),
            P("fsdp"),
            P("fsdp"),
        ),
        check_vma=False,
    )
```

```python
import functools

import jax
import jax.numpy as jnp
from jax import lax
from jax.experimental import pallas as pl
from jax.experimental.pallas import tpu as pltpu
from jax.sharding import PartitionSpec as P

HEADS = 12
HEAD_DIM = 64
WIN = 256


epsilon = 1e-06


def norm_rows(values, gain_vec, shift_vec):
    row_mean = jnp.mean(values, axis=-1, keepdims=True)
    centered = values - row_mean
    variance = jnp.mean(centered * centered, axis=-1, keepdims=True)
    return centered * lax.rsqrt(variance + epsilon) * gain_vec + shift_vec


def gelu_exact(values):
    return jax.nn.gelu(values, approximate=False)


def forward_pass(full, tok_rows, masked):
    (
        gain_one,
        shift_one,
        qkv_w,
        qkv_b,
        proj_w,
        proj_b,
        gain_two,
        shift_two,
        up_w,
        up_b,
        down_w,
        down_b,
        mask_vec,
    ) = full
    row_count = tok_rows.shape[0]
    width = tok_rows.shape[1]
    frames = row_count // WIN
    mixed_in = jnp.where(
        masked[:, None] > 0, mask_vec.astype(jnp.float32)[None, :], tok_rows.astype(jnp.float32)
    )
    normed = norm_rows(
        mixed_in, gain_one.astype(jnp.float32), shift_one.astype(jnp.float32)
    ).astype(jnp.bfloat16)
    packed = (
        jnp.dot(normed, qkv_w, preferred_element_type=jnp.float32) + qkv_b.astype(jnp.float32)
    ).astype(jnp.bfloat16)
    heads_view = packed.reshape(frames, WIN, 3, HEADS, HEAD_DIM)
    scores = jnp.einsum(
        "fqhd,fkhd->fhqk",
        heads_view[:, :, 0],
        heads_view[:, :, 1],
        preferred_element_type=jnp.float32,
    ) * HEAD_DIM ** (-0.5)
    row_max = jnp.max(scores, axis=-1, keepdims=True)
    exp_terms = jnp.exp(scores - row_max)
    row_total = jnp.sum(exp_terms, axis=-1, keepdims=True)
    probs_low = (exp_terms / row_total).astype(jnp.bfloat16)
    log_total = row_max + jnp.log(row_total)
    attended = jnp.einsum(
        "fhqk,fkhd->fqhd", probs_low, heads_view[:, :, 2], preferred_element_type=jnp.float32
    )
    attended = attended.reshape(row_count, width).astype(jnp.bfloat16)
    middle = (
        mixed_in
        + jnp.dot(attended, proj_w, preferred_element_type=jnp.float32)
        + proj_b.astype(jnp.float32)
    )
    normed_two = norm_rows(
        middle, gain_two.astype(jnp.float32), shift_two.astype(jnp.float32)
    ).astype(jnp.bfloat16)
    hidden_pre = jnp.dot(normed_two, up_w, preferred_element_type=jnp.float32) + up_b.astype(
        jnp.float32
    )
    hidden_act = gelu_exact(hidden_pre).astype(jnp.bfloat16)
    result = (
        middle
        + jnp.dot(hidden_act, down_w, preferred_element_type=jnp.float32)
        + down_b.astype(jnp.float32)
    )
    saved = (
        mixed_in,
        normed,
        packed,
        log_total,
        attended,
        middle,
        normed_two,
        hidden_pre,
        hidden_act,
    )
    return (result, saved)


def mlp_backward(full, saved, cotangent):
    (
        gain_one,
        shift_one,
        qkv_w,
        qkv_b,
        proj_w,
        proj_b,
        gain_two,
        shift_two,
        up_w,
        up_b,
        down_w,
        down_b,
        mask_vec,
    ) = full
    mixed_in, normed, packed, log_total, attended, middle, normed_two, hidden_pre, hidden_act = (
        saved
    )
    down_in = cotangent.astype(jnp.bfloat16)
    grad_down = jnp.einsum("tf,td->fd", hidden_act, down_in, preferred_element_type=jnp.float32)
    grad_down_b = jnp.sum(down_in.astype(jnp.float32), axis=0)
    grad_act = jnp.einsum("td,fd->tf", down_in, down_w, preferred_element_type=jnp.float32)
    gelu_value, gelu_pull = jax.vjp(gelu_exact, hidden_pre)
    grad_pre = gelu_pull(grad_act)[0].astype(jnp.bfloat16)
    grad_up = jnp.einsum("td,tf->df", normed_two, grad_pre, preferred_element_type=jnp.float32)
    grad_up_b = jnp.sum(grad_pre.astype(jnp.float32), axis=0)
    grad_norm_two = jnp.einsum("tf,df->td", grad_pre, up_w, preferred_element_type=jnp.float32)
    norm_value, norm_pull = jax.vjp(
        norm_rows, middle, gain_two.astype(jnp.float32), shift_two.astype(jnp.float32)
    )
    grad_middle, grad_gain_two, grad_shift_two = norm_pull(grad_norm_two)
    grad_middle = grad_middle + cotangent
    return (
        grad_middle,
        (grad_gain_two, grad_shift_two, grad_up, grad_up_b, grad_down, grad_down_b),
    )


def attn_backward(full, saved, grad_middle, masked):
    (
        gain_one,
        shift_one,
        qkv_w,
        qkv_b,
        proj_w,
        proj_b,
        gain_two,
        shift_two,
        up_w,
        up_b,
        down_w,
        down_b,
        mask_vec,
    ) = full
    mixed_in, normed, packed, log_total, attended, middle, normed_two, hidden_pre, hidden_act = (
        saved
    )
    row_count = grad_middle.shape[0]
    width = grad_middle.shape[1]
    frames = row_count // WIN
    proj_in = grad_middle.astype(jnp.bfloat16)
    grad_proj = jnp.einsum("td,te->de", attended, proj_in, preferred_element_type=jnp.float32)
    grad_proj_b = jnp.sum(proj_in.astype(jnp.float32), axis=0)
    grad_att = jnp.einsum("te,de->td", proj_in, proj_w, preferred_element_type=jnp.float32).astype(
        jnp.bfloat16
    )
    grad_att = grad_att.reshape(frames, WIN, HEADS, HEAD_DIM)
    heads_view = packed.reshape(frames, WIN, 3, HEADS, HEAD_DIM)
    query_part = heads_view[:, :, 0]
    key_part = heads_view[:, :, 1]
    value_part = heads_view[:, :, 2]
    score_scale = HEAD_DIM ** (-0.5)
    scores = (
        jnp.einsum("fqhd,fkhd->fhqk", query_part, key_part, preferred_element_type=jnp.float32)
        * score_scale
    )
    probs_full = jnp.exp(scores - log_total)
    probs_low = probs_full.astype(jnp.bfloat16)
    grad_value = jnp.einsum(
        "fhqk,fqhd->fkhd", probs_low, grad_att, preferred_element_type=jnp.float32
    )
    grad_probs = jnp.einsum(
        "fqhd,fkhd->fhqk", grad_att, value_part, preferred_element_type=jnp.float32
    )
    row_dot = jnp.sum(grad_probs * probs_full, axis=-1, keepdims=True)
    grad_scores = (probs_full * (grad_probs - row_dot)).astype(jnp.bfloat16)
    grad_query = (
        jnp.einsum("fhqk,fkhd->fqhd", grad_scores, key_part, preferred_element_type=jnp.float32)
        * score_scale
    )
    grad_key = (
        jnp.einsum("fhqk,fqhd->fkhd", grad_scores, query_part, preferred_element_type=jnp.float32)
        * score_scale
    )
    grad_packed = (
        jnp.stack([grad_query, grad_key, grad_value], axis=2)
        .reshape(row_count, 3 * width)
        .astype(jnp.bfloat16)
    )
    grad_qkv = jnp.einsum("td,te->de", normed, grad_packed, preferred_element_type=jnp.float32)
    grad_qkv_b = jnp.sum(grad_packed.astype(jnp.float32), axis=0)
    grad_normed = jnp.einsum("te,de->td", grad_packed, qkv_w, preferred_element_type=jnp.float32)
    first_value, first_pull = jax.vjp(
        norm_rows, mixed_in, gain_one.astype(jnp.float32), shift_one.astype(jnp.float32)
    )
    grad_mixed, grad_gain_one, grad_shift_one = first_pull(grad_normed)
    grad_mixed = grad_mixed + grad_middle
    chosen = masked[:, None] > 0
    tok_grad = jnp.where(chosen, 0.0, grad_mixed)
    grad_mask = jnp.sum(jnp.where(chosen, grad_mixed, 0.0), axis=0)
    return (
        tok_grad,
        (grad_gain_one, grad_shift_one, grad_qkv, grad_qkv_b, grad_proj, grad_proj_b, grad_mask),
    )


def per_device(
    tokens,
    mask_bits,
    pad_flags,
    ln1_gain,
    ln1_bias,
    qkv_weight,
    qkv_bias,
    proj_weight,
    proj_bias,
    ln2_gain,
    ln2_bias,
    fc1_weight,
    fc1_bias,
    fc2_weight,
    fc2_bias,
    mask_embed,
    out_grad,
):
    full = (
        lax.all_gather(ln1_gain, "fsdp", axis=0, tiled=True),
        lax.all_gather(ln1_bias, "fsdp", axis=0, tiled=True),
        lax.all_gather(qkv_weight, "fsdp", axis=0, tiled=True),
        lax.all_gather(qkv_bias, "fsdp", axis=0, tiled=True),
        lax.all_gather(proj_weight, "fsdp", axis=0, tiled=True),
        lax.all_gather(proj_bias, "fsdp", axis=0, tiled=True),
        lax.all_gather(ln2_gain, "fsdp", axis=0, tiled=True),
        lax.all_gather(ln2_bias, "fsdp", axis=0, tiled=True),
        lax.all_gather(fc1_weight, "fsdp", axis=0, tiled=True),
        lax.all_gather(fc1_bias, "fsdp", axis=0, tiled=True),
        lax.all_gather(fc2_weight, "fsdp", axis=0, tiled=True),
        lax.all_gather(fc2_bias, "fsdp", axis=0, tiled=True),
        lax.all_gather(mask_embed, "fsdp", axis=0, tiled=True),
    )
    result, saved = forward_pass(full, tokens, mask_bits)
    full_back = (
        lax.all_gather(ln1_gain, "fsdp", axis=0, tiled=True),
        lax.all_gather(ln1_bias, "fsdp", axis=0, tiled=True),
        lax.all_gather(qkv_weight, "fsdp", axis=0, tiled=True),
        lax.all_gather(qkv_bias, "fsdp", axis=0, tiled=True),
        lax.all_gather(proj_weight, "fsdp", axis=0, tiled=True),
        lax.all_gather(proj_bias, "fsdp", axis=0, tiled=True),
        lax.all_gather(ln2_gain, "fsdp", axis=0, tiled=True),
        lax.all_gather(ln2_bias, "fsdp", axis=0, tiled=True),
        lax.all_gather(fc1_weight, "fsdp", axis=0, tiled=True),
        lax.all_gather(fc1_bias, "fsdp", axis=0, tiled=True),
        lax.all_gather(fc2_weight, "fsdp", axis=0, tiled=True),
        lax.all_gather(fc2_bias, "fsdp", axis=0, tiled=True),
        lax.all_gather(mask_embed, "fsdp", axis=0, tiled=True),
    )
    kept_acts = forward_pass(full_back, tokens, mask_bits)[1]
    row_count = tokens.shape[0]
    frames = row_count // WIN
    frame_keep = (1 - pad_flags).astype(jnp.float32)
    tok_weight = (mask_bits.astype(jnp.float32).reshape(frames, WIN) * frame_keep[:, None]).reshape(
        row_count
    )
    cotangent = out_grad.astype(jnp.float32) * tok_weight[:, None]
    grad_middle, mlp_grads = mlp_backward(full_back, kept_acts, cotangent)
    tok_grad, attn_grads = attn_backward(full_back, kept_acts, grad_middle, mask_bits)
    shares = (
        lax.psum_scatter(attn_grads[0], "fsdp", scatter_dimension=0, tiled=True),
        lax.psum_scatter(attn_grads[1], "fsdp", scatter_dimension=0, tiled=True),
        lax.psum_scatter(attn_grads[2], "fsdp", scatter_dimension=0, tiled=True),
        lax.psum_scatter(attn_grads[3], "fsdp", scatter_dimension=0, tiled=True),
        lax.psum_scatter(attn_grads[4], "fsdp", scatter_dimension=0, tiled=True),
        lax.psum_scatter(attn_grads[5], "fsdp", scatter_dimension=0, tiled=True),
        lax.psum_scatter(mlp_grads[0], "fsdp", scatter_dimension=0, tiled=True),
        lax.psum_scatter(mlp_grads[1], "fsdp", scatter_dimension=0, tiled=True),
        lax.psum_scatter(mlp_grads[2], "fsdp", scatter_dimension=0, tiled=True),
        lax.psum_scatter(mlp_grads[3], "fsdp", scatter_dimension=0, tiled=True),
        lax.psum_scatter(mlp_grads[4], "fsdp", scatter_dimension=0, tiled=True),
        lax.psum_scatter(mlp_grads[5], "fsdp", scatter_dimension=0, tiled=True),
        lax.psum_scatter(attn_grads[6], "fsdp", scatter_dimension=0, tiled=True),
    )
    return (
        result.astype(jnp.bfloat16),
        tok_grad,
        shares[0],
        shares[1],
        shares[2],
        shares[3],
        shares[4],
        shares[5],
        shares[6],
        shares[7],
        shares[8],
        shares[9],
        shares[10],
        shares[11],
        shares[12],
    )


F32 = jnp.float32
BF16 = jnp.bfloat16
LANES = 128
ROWS = 48
COLS = 384
PIECES = 12
CUT = 16
RINGS = dict(l0=2, l1=4, lz=4, lt=4, l2=4, l3=4)
CREDIT_RINGS = ["l0", "l1", "lt", "l2", "l2"] + ["lz"] * 4 + ["l3"] * 4
SHORT = 11
LONG_AT = (0, 2, 5, 8, 11, 14, 17, 20, 22, 23)
SHORT_AT = (0, 2, 5, 8, 11, 13, 14)
STARTS = (0, 1, 3, 5, 8, 10, 13, 16, 19, 22, 25, 30, 36)
MESH_ID = pl.DeviceIdType.MESH


def dot_nn(a, b):
    return lax.dot_general(a, b, (((1,), (0,)), ((), ())), preferred_element_type=F32)


def dot_nt(a, b):
    return lax.dot_general(a, b, (((1,), (1,)), ((), ())), preferred_element_type=F32)


def dot_tn(a, b):
    return lax.dot_general(a, b, (((0,), (0,)), ((), ())), preferred_element_type=F32)


def row_stats(values):
    row_mean = jnp.mean(values, axis=-1, keepdims=True)
    centered = values - row_mean
    return row_mean, lax.rsqrt(jnp.mean(centered * centered, axis=-1, keepdims=True) + epsilon)


def gelu_and_slope(x):
    phi = 0.5 + 0.5 * lax.erf(x * 0.7071067811865476)
    return x * phi, phi + x * jnp.exp(x * x * -0.5) * 0.3989422804014327


def norm_backward(x, row_mean, row_scale, grad, gain):
    x_hat = (x - row_mean) * row_scale
    prod = grad * x_hat
    grad_gain = jnp.sum(prod, axis=0, keepdims=True)
    grad_shift = jnp.sum(grad, axis=0, keepdims=True)
    dx = grad * gain
    mean_one = jnp.mean(dx, axis=-1, keepdims=True)
    mean_two = jnp.mean(dx * x_hat, axis=-1, keepdims=True)
    return row_scale * (dx - mean_one - x_hat * mean_two), grad_gain, grad_shift


SMALL_ROWS = (
    ("ln1_gain", 0, 0, 24),
    ("ln1_bias", 0, 24, 24),
    ("proj_bias", 0, 48, 24),
    ("ln2_gain", 0, 72, 24),
    ("ln2_bias", 0, 96, 24),
    ("fc2_bias", 1, 0, 24),
    ("mask_embed", 1, 24, 24),
    ("qkv_bias", 1, 48, 72),
    ("fc1_bias", 2, 0, 96),
)


def spread_tables(lane0, width):
    count = 32 * width
    k = lax.broadcasted_iota(jnp.int32, (1, count), 1)
    pick = lax.broadcasted_iota(jnp.int32, (LANES, count), 0) == lax.rem(k, width) + lane0
    owner = lax.broadcasted_iota(jnp.int32, (32, count), 0) == lax.div(k, width)
    return jnp.where(pick, 1.0, 0.0).astype(BF16), owner


SCRATCH = dict(
    tok=((1024, 768), BF16),
    dm=((1024, 768), BF16),
    st=((1024, 8), F32),
    v24=((8, 768), F32),
    bqkv=((1, 2304), F32),
    bfc1=((1, 3072), F32),
    gv=((8, 768), F32),
    gbqkv=((1, 2304), F32),
    gbfc1=((1, 3072), F32),
    normed=((1024, 768), BF16),
    n2=((1024, 768), BF16),
    tr=((768, 1024), BF16),
    packed=((1024, 2304), BF16),
    att=((1024, 768), BF16),
    mid=((1024, 768), F32),
    hact=((1024, 3072), BF16),
    gp=((11, 768, COLS), BF16),
    dn=((1024, 768), F32),
    lse=((24, 8, 256), F32),
    wa=((8, 768, COLS), BF16),
    w1=((8, 768, COLS), BF16),
    w2=((8, 768, COLS), BF16),
    g2=((8, 768, COLS), BF16),
    sv=((4, 4, 2, 8, LANES), F32),
    sg=((4, 4, 2, 8, LANES), F32),
    fs=((8, ROWS, COLS), F32),
    fr=((8, ROWS // 2, COLS), F32),
    l0=((RINGS["l0"], 4, 4, ROWS, COLS), BF16),
    l1=((RINGS["l1"], 4, CUT, COLS), BF16),
    lz=((RINGS["lz"], 4, ROWS - CUT, COLS), BF16),
    lt=((RINGS["lt"], ROWS - CUT, COLS), BF16),
    l2=((RINGS["l2"], 2, 4, ROWS, COLS), BF16),
    l3=((RINGS["l3"], 4, ROWS, COLS), BF16),
    l1s=((4, ROWS, COLS), BF16),
    l3s=((4, ROWS, COLS), BF16),
    s0=((4, 4, 8, LANES), F32),
    s1=((4, 8, LANES), F32),
    s2=((2, 4, 8, LANES), F32),
    s3=((4, 8, LANES), F32),
)
SEMS = dict(
    ld=pltpu.SemaphoreType.DMA((8,)),
    prep=pltpu.SemaphoreType.DMA((2,)),
    sent=pltpu.SemaphoreType.DMA((PIECES + 1, 14)),
    came=pltpu.SemaphoreType.DMA((PIECES + 1, 14)),
    credit=pltpu.SemaphoreType.REGULAR((26,)),
)


class Refs:
    pass


def fused_kernel(*refs):
    r = Refs()
    names = ["tok_in", "og_in", "mask", "pad", "small", "sq", "sp", "s1w", "s2w"]
    names += ["bo", "ig", "oq", "op", "o1", "o2", "osm"]
    names += list(SCRATCH) + list(SEMS)
    for name, ref in zip(names, refs):
        setattr(r, name, ref)

    me = lax.axis_index("fsdp")
    core = lax.rem(me, 2)
    other = 1 - core
    chip = lax.div(me, 2)
    xpos = lax.rem(chip, 2)
    ypos = lax.rem(lax.div(chip, 2), 2)
    zpos = lax.div(chip, 4)
    xy = lax.rem(chip, 4)
    xy_x = xy + 1 - 2 * xpos
    xy_y = xy + 2 - 4 * ypos
    xy_d = xy_x + 2 - 4 * ypos
    sib = me + 1 - 2 * core
    x_dev = me + 2 - 4 * xpos
    y_dev = me + 4 - 8 * ypos

    def z_of(k):
        return lax.rem(zpos + k, 4)

    def z_dev(k):
        return me + 8 * (z_of(k) - zpos)

    def remote(src, dst, ssem, rsem, dev):
        return pltpu.make_async_remote_copy(
            src_ref=src,
            dst_ref=dst,
            send_sem=ssem,
            recv_sem=rsem,
            device_id=(dev,),
            device_id_type=MESH_ID,
        )

    wa_v = r.wa.reshape(2, 4, 4, 4, ROWS, COLS)
    w1_v = r.w1.reshape(2, 4, 4, 4, ROWS, COLS)
    w2_v = r.w2.reshape(2, 4, 4, 2, 2, ROWS, COLS)
    w2_shard = r.w2.reshape(2, 4, 4, 2, 2 * ROWS, COLS)
    w2_m = r.w2.reshape(2, 3072, COLS)
    wa_m = r.wa.reshape(2, 4, 768, COLS)
    w1_m = r.w1.reshape(2, 4, 768, COLS)
    g2_v = r.g2.reshape(2, 4, 4, 2, 2, ROWS, COLS)
    g2_m = r.g2.reshape(2, 3072, COLS)
    ga_v = r.gp.reshape(11, 4, 4, ROWS, COLS)
    gp_m = r.gp.reshape(11 * 768, COLS)

    def weight_piece(p, half):
        if p == 0:
            return r.sv.at[:, :, half]
        if p <= 4:
            return wa_v.at[half, p - 1]
        if p <= 8:
            return w1_v.at[half, p - 5]
        return w2_v.at[(p - 9) % 2, :, :, half, (p - 9) // 2]

    def grad_piece(p, half):
        if p == 0:
            return r.sg.at[:, :, half]
        if p <= 4:
            return ga_v.at[half * 4 + p - 1]
        if p <= 8:
            return w1_v.at[half, p - 5]
        return g2_v.at[(p - 9) % 2, :, :, half, (p - 9) // 2]

    def ag_copy(p, i, src, dst, dev):
        return remote(src, dst, r.sent.at[p, i], r.came.at[p, i], dev)

    def rows_one(p):
        return pl.ds(0, CUT) if p else pl.ds(0, 8)

    def rs_rows_one(n):
        return pl.ds(0, ROWS) if SHORT <= n < PIECES else rows_one(order[n])

    rows_two = pl.ds(CUT, ROWS - CUT)

    def sides(p):
        along_x, along_y = (x_dev, xy_x), (y_dev, xy_y)
        return (along_x, along_y) if p % 2 == 0 else (along_y, along_x)

    at_start, at_end = zpos == 0, zpos == 3
    inside = jnp.logical_and(zpos > 0, zpos < 3)

    def along_z(fn):
        pl.when(jnp.logical_not(at_end))(lambda: fn(1))
        fn(2)
        pl.when(jnp.logical_not(at_start))(lambda: fn(3))

    def pass_to_end(fn):
        pl.when(zpos == 1)(lambda: fn(3, 3))
        pl.when(zpos == 2)(lambda: fn(0, 1))

    def ag_z(p, k, at):
        return ag_copy(p, k - 1, at, at, z_dev(k))

    def ag_z2(p, k, at):
        return ag_copy(p, 8 + k, at, at, z_dev(k))

    def ag_z_from(p, k, at, base=0):
        return ag_copy(p, base + k - 1, at, at, z_dev(k))

    def ag_pass(p, far, k, at, base=0):
        return ag_copy(p, base + (0 if k == 3 else 2), at, at, z_dev(k))

    def ag_x(p, k, v):
        at = v.at[z_of(4 - k), xy] if k else v.at[zpos, xy]
        return ag_copy(p, 4 if k else 3, at, at, x_dev)

    def ag_y(p, k, v):
        at = v.at[z_of(4 - k), xy] if k else v.at[zpos, xy]
        return ag_copy(p, 6 if k else 5, at, at, y_dev)

    def own_from(p, side, v):
        at = v.at[zpos, sides(p)[side][1]]
        return ag_copy(p, 3 if side == p % 2 else 5, at, at, sides(p)[side][0])

    def three_from(p, side, v):
        at = v.at[pl.ds(0, 3), sides(p)[side][1]]
        return ag_copy(p, 4 if side == p % 2 else 6, at, at, sides(p)[side][0])

    def ag_one(p, v, col):
        at = v.at[:, col, rows_one(p)]
        return ag_copy(p, 7, at, at, sides(p)[1][0])

    def ag_two(p, v, col):
        at = v.at[zpos, col, rows_two]
        return ag_copy(p, 8, at, at, sides(p)[0][0])

    def ag_a(p):
        v = weight_piece(p, core)
        along_z(lambda k: ag_z(p, k, v.at[zpos, xy]).start())
        ag_x(p, 0, v).start()
        ag_y(p, 0, v).start()

    def ag_b(p):
        v = weight_piece(p, core)
        for k in (1, 3):
            ag_z_from(p, k, v.at[z_of(4 - k), xy]).wait_recv()
            ag_x(p, k, v).start()
            ag_y(p, k, v).start()

    def ag_b2(p):
        v = weight_piece(p, core)
        ag_z_from(p, 2, v.at[z_of(2), xy]).wait_recv()
        pass_to_end(lambda far, k: ag_pass(p, far, k, v.at[far, xy]).start())
        ag_x(p, 2, v).start()
        ag_y(p, 2, v).start()

    def ag_c2(p):
        if p:
            v = weight_piece(p, core)
            own_from(p, 1, v).wait_recv()
            ag_two(p, v, sides(p)[1][1]).start()

    def ag_c3(p):
        if p:
            v = weight_piece(p, core)
            ag_two(p, v, xy_d).wait_recv()
            along_z(lambda k: ag_z2(p, k, v.at[zpos, xy_d, rows_two]).start())

    def ag_c1(p):
        v = weight_piece(p, core)
        own_from(p, 0, v).wait_recv()
        three_from(p, 0, v).wait_recv()
        ag_one(p, v, sides(p)[0][1]).start()

    def ag_c4(p):
        if p:
            v = weight_piece(p, core)
            ag_z_from(p, 2, v.at[z_of(2), xy_d, rows_two], 9).wait_recv()
            pass_to_end(
                lambda far, k: ag_pass(p, far, k, v.at[far, xy_d, rows_two], 9).start()
            )

    def ag_d(p):
        v = weight_piece(p, core)
        if p == 0:
            own_from(p, 1, v).wait_recv()
        three_from(p, 1, v).wait_recv()
        ag_one(p, v, xy_d).wait_recv()
        if p:
            for k in (1, 3):
                ag_z_from(p, k, v.at[z_of(4 - k), xy_d, rows_two], 9).wait_recv()
        ag_copy(p, 12, v, v, sib).start()

    def ag_e(p):
        v = weight_piece(p, other)
        ag_copy(p, 12, v, v, sib).wait_recv()

    def ag_f(p):
        v = weight_piece(p, core)
        along_z(lambda k: ag_z(p, k, v.at[zpos, xy]).wait_send())
        pass_to_end(lambda far, k: ag_pass(p, far, k, v.at[far, xy]).wait_send())
        ag_x(p, 0, v).wait_send()
        ag_y(p, 0, v).wait_send()
        three = v.at[pl.ds(0, 3), xy]
        ag_copy(p, 4, three, three, x_dev).wait_send()
        ag_copy(p, 6, three, three, y_dev).wait_send()
        ag_one(p, v, sides(p)[0][1]).wait_send()
        if p:
            ag_two(p, v, sides(p)[1][1]).wait_send()
            along_z(lambda k: ag_z2(p, k, v.at[zpos, xy_d, rows_two]).wait_send())
            pass_to_end(
                lambda far, k: ag_pass(p, far, k, v.at[far, xy_d, rows_two], 9).wait_send()
            )
        ag_copy(p, 12, v, v, sib).wait_send()

    ahead = 3

    def ag_step(s):
        for lag, stage in AG_STAGES:
            if 0 <= s - lag <= PIECES and not (lag < 0 and stage is ag_a and s - lag < ahead):
                stage(s - lag)

    AG_STAGES = (
        (-ahead, ag_a),
        (0, ag_b),
        (-1, ag_b2),
        (-1, ag_c2),
        (0, ag_c3),
        (1, ag_c1),
        (1, ag_c4),
        (2, ag_d),
    )

    order = [9, 10, 11, 12, 5, 6, 7, 8, 4, 1, 2, 3, 0]

    def rs_bufs(n):
        if n == PIECES:
            return r.s0, r.s1, r.s2, r.s3
        ring = [getattr(r, name).at[n % RINGS[name]] for name in ("l0", "l1", "l2", "l3")]
        if n >= SHORT:
            ring[1], ring[3] = r.l1s, r.l3s
        return tuple(ring)

    def rs_copy(n, i, src, dst, dev):
        return remote(src, dst, r.sent.at[n, i], r.came.at[n, i], dev)

    def credit_wait(n, i):
        if RINGS[CREDIT_RINGS[i]] <= n < (PIECES if i in (0, 3, 4) else SHORT):
            pl.semaphore_wait(r.credit.at[2 * i + n % 2], 1)

    def credit_give(n, i, dev):
        if n < (PIECES if i in (0, 3, 4) else SHORT) - RINGS[CREDIT_RINGS[i]]:
            at = r.credit.at[2 * i + n % 2]
            pl.semaphore_signal(at, inc=1, device_id=(dev,), device_id_type=MESH_ID)

    def add_to(g, at, landed):
        g[at] = (g[at].astype(F32) + landed.astype(F32)).astype(g.dtype)

    def z_send(n, first, block, land, k):
        return rs_copy(n, first + k - 1, block(z_of(k)), land.at[k - 1], z_dev(k))

    def z_far(n, first, block, land, k):
        return rs_copy(n, first + 3, block(3 if k == 1 else 0), land.at[3], z_dev(k))

    def sum_z_start(n, first, credit, block, land):
        def near(k):
            credit_wait(n, credit + k - 1)
            z_send(n, first, block, land, k).start()

        def far(k):
            near(2)
            credit_wait(n, credit + 3)
            z_far(n, first, block, land, k).start()

        pl.when(jnp.logical_not(at_end))(lambda: near(1))
        pl.when(jnp.logical_not(at_start))(lambda: near(3))
        pl.when(at_start)(lambda: far(1))
        pl.when(at_end)(lambda: far(3))

    def sum_z_pass(n, first, credit, block, land):
        def go():
            z_far(n, first, block, land, 1).wait_recv()
            add_to(block(z_of(2)), Ellipsis, land[3])
            pl.when(zpos == 1)(lambda: credit_give(n, credit + 3, z_dev(3)))
            pl.when(zpos == 2)(lambda: credit_give(n, credit + 3, z_dev(1)))
            credit_wait(n, credit + 1)
            z_send(n, first, block, land, 2).start()

        pl.when(inside)(go)

    def sum_z_end(n, first, credit, block, land):
        z_send(n, first, block, land, 2).wait_recv()
        pl.when(jnp.logical_not(at_start))(lambda: z_send(n, first, block, land, 1).wait_recv())
        pl.when(jnp.logical_not(at_end))(lambda: z_send(n, first, block, land, 3).wait_recv())
        total = land[0].astype(F32) + land[1].astype(F32) + land[2].astype(F32)

        def give():
            credit_give(n, credit + 1, z_dev(2))
            pl.when(jnp.logical_not(at_start))(lambda: credit_give(n, credit, z_dev(3)))
            pl.when(jnp.logical_not(at_end))(lambda: credit_give(n, credit + 2, z_dev(1)))

        return total, give

    def sum_z_sent(n, first, block, land):
        z_send(n, first, block, land, 2).wait_send()
        pl.when(jnp.logical_not(at_end))(lambda: z_send(n, first, block, land, 1).wait_send())
        pl.when(jnp.logical_not(at_start))(lambda: z_send(n, first, block, land, 3).wait_send())
        pl.when(at_start)(lambda: z_far(n, first, block, land, 1).wait_send())
        pl.when(at_end)(lambda: z_far(n, first, block, land, 3).wait_send())

    def diagonal(n):
        g = grad_piece(order[n], core)
        return lambda z: g.at[z, xy_d, rows_two], r.lz.at[n % RINGS["lz"]]

    def own_line(n):
        g = grad_piece(order[n], core)
        return lambda z: g.at[z, xy], rs_bufs(n)[3]

    def rs_main(n):
        p = order[n]
        g, land = grad_piece(p, core), rs_bufs(n)[2]
        (a_dev, a), (b_dev, b) = sides(n)
        one = rs_rows_one(n)
        early, late_one, late_two = [], [], []
        if n < SHORT:
            early.append((7, g.at[:, a, rows_two], land.at[0, :, rows_two], a_dev))
        late_one.append((7, g.at[:, a, one], land.at[0, :, one], a_dev))
        early.append((8, g.at[:, b, one], land.at[1, :, one], b_dev))
        if n < SHORT:
            for k in (1, 2, 3):
                z = z_of(k)
                early.append((8, g.at[z, b, rows_two], land.at[1, z, rows_two], b_dev))
            late_two.append((8, g.at[zpos, b, rows_two], land.at[1, zpos, rows_two], b_dev))
        return [[rs_copy(n, *entry) for entry in group] for group in (early, late_one, late_two)]

    def rs_all(n):
        g, land = grad_piece(order[n], core), rs_bufs(n)[2]
        (a_dev, a), (b_dev, b) = sides(n)
        return [
            rs_copy(n, 7, g.at[:, a], land.at[0], a_dev),
            rs_copy(n, 8, g.at[:, b], land.at[1], b_dev),
        ]

    def rs_one(n):
        p = order[n]
        return rs_copy(
            n, 1, grad_piece(p, core).at[:, xy_d, rs_rows_one(n)], rs_bufs(n)[1], sides(n)[1][0]
        )

    def rs_two(n):
        p = order[n]
        return rs_copy(
            n,
            6,
            grad_piece(p, core).at[zpos, xy_d, rows_two],
            r.lt.at[n % RINGS["lt"]],
            sides(n)[0][0],
        )

    def rs_swap(n):
        p = order[n]
        half = pl.ds(pl.multiple_of(other * 24, 8), 24)
        return rs_copy(n, 13, r.fs.at[p - 1, half], r.fr.at[p - 1], sib)

    def rs_0(n):
        credit_wait(n, 0)
        rs_copy(n, 0, grad_piece(order[n], other), rs_bufs(n)[0], sib).start()

    def rs_1(n):
        p = order[n]
        l0 = rs_bufs(n)[0]
        g = grad_piece(p, core)
        rs_copy(n, 0, grad_piece(p, other), l0, sib).wait_recv()

        def body(i, carry):
            g[i] = (g[i].astype(F32) + l0[i].astype(F32)).astype(g.dtype)
            return carry

        lax.fori_loop(0, 4, body, 0)
        credit_give(n, 0, sib)
        credit_wait(n, 1)
        rs_one(n).start()
        if n < SHORT:
            sum_z_start(n, 2, 5, *diagonal(n))

    def rs_early(n):
        credit_wait(n, 3)
        credit_wait(n, 4)
        for copy in rs_main(n)[0]:
            copy.start()

    def rs_2(n):
        p = order[n]
        g, l1 = grad_piece(p, core), rs_bufs(n)[1]
        (a_dev, a), (b_dev, b) = sides(n)
        rs_one(n).wait_recv()
        for z in range(4):
            add_to(g, (z, a, rs_rows_one(n)), l1[z])
        credit_give(n, 1, b_dev)
        if n < SHORT:
            sum_z_pass(n, 2, 5, *diagonal(n))
        else:
            rs_early(n)
            for copy in rs_main(n)[1]:
                copy.start()

    def rs_3(n):
        p = order[n]
        if p:
            g = grad_piece(p, core)
            total, give = sum_z_end(n, 2, 5, *diagonal(n))
            add_to(g, (zpos, xy_d, rows_two), total)
            give()
            credit_wait(n, 2)
            rs_two(n).start()
            rs_early(n)
            for copy in rs_main(n)[1]:
                copy.start()

    def rs_4(n):
        p = order[n]
        if p:
            g = grad_piece(p, core)
            (a_dev, a), (b_dev, b) = sides(n)
            rs_two(n).wait_recv()
            add_to(g, (zpos, b, rows_two), r.lt[n % RINGS["lt"]])
            credit_give(n, 2, a_dev)
            for copy in rs_main(n)[2]:
                copy.start()

    def rs_5(n):
        p = order[n]
        g, l2 = grad_piece(p, core), rs_bufs(n)[2]
        (a_dev, a), (b_dev, b) = sides(n)
        for copy in rs_all(n):
            copy.wait_recv()
        for z in range(4):
            add_to(g, (z, xy), l2[0, z].astype(F32) + l2[1, z].astype(F32))
        credit_give(n, 3, a_dev)
        credit_give(n, 4, b_dev)
        if n < SHORT:
            sum_z_start(n, 9, 9, *own_line(n))
        else:
            for k in (1, 2, 3):
                z_send(n, 9, *own_line(n), k).start()

    def rs_6(n):
        sum_z_pass(n, 9, 9, *own_line(n))

    def rs_7(n):
        p = order[n]
        if n < SHORT:
            total, give = sum_z_end(n, 9, 9, *own_line(n))
        else:
            land = rs_bufs(n)[3]
            for k in (1, 2, 3):
                z_send(n, 9, *own_line(n), k).wait_recv()
            total = land[0].astype(F32) + land[1].astype(F32) + land[2].astype(F32)
        total = total + grad_piece(p, core)[zpos, xy].astype(F32)
        if p == 0:
            r.osm[...] = total
        elif p >= 9:
            i, j = (p - 9) // 2, (p - 9) % 2
            r.o2[ROWS * i : ROWS * (i + 1), COLS * j : COLS * (j + 1)] = total
        else:
            r.fs[p - 1] = total
            rs_swap(n).start()
        if n < SHORT:
            give()

    def rs_8(n):
        p = order[n]
        if p == 0 or p >= 9:
            return
        mine = pl.ds(pl.multiple_of(core * 24, 8), 24)
        rs_swap(n).wait_recv()
        out, first = (r.oq, 0) if p <= 3 else ((r.op, 0) if p == 4 else (r.o1, p - 5))
        for g in range(3):
            lanes = slice(LANES * g, LANES * (g + 1))
            base = 768 * g + 256 * (p - 1) if p <= 3 else 768 * first + 256 * g
            out[:, pl.ds(pl.multiple_of(base + LANES * core, LANES), LANES)] = r.fs[
                p - 1, mine, lanes
            ]
            out[:, pl.ds(pl.multiple_of(base + LANES * other, LANES), LANES)] = r.fr[
                p - 1, :, lanes
            ]

    def rs_9(n):
        p = order[n]
        rs_copy(n, 0, grad_piece(p, other), rs_bufs(n)[0], sib).wait_send()
        rs_one(n).wait_send()
        for copy in rs_all(n):
            copy.wait_send()
        if n < SHORT:
            sum_z_sent(n, 2, *diagonal(n))
            rs_two(n).wait_send()
            sum_z_sent(n, 9, *own_line(n))
        else:
            for k in (1, 2, 3):
                z_send(n, 9, *own_line(n), k).wait_send()
        if 1 <= p <= 8:
            rs_swap(n).wait_send()

    rs_long = list(zip((rs_0, rs_1, rs_2, rs_3, rs_4, rs_5, rs_6, rs_7, rs_8, rs_9), LONG_AT))
    rs_short = list(zip((rs_0, rs_1, rs_2, rs_5, rs_7, rs_8, rs_9), SHORT_AT))

    def rs_tick(tick):
        for n in range(PIECES + 1):
            for stage, after in rs_long if n < SHORT else rs_short:
                if STARTS[n] + after == tick:
                    stage(n)

    def rows_of(f):
        return pl.ds(pl.multiple_of(f * WIN, WIN), WIN)

    def loop(count, body, ticks=()):
        def step(i, carry):
            body(i)
            for k, tick in enumerate(ticks):
                if tick is not None:
                    pl.when(i == k)(tick)
            return carry

        lax.fori_loop(0, count, step, 0)

    def steps(fn, *numbers):
        return [functools.partial(fn, s) if s is not None else None for s in numbers]

    def natural(ref, lead, rows):
        parts = []
        for g in range(3):
            for h in range(2):
                parts.append(ref[(h, *lead, rows, pl.ds(LANES * g, LANES))])
        return parts

    def put(ref, lead, rows, value):
        for g in range(3):
            for h in range(2):
                at = 256 * g + LANES * h
                ref[(h, *lead, rows, pl.ds(LANES * g, LANES))] = value[:, at : at + LANES]

    def put_a(piece, rows, value):
        for g in range(3):
            for h in range(2):
                at = 256 * g + LANES * h
                r.gp[4 * h + piece, rows, LANES * g : LANES * (g + 1)] = value[:, at : at + LANES]

    def pre_rows(t, h, s):
        return pl.ds(pl.multiple_of((2 * t + h) * 1024 + s.start, 8), s.stop - s.start)

    def pre_tile(t, s):
        return jnp.concatenate([gp_m[pre_rows(t, h, s), :] for h in range(2)], axis=1)

    def mixed_in(f):
        rw = rows_of(f)
        return jnp.where(r.st[rw, 0:1] > 0, r.v24[6:7, :], r.tok[rw, :].astype(F32))

    def masks():
        bits = jnp.transpose(r.mask[...].astype(F32))
        for j in range(8):
            keep = 1.0 - r.pad[j // 2].astype(F32)
            col = bits[:, j : j + 1]
            r.st[LANES * j : LANES * (j + 1), 0:1] = col
            r.st[LANES * j : LANES * (j + 1), 1:2] = col * keep

    def mask_grad(f):
        rw = rows_of(f)
        r.dm[rw, :] = (r.dm[rw, :].astype(F32) * r.st[rw, 1:2]).astype(BF16)

    def spread_small():
        table = r.sv[...].reshape(32, 8, LANES)
        rows = [table[:, i, :].astype(BF16) for i in range(3)]
        at = 0
        for name, row, lane0, width in SMALL_ROWS:
            pick, owner = spread_tables(lane0, width)
            full = jnp.sum(jnp.where(owner, dot_nn(rows[row], pick), 0.0), axis=0, keepdims=True)
            if name == "qkv_bias":
                for t in range(3):
                    for g in range(3):
                        at_piece, at_whole = 768 * t + 256 * g, 768 * g + 256 * t
                        r.bqkv[:, at_piece : at_piece + 256] = full[:, at_whole : at_whole + 256]
            elif name == "fc1_bias":
                r.bfc1[...] = full
            else:
                r.v24[at : at + 1, :] = full
                at += 1
        r.gv[...] = jnp.zeros_like(r.gv)

    def collect_small():
        table = [jnp.zeros((32, LANES), F32) for _ in range(3)]
        at = 0
        for name, row, lane0, width in SMALL_ROWS:
            pick, owner = spread_tables(lane0, width)
            if name == "qkv_bias":
                chunks = [768 * t + 256 * g for g in range(3) for t in range(3)]
                full = jnp.concatenate([r.gbqkv[:, c : c + 256] for c in chunks], axis=1)
            elif name == "fc1_bias":
                full = r.gbfc1[...]
            else:
                full = r.gv[at : at + 1, :]
                at += 1
            parts = jnp.where(owner, full, 0.0)
            for _ in range(3):
                high = parts.astype(BF16)
                table[row] = table[row] + dot_nt(high, pick)
                parts = parts - high.astype(F32)
        flat = r.sg.reshape(256, LANES)
        r.sg[...] = jnp.zeros_like(r.sg)
        for i in range(3):
            flat[pl.ds(i, 32, stride=8), :] = table[i]

    def ln1(f):
        rw = rows_of(f)
        x = mixed_in(f)
        row_mean, row_scale = row_stats(x)
        r.st[rw, 2:3] = row_mean
        r.st[rw, 3:4] = row_scale
        r.normed[rw, :] = ((x - row_mean) * row_scale * r.v24[0:1, :] + r.v24[1:2, :]).astype(BF16)

    def qkv(t):
        w = jnp.concatenate(natural(wa_m, (t,), pl.ds(0, 768)), axis=1)
        cols = tile(t)
        bias = r.bqkv[:, cols]
        for i in range(4):
            s = slice(WIN * i, WIN * (i + 1))
            r.packed[s, cols] = (dot_nn(r.normed[s, :], w) + bias).astype(BF16)

    def part(t, i, pair):
        return pl.ds(pl.multiple_of(768 * t + 256 * i + LANES * pair, LANES), LANES)

    def head_cols(t, pair):
        return pl.ds(pl.multiple_of(256 * t + LANES * pair, LANES), LANES)

    low_lanes = lax.broadcasted_iota(jnp.int32, (WIN, LANES), 1) < HEAD_DIM

    def two_heads(a):
        z = jnp.zeros_like(a)
        return jnp.concatenate([jnp.where(low_lanes, a, z), jnp.where(low_lanes, z, a)], axis=0)

    def attention(t, f, pair):
        rw = rows_of(f)
        q2 = r.packed[rw, part(t, 0, pair)] * jnp.asarray(0.125, BF16)
        k2 = r.packed[rw, part(t, 1, pair)]
        v2 = r.packed[rw, part(t, 2, pair)]
        scores = dot_nt(two_heads(q2), k2)
        row_max = jnp.max(scores, axis=1, keepdims=True)
        e = jnp.exp(scores - row_max)
        total = jnp.sum(e, axis=1, keepdims=True)
        inv = 1.0 / total
        log_total = row_max + jnp.log(total)
        for h in range(2):
            col = jnp.broadcast_to(log_total[WIN * h : WIN * (h + 1)], (WIN, 8))
            r.lse[f * 6 + 2 * t + pair, h : h + 1, :] = jnp.transpose(col)[0:1]
        e = e.astype(BF16)
        out = dot_nn(jnp.concatenate([e[:WIN], e[WIN:]], axis=1), two_heads(v2))
        scale = jnp.where(
            low_lanes,
            jnp.broadcast_to(inv[:WIN], (WIN, LANES)),
            jnp.broadcast_to(inv[WIN:], (WIN, LANES)),
        )
        r.att[rw, head_cols(t, pair)] = (out * scale).astype(BF16)

    def heads_forward(t, between):
        qkv(t)
        for f in range(4):
            for pair in range(2):
                attention(t, f, pair)
            if f == 1:
                for k, tick in enumerate(between):
                    if tick is not None:
                        pl.when(t == k)(tick)

    def project(f):
        rw = rows_of(f)
        w = jnp.concatenate(natural(wa_m, (3,), pl.ds(0, 768)), axis=1)
        middle = mixed_in(f) + (dot_nn(r.att[rw, :], w) + r.v24[2:3, :])
        r.mid[rw, :] = middle
        row_mean, row_scale = row_stats(middle)
        r.st[rw, 4:5] = row_mean
        r.st[rw, 5:6] = row_scale
        r.n2[rw, :] = ((middle - row_mean) * row_scale * r.v24[3:4, :] + r.v24[4:5, :]).astype(BF16)

    def tile(t):
        return pl.ds(pl.multiple_of(t * 768, 768), 768)

    def fc1(t):
        w = jnp.concatenate(natural(w1_m, (t,), pl.ds(0, 768)), axis=1)
        cols = tile(t)
        bias = r.bfc1[:, cols]
        for i in range(4):
            s = slice(WIN * i, WIN * (i + 1))
            act, slope = gelu_and_slope(dot_nn(r.n2[s, :], w) + bias)
            r.hact[s, cols] = act.astype(BF16)
            slope = slope.astype(BF16)
            gp_m[pre_rows(t, 0, s), :] = slope[:, :COLS]
            gp_m[pre_rows(t, 1, s), :] = slope[:, COLS:]

    def turn(src):
        def body(f):
            rw = rows_of(f)
            r.tr[:, rw] = r.normed[rw, :].T if src == 0 else r.n2[rw, :].T

        return body

    def fc2(n):
        cols = pl.ds(pl.multiple_of(n * 256, 256), 256)
        parts = []
        for i in range(2):
            g = 2 * n + i
            lanes = pl.ds(pl.multiple_of(lax.rem(g, 3) * LANES, LANES), LANES)
            parts.append(w2_m[lax.div(g, 3), :, lanes])
        w = jnp.concatenate(parts, axis=1)
        for i in range(4):
            s = slice(WIN * i, WIN * (i + 1))
            r.n2[s, cols] = (
                dot_nn(r.hact[s, :], w) + (r.mid[s, cols] + r.v24[5:6, cols])
            ).astype(BF16)

    def grad_fc2(t):
        cols = tile(t)
        g = dot_tn(r.hact[:, cols], r.dm[...]).astype(BF16)
        g2_m[0, cols, :] = g[:, :COLS]
        g2_m[1, cols, :] = g[:, COLS:]

    def grad_pre(t):
        cols = tile(t)
        w = jnp.concatenate([w2_m[0, cols, :], w2_m[1, cols, :]], axis=1)
        sums = jnp.zeros((1, 768), F32)
        for i in range(4):
            s = slice(WIN * i, WIN * (i + 1))
            d = (dot_nt(r.dm[s, :], w) * pre_tile(t, s).astype(F32)).astype(BF16)
            gp_m[pre_rows(t, 0, s), :] = d[:, :COLS]
            gp_m[pre_rows(t, 1, s), :] = d[:, COLS:]
            sums = sums + jnp.sum(d.astype(F32), axis=0, keepdims=True)
        r.gbfc1[:, cols] = sums

    def grad_fc1(t):
        put(w1_m, (t,), pl.ds(0, 768), dot_nn(r.tr[...], pre_tile(t, slice(0, 1024))).astype(BF16))

    def grad_norm_two(n):
        rw = rows_of(n)
        parts = []
        for t in range(4):
            parts += natural(w1_m, (t,), rw)
        w = jnp.concatenate(parts, axis=1)
        for i in range(4):
            s = slice(WIN * i, WIN * (i + 1))
            pre = jnp.concatenate([pre_tile(t, s) for t in range(4)], axis=1)
            r.dn[s, rw] = dot_nt(pre, w)

    def grad_middle(f):
        rw = rows_of(f)
        dy = r.dm[rw, :].astype(F32)
        dx, gain, shift = norm_backward(
            r.mid[rw, :], r.st[rw, 4:5], r.st[rw, 5:6], r.dn[rw, :], r.v24[3:4, :]
        )
        d = dy + dx
        low = d.astype(BF16)
        r.mid[rw, :] = d
        r.dm[rw, :] = low
        r.gv[3:4, :] += gain
        r.gv[4:5, :] += shift
        r.gv[5:6, :] += jnp.sum(dy, axis=0, keepdims=True)
        r.gv[2:3, :] += jnp.sum(low.astype(F32), axis=0, keepdims=True)

    def grad_proj(j):
        rw = rows_of(j)
        put_a(3, rw, dot_tn(r.att[:, rw], r.dm[...]).astype(BF16))

    def grad_att(f):
        rw = rows_of(f)
        w = jnp.concatenate(natural(wa_m, (3,), pl.ds(0, 768)), axis=1)
        r.n2[rw, :] = dot_nt(r.dm[rw, :], w).astype(BF16)

    def attention_backward(t, f, pair):
        rw = rows_of(f)
        q2 = r.packed[rw, part(t, 0, pair)] * jnp.asarray(0.125, BF16)
        k2 = r.packed[rw, part(t, 1, pair)]
        v2 = r.packed[rw, part(t, 2, pair)]
        qs, ds, ks = two_heads(q2), two_heads(r.n2[rw, head_cols(t, pair)]), two_heads(k2)
        at = f * 6 + 2 * t + pair
        log_total = jnp.concatenate([r.lse[at, 0:1, :], r.lse[at, 1:2, :]], axis=1)
        probs = jnp.exp(dot_nt(k2, qs) - log_total)
        prod = probs * dot_nt(v2, ds)
        row_dot = jnp.sum(prod, axis=0, keepdims=True)
        d_scores = (prod - probs * row_dot).astype(BF16)
        r.packed[rw, part(t, 2, pair)] = dot_nn(probs.astype(BF16), ds).astype(BF16)
        r.packed[rw, part(t, 1, pair)] = dot_nn(d_scores, qs).astype(BF16)
        stacked = jnp.concatenate([d_scores[:, :WIN], d_scores[:, WIN:]], axis=0)
        r.packed[rw, part(t, 0, pair)] = (dot_tn(stacked, ks) * 0.125).astype(BF16)

    def heads_backward(t):
        def body(f):
            for pair in range(2):
                attention_backward(t, f, pair)

        return body

    def grad_qkv(t):
        cols = tile(t)
        d = r.packed[:, cols]
        put_a(t, slice(None), dot_nn(r.tr[...], d).astype(BF16))
        r.gbqkv[:, cols] = jnp.sum(d.astype(F32), axis=0, keepdims=True)

    def grad_norm_one(n):
        rw = rows_of(n)
        parts = []
        for t in range(3):
            parts += natural(wa_m, (t,), rw)
        w = jnp.concatenate(parts, axis=1)
        for i in range(4):
            s = slice(WIN * i, WIN * (i + 1))
            r.dn[s, rw] = dot_nt(r.packed[s, :], w)

    def grad_mixed(f):
        rw = rows_of(f)
        dx, gain, shift = norm_backward(
            mixed_in(f), r.st[rw, 2:3], r.st[rw, 3:4], r.dn[rw, :], r.v24[0:1, :]
        )
        d = r.mid[rw, :] + dx
        chosen = r.st[rw, 0:1] > 0
        r.dn[rw, :] = jnp.where(chosen, 0.0, d)
        r.gv[0:1, :] += gain
        r.gv[1:2, :] += shift
        r.gv[6:7, :] += jnp.sum(jnp.where(chosen, d, 0.0), axis=0, keepdims=True)

    loads = [
        pltpu.make_async_copy(r.og_in, r.dm, r.ld.at[0]),
        pltpu.make_async_copy(r.tok_in, r.tok, r.ld.at[1]),
    ]
    for q in range(2):
        loads.append(
            pltpu.make_async_copy(
                r.s2w.at[:, pl.ds(COLS * q, COLS)], w2_shard.at[q, zpos, xy, core], r.ld.at[2 + q]
            )
        )
    loads.append(pltpu.make_async_copy(r.small, r.sv.at[zpos, xy, core], r.ld.at[4]))
    for copy in loads:
        copy.start()

    for land in (r.lz, r.l3):
        for slot in range(land.shape[0]):
            land[slot, 0] = jnp.zeros_like(land[slot, 0])
            land[slot, 2] = jnp.zeros_like(land[slot, 2])

    barrier = pltpu.get_barrier_semaphore()
    peers = [sib, x_dev, y_dev, z_dev(1), z_dev(2), z_dev(3)]
    for dev in peers:
        pl.semaphore_signal(barrier, inc=1, device_id=(dev,), device_id_type=MESH_ID)

    def shard_half(t, half):
        ref, first = (r.sq, 0) if t < 3 else ((r.sp, 0) if t == 3 else (r.s1w, t - 4))
        parts = []
        for g in range(3):
            base = 768 * g + 256 * t if t < 3 else 768 * first + 256 * g
            a = ref[:, base : base + LANES].astype(F32)
            b = ref[:, base + LANES : base + 2 * LANES].astype(F32)
            parts.append(jnp.where(half == 0, a, b))
        return jnp.concatenate(parts, axis=1)

    for t in range(8):
        away = jnp.concatenate([shard_half(t, other), jnp.zeros((8, COLS), F32)], axis=0)
        r.l0[0, t // 4, t % 4, 0:32] = away.astype(BF16)
    pl.semaphore_wait(barrier, len(peers))
    away, came = [r.l0.at[i, pl.ds(0, 2), :, pl.ds(0, 32)] for i in range(2)]
    swap = remote(away, came, r.prep.at[0], r.prep.at[1], sib)
    swap.start()
    loads[4].wait()
    ag_a(0)
    swap.wait()
    for t in range(8):
        here = shard_half(t, core)
        there = r.l0[1, t // 4, t % 4, 0:32].astype(F32)[:24]
        block = jnp.concatenate(
            [jnp.where(core == 0, here, there), jnp.where(core == 0, there, here)], axis=0
        ).astype(BF16)
        if t < 4:
            wa_v[core, t, zpos, xy] = block
        else:
            w1_v[core, t - 4, zpos, xy] = block
        if t + 1 < ahead:
            ag_a(t + 1)
    ag_step(-1)
    loads[2].wait()
    loads[3].wait()
    def ag(*numbers):
        def go():
            for s in numbers:
                ag_step(s)

        return go

    def rs(*numbers):
        def go():
            for s in numbers:
                rs_tick(s)

        return go

    def arrive(p, *numbers):
        def go():
            ag(*numbers)()
            ag_e(p)

        return go

    ag_step(0)
    masks()
    ag_step(1)
    loads[0].wait()
    loop(4, mask_grad)
    ag_step(2)
    ag_e(0)
    ag_step(3)
    loads[1].wait()
    spread_small()
    loop(4, ln1)
    ag_e(1)
    loop(
        3,
        functools.partial(heads_forward, between=[ag(4), ag(6), ag(8)]),
        [arrive(2, 5), arrive(3, 7), arrive(4, 9)],
    )
    loop(4, project, [None, ag(10), None, None])
    keep_middle = pltpu.make_async_copy(r.mid, r.ig, r.ld.at[5])
    keep_middle.start()
    ag_e(5)
    loop(4, fc1, [arrive(6, 11), arrive(7), arrive(8, 12), ag(13)])
    loop(4, turn(1))
    for p in range(9):
        ag_f(p)
    loop(4, grad_fc2, [None, ag(14), None, None])
    rs_tick(0)
    for p in range(9, PIECES + 1):
        ag_e(p)
        ag_f(p)
    loop(4, grad_pre, [rs(1), rs(2), rs(3), rs(4)])
    loop(3, grad_norm_two, [rs(5), rs(6), rs(7)])
    loop(4, grad_fc1, [rs(8), rs(9), rs(10), rs(11)])
    keep_middle.wait()
    loop(4, grad_middle, [None, rs(12), None, rs(13)])
    loop(3, grad_proj)
    rs_tick(14)
    loop(4, grad_att)
    rs_tick(15)
    loop(4, turn(0))
    loop(4, heads_backward(0), [rs(16), rs(17), rs(18), rs(19)])
    grad_qkv(0)
    rs_tick(20)
    loop(4, heads_backward(1), [rs(21), rs(22), rs(23), rs(24)])
    grad_qkv(1)
    rs_tick(25)
    loop(4, heads_backward(2), [rs(26), rs(27), rs(28), rs(29)])
    grad_qkv(2)
    rs_tick(30)
    loop(3, grad_norm_one, [rs(31), rs(32), rs(33)])
    loop(4, grad_mixed, [None, rs(34), None, rs(35)])
    load_middle = pltpu.make_async_copy(r.ig, r.mid, r.ld.at[6])
    load_middle.start()
    collect_small()
    rs_tick(36)
    load_middle.wait()
    write_grad = pltpu.make_async_copy(r.dn, r.ig, r.ld.at[7])
    write_grad.start()
    rs_tick(37)
    loop(3, fc2, [rs(38, 39), rs(40, 41), rs(42, 43)])
    write_out = pltpu.make_async_copy(r.n2, r.bo, r.ld.at[0])
    write_out.start()
    last = max(at + (LONG_AT if n < SHORT else SHORT_AT)[-1] for n, at in enumerate(STARTS))
    for tick in range(44, last + 1):
        rs_tick(tick)
    write_grad.wait()
    write_out.wait()


HAND_PARTS = 4


def hand_over(*refs):
    arrays, small, outs = refs[:6], refs[6], refs[7:13]
    vectors, held, (in_sems, out_sems) = refs[13:-8], refs[-8:-2], refs[-2:]
    loads, stores = [], []
    for src, buf, dst in zip(arrays, held, outs):
        parts = HAND_PARTS if src.shape[0] == 1024 else 1
        rows = src.shape[0] // parts
        for i in range(parts):
            at, n = pl.ds(rows * i, rows), len(loads)
            loads.append(pltpu.make_async_copy(src.at[at], buf.at[at], in_sems.at[n]))
            stores.append(pltpu.make_async_copy(buf.at[at], dst.at[at], out_sems.at[n]))
    for copy in loads:
        copy.start()
    for ref, (_, row, lane0, width) in zip(vectors, SMALL_ROWS):
        ref[...] = small[row : row + 1, lane0 : lane0 + width]
    for load, store in zip(loads, stores):
        load.wait()
        store.start()
    for copy in stores:
        copy.wait()


def fused_device(
    tokens,
    mask_bits,
    pad_flags,
    ln1_gain,
    ln1_bias,
    qkv_weight,
    qkv_bias,
    proj_weight,
    proj_bias,
    ln2_gain,
    ln2_bias,
    fc1_weight,
    fc1_bias,
    fc2_weight,
    fc2_bias,
    mask_embed,
    out_grad,
):
    held = dict(
        ln1_gain=ln1_gain,
        ln1_bias=ln1_bias,
        proj_bias=proj_bias,
        ln2_gain=ln2_gain,
        ln2_bias=ln2_bias,
        fc2_bias=fc2_bias,
        mask_embed=mask_embed,
        qkv_bias=qkv_bias,
        fc1_bias=fc1_bias,
    )
    small = jnp.zeros((8 * LANES,), F32)
    for name, row, lane0, width in SMALL_ROWS:
        first = row * LANES + lane0
        small = small + jnp.pad(held[name].astype(F32), (first, 8 * LANES - first - width))
    small = small.reshape(8, LANES)
    any_spec = pl.BlockSpec(memory_space=pl.ANY)
    vmem = pl.BlockSpec(memory_space=pltpu.VMEM)
    smem = pl.BlockSpec(memory_space=pltpu.SMEM)
    shape = jax.ShapeDtypeStruct
    outs = pl.pallas_call(
        fused_kernel,
        out_shape=(
            shape((1024, 768), BF16),
            shape((1024, 768), F32),
            shape((24, 2304), F32),
            shape((24, 768), F32),
            shape((24, 3072), F32),
            shape((96, 768), F32),
            shape((8, LANES), F32),
        ),
        in_specs=[any_spec, any_spec, vmem, smem, any_spec, vmem, vmem, vmem, any_spec],
        out_specs=(any_spec, any_spec, vmem, vmem, vmem, vmem, vmem),
        scratch_shapes=[pltpu.VMEM(*spec) for spec in SCRATCH.values()] + list(SEMS.values()),
        compiler_params=pltpu.CompilerParams(
            collective_id=0, has_side_effects=True, vmem_limit_bytes=64 * 2**20
        ),
    )(
        tokens,
        out_grad,
        mask_bits.reshape(8, LANES),
        pad_flags,
        small,
        qkv_weight,
        proj_weight,
        fc1_weight,
        fc2_weight,
    )
    held = pl.pallas_call(
        hand_over,
        out_shape=tuple(shape(o.shape, o.dtype) for o in outs[:6])
        + tuple(shape((1, width), F32) for _, _, _, width in SMALL_ROWS),
        in_specs=[any_spec] * 6 + [vmem],
        out_specs=(any_spec,) * 6 + (vmem,) * len(SMALL_ROWS),
        scratch_shapes=[pltpu.VMEM(o.shape, o.dtype) for o in outs[:6]]
        + [pltpu.SemaphoreType.DMA((6 * HAND_PARTS,)), pltpu.SemaphoreType.DMA((6 * HAND_PARTS,))],
        compiler_params=pltpu.CompilerParams(vmem_limit_bytes=63 * 2**20),
    )(*outs)
    block_out, input_grad, gq, gpj, g1, g2 = held[:6]
    v = {entry[0]: vec.reshape(entry[3]) for entry, vec in zip(SMALL_ROWS, held[6:])}
    return (
        block_out,
        input_grad,
        v["ln1_gain"],
        v["ln1_bias"],
        gq,
        v["qkv_bias"],
        gpj,
        v["proj_bias"],
        v["ln2_gain"],
        v["ln2_bias"],
        g1,
        v["fc1_bias"],
        g2,
        v["fc2_bias"],
        v["mask_embed"],
    )


def solution(mesh):
    placed = (
        P("fsdp", None),
        P("fsdp"),
        P("fsdp"),
        P("fsdp"),
        P("fsdp"),
        P("fsdp", None),
        P("fsdp"),
        P("fsdp", None),
        P("fsdp"),
        P("fsdp"),
        P("fsdp"),
        P("fsdp", None),
        P("fsdp"),
        P("fsdp", None),
        P("fsdp"),
        P("fsdp"),
        P("fsdp", None),
    )
    return jax.shard_map(
        fused_device if mesh.shape["fsdp"] == 32 else per_device,
        mesh=mesh,
        in_specs=placed,
        out_specs=(
            P("fsdp", None),
            P("fsdp", None),
            P("fsdp"),
            P("fsdp"),
            P("fsdp", None),
            P("fsdp"),
            P("fsdp", None),
            P("fsdp"),
            P("fsdp"),
            P("fsdp"),
            P("fsdp", None),
            P("fsdp"),
            P("fsdp", None),
            P("fsdp"),
            P("fsdp"),
        ),
        check_vma=False,
    )
```

```python
import functools

import jax
import jax.numpy as jnp
from jax import lax
from jax.experimental import pallas as pl
from jax.experimental.pallas import tpu as pltpu
from jax.sharding import PartitionSpec as P

HEADS = 12
HEAD_DIM = 64
WIN = 256


epsilon = 1e-06


def norm_rows(values, gain_vec, shift_vec):
    row_mean = jnp.mean(values, axis=-1, keepdims=True)
    centered = values - row_mean
    variance = jnp.mean(centered * centered, axis=-1, keepdims=True)
    return centered * lax.rsqrt(variance + epsilon) * gain_vec + shift_vec


def gelu_exact(values):
    return jax.nn.gelu(values, approximate=False)


def forward_pass(full, tok_rows, masked):
    (
        gain_one,
        shift_one,
        qkv_w,
        qkv_b,
        proj_w,
        proj_b,
        gain_two,
        shift_two,
        up_w,
        up_b,
        down_w,
        down_b,
        mask_vec,
    ) = full
    row_count = tok_rows.shape[0]
    width = tok_rows.shape[1]
    frames = row_count // WIN
    mixed_in = jnp.where(
        masked[:, None] > 0, mask_vec.astype(jnp.float32)[None, :], tok_rows.astype(jnp.float32)
    )
    normed = norm_rows(
        mixed_in, gain_one.astype(jnp.float32), shift_one.astype(jnp.float32)
    ).astype(jnp.bfloat16)
    packed = (
        jnp.dot(normed, qkv_w, preferred_element_type=jnp.float32) + qkv_b.astype(jnp.float32)
    ).astype(jnp.bfloat16)
    heads_view = packed.reshape(frames, WIN, 3, HEADS, HEAD_DIM)
    scores = jnp.einsum(
        "fqhd,fkhd->fhqk",
        heads_view[:, :, 0],
        heads_view[:, :, 1],
        preferred_element_type=jnp.float32,
    ) * HEAD_DIM ** (-0.5)
    row_max = jnp.max(scores, axis=-1, keepdims=True)
    exp_terms = jnp.exp(scores - row_max)
    row_total = jnp.sum(exp_terms, axis=-1, keepdims=True)
    probs_low = (exp_terms / row_total).astype(jnp.bfloat16)
    log_total = row_max + jnp.log(row_total)
    attended = jnp.einsum(
        "fhqk,fkhd->fqhd", probs_low, heads_view[:, :, 2], preferred_element_type=jnp.float32
    )
    attended = attended.reshape(row_count, width).astype(jnp.bfloat16)
    middle = (
        mixed_in
        + jnp.dot(attended, proj_w, preferred_element_type=jnp.float32)
        + proj_b.astype(jnp.float32)
    )
    normed_two = norm_rows(
        middle, gain_two.astype(jnp.float32), shift_two.astype(jnp.float32)
    ).astype(jnp.bfloat16)
    hidden_pre = jnp.dot(normed_two, up_w, preferred_element_type=jnp.float32) + up_b.astype(
        jnp.float32
    )
    hidden_act = gelu_exact(hidden_pre).astype(jnp.bfloat16)
    result = (
        middle
        + jnp.dot(hidden_act, down_w, preferred_element_type=jnp.float32)
        + down_b.astype(jnp.float32)
    )
    saved = (
        mixed_in,
        normed,
        packed,
        log_total,
        attended,
        middle,
        normed_two,
        hidden_pre,
        hidden_act,
    )
    return (result, saved)


def mlp_backward(full, saved, cotangent):
    (
        gain_one,
        shift_one,
        qkv_w,
        qkv_b,
        proj_w,
        proj_b,
        gain_two,
        shift_two,
        up_w,
        up_b,
        down_w,
        down_b,
        mask_vec,
    ) = full
    mixed_in, normed, packed, log_total, attended, middle, normed_two, hidden_pre, hidden_act = (
        saved
    )
    down_in = cotangent.astype(jnp.bfloat16)
    grad_down = jnp.einsum("tf,td->fd", hidden_act, down_in, preferred_element_type=jnp.float32)
    grad_down_b = jnp.sum(down_in.astype(jnp.float32), axis=0)
    grad_act = jnp.einsum("td,fd->tf", down_in, down_w, preferred_element_type=jnp.float32)
    gelu_value, gelu_pull = jax.vjp(gelu_exact, hidden_pre)
    grad_pre = gelu_pull(grad_act)[0].astype(jnp.bfloat16)
    grad_up = jnp.einsum("td,tf->df", normed_two, grad_pre, preferred_element_type=jnp.float32)
    grad_up_b = jnp.sum(grad_pre.astype(jnp.float32), axis=0)
    grad_norm_two = jnp.einsum("tf,df->td", grad_pre, up_w, preferred_element_type=jnp.float32)
    norm_value, norm_pull = jax.vjp(
        norm_rows, middle, gain_two.astype(jnp.float32), shift_two.astype(jnp.float32)
    )
    grad_middle, grad_gain_two, grad_shift_two = norm_pull(grad_norm_two)
    grad_middle = grad_middle + cotangent
    return (
        grad_middle,
        (grad_gain_two, grad_shift_two, grad_up, grad_up_b, grad_down, grad_down_b),
    )


def attn_backward(full, saved, grad_middle, masked):
    (
        gain_one,
        shift_one,
        qkv_w,
        qkv_b,
        proj_w,
        proj_b,
        gain_two,
        shift_two,
        up_w,
        up_b,
        down_w,
        down_b,
        mask_vec,
    ) = full
    mixed_in, normed, packed, log_total, attended, middle, normed_two, hidden_pre, hidden_act = (
        saved
    )
    row_count = grad_middle.shape[0]
    width = grad_middle.shape[1]
    frames = row_count // WIN
    proj_in = grad_middle.astype(jnp.bfloat16)
    grad_proj = jnp.einsum("td,te->de", attended, proj_in, preferred_element_type=jnp.float32)
    grad_proj_b = jnp.sum(proj_in.astype(jnp.float32), axis=0)
    grad_att = jnp.einsum("te,de->td", proj_in, proj_w, preferred_element_type=jnp.float32).astype(
        jnp.bfloat16
    )
    grad_att = grad_att.reshape(frames, WIN, HEADS, HEAD_DIM)
    heads_view = packed.reshape(frames, WIN, 3, HEADS, HEAD_DIM)
    query_part = heads_view[:, :, 0]
    key_part = heads_view[:, :, 1]
    value_part = heads_view[:, :, 2]
    score_scale = HEAD_DIM ** (-0.5)
    scores = (
        jnp.einsum("fqhd,fkhd->fhqk", query_part, key_part, preferred_element_type=jnp.float32)
        * score_scale
    )
    probs_full = jnp.exp(scores - log_total)
    probs_low = probs_full.astype(jnp.bfloat16)
    grad_value = jnp.einsum(
        "fhqk,fqhd->fkhd", probs_low, grad_att, preferred_element_type=jnp.float32
    )
    grad_probs = jnp.einsum(
        "fqhd,fkhd->fhqk", grad_att, value_part, preferred_element_type=jnp.float32
    )
    row_dot = jnp.sum(grad_probs * probs_full, axis=-1, keepdims=True)
    grad_scores = (probs_full * (grad_probs - row_dot)).astype(jnp.bfloat16)
    grad_query = (
        jnp.einsum("fhqk,fkhd->fqhd", grad_scores, key_part, preferred_element_type=jnp.float32)
        * score_scale
    )
    grad_key = (
        jnp.einsum("fhqk,fqhd->fkhd", grad_scores, query_part, preferred_element_type=jnp.float32)
        * score_scale
    )
    grad_packed = (
        jnp.stack([grad_query, grad_key, grad_value], axis=2)
        .reshape(row_count, 3 * width)
        .astype(jnp.bfloat16)
    )
    grad_qkv = jnp.einsum("td,te->de", normed, grad_packed, preferred_element_type=jnp.float32)
    grad_qkv_b = jnp.sum(grad_packed.astype(jnp.float32), axis=0)
    grad_normed = jnp.einsum("te,de->td", grad_packed, qkv_w, preferred_element_type=jnp.float32)
    first_value, first_pull = jax.vjp(
        norm_rows, mixed_in, gain_one.astype(jnp.float32), shift_one.astype(jnp.float32)
    )
    grad_mixed, grad_gain_one, grad_shift_one = first_pull(grad_normed)
    grad_mixed = grad_mixed + grad_middle
    chosen = masked[:, None] > 0
    tok_grad = jnp.where(chosen, 0.0, grad_mixed)
    grad_mask = jnp.sum(jnp.where(chosen, grad_mixed, 0.0), axis=0)
    return (
        tok_grad,
        (grad_gain_one, grad_shift_one, grad_qkv, grad_qkv_b, grad_proj, grad_proj_b, grad_mask),
    )


def per_device(
    tokens,
    mask_bits,
    pad_flags,
    ln1_gain,
    ln1_bias,
    qkv_weight,
    qkv_bias,
    proj_weight,
    proj_bias,
    ln2_gain,
    ln2_bias,
    fc1_weight,
    fc1_bias,
    fc2_weight,
    fc2_bias,
    mask_embed,
    out_grad,
):
    full = (
        lax.all_gather(ln1_gain, "fsdp", axis=0, tiled=True),
        lax.all_gather(ln1_bias, "fsdp", axis=0, tiled=True),
        lax.all_gather(qkv_weight, "fsdp", axis=0, tiled=True),
        lax.all_gather(qkv_bias, "fsdp", axis=0, tiled=True),
        lax.all_gather(proj_weight, "fsdp", axis=0, tiled=True),
        lax.all_gather(proj_bias, "fsdp", axis=0, tiled=True),
        lax.all_gather(ln2_gain, "fsdp", axis=0, tiled=True),
        lax.all_gather(ln2_bias, "fsdp", axis=0, tiled=True),
        lax.all_gather(fc1_weight, "fsdp", axis=0, tiled=True),
        lax.all_gather(fc1_bias, "fsdp", axis=0, tiled=True),
        lax.all_gather(fc2_weight, "fsdp", axis=0, tiled=True),
        lax.all_gather(fc2_bias, "fsdp", axis=0, tiled=True),
        lax.all_gather(mask_embed, "fsdp", axis=0, tiled=True),
    )
    result, saved = forward_pass(full, tokens, mask_bits)
    full_back = (
        lax.all_gather(ln1_gain, "fsdp", axis=0, tiled=True),
        lax.all_gather(ln1_bias, "fsdp", axis=0, tiled=True),
        lax.all_gather(qkv_weight, "fsdp", axis=0, tiled=True),
        lax.all_gather(qkv_bias, "fsdp", axis=0, tiled=True),
        lax.all_gather(proj_weight, "fsdp", axis=0, tiled=True),
        lax.all_gather(proj_bias, "fsdp", axis=0, tiled=True),
        lax.all_gather(ln2_gain, "fsdp", axis=0, tiled=True),
        lax.all_gather(ln2_bias, "fsdp", axis=0, tiled=True),
        lax.all_gather(fc1_weight, "fsdp", axis=0, tiled=True),
        lax.all_gather(fc1_bias, "fsdp", axis=0, tiled=True),
        lax.all_gather(fc2_weight, "fsdp", axis=0, tiled=True),
        lax.all_gather(fc2_bias, "fsdp", axis=0, tiled=True),
        lax.all_gather(mask_embed, "fsdp", axis=0, tiled=True),
    )
    kept_acts = forward_pass(full_back, tokens, mask_bits)[1]
    row_count = tokens.shape[0]
    frames = row_count // WIN
    frame_keep = (1 - pad_flags).astype(jnp.float32)
    tok_weight = (mask_bits.astype(jnp.float32).reshape(frames, WIN) * frame_keep[:, None]).reshape(
        row_count
    )
    cotangent = out_grad.astype(jnp.float32) * tok_weight[:, None]
    grad_middle, mlp_grads = mlp_backward(full_back, kept_acts, cotangent)
    tok_grad, attn_grads = attn_backward(full_back, kept_acts, grad_middle, mask_bits)
    shares = (
        lax.psum_scatter(attn_grads[0], "fsdp", scatter_dimension=0, tiled=True),
        lax.psum_scatter(attn_grads[1], "fsdp", scatter_dimension=0, tiled=True),
        lax.psum_scatter(attn_grads[2], "fsdp", scatter_dimension=0, tiled=True),
        lax.psum_scatter(attn_grads[3], "fsdp", scatter_dimension=0, tiled=True),
        lax.psum_scatter(attn_grads[4], "fsdp", scatter_dimension=0, tiled=True),
        lax.psum_scatter(attn_grads[5], "fsdp", scatter_dimension=0, tiled=True),
        lax.psum_scatter(mlp_grads[0], "fsdp", scatter_dimension=0, tiled=True),
        lax.psum_scatter(mlp_grads[1], "fsdp", scatter_dimension=0, tiled=True),
        lax.psum_scatter(mlp_grads[2], "fsdp", scatter_dimension=0, tiled=True),
        lax.psum_scatter(mlp_grads[3], "fsdp", scatter_dimension=0, tiled=True),
        lax.psum_scatter(mlp_grads[4], "fsdp", scatter_dimension=0, tiled=True),
        lax.psum_scatter(mlp_grads[5], "fsdp", scatter_dimension=0, tiled=True),
        lax.psum_scatter(attn_grads[6], "fsdp", scatter_dimension=0, tiled=True),
    )
    return (
        result.astype(jnp.bfloat16),
        tok_grad,
        shares[0],
        shares[1],
        shares[2],
        shares[3],
        shares[4],
        shares[5],
        shares[6],
        shares[7],
        shares[8],
        shares[9],
        shares[10],
        shares[11],
        shares[12],
    )


F32 = jnp.float32
BF16 = jnp.bfloat16
LANES = 128
ROWS = 48
COLS = 384
PIECES = 12
CUT = 16
RINGS = dict(l0=2, l1=4, lz=4, lt=4, l2=4, l3=4)
CREDIT_RINGS = ["l0", "l1", "lt", "l2", "l2"] + ["lz"] * 4 + ["l3"] * 4
SHORT = 11
DIRECT = 1
LONG_AT = (0, 2, 5, 8, 11, 14, 17, 20, 22, 23)
SHORT_AT = (0, 2, 5, 8, 11, 13, 14)
SMALL_AT = (0, 1, 3, 5, 7, 8, 9)
STARTS = (0, 1, 3, 5, 8, 10, 13, 16, 19, 22, 25, 30, 36)
MESH_ID = pl.DeviceIdType.MESH


def dot_nn(a, b):
    return lax.dot_general(a, b, (((1,), (0,)), ((), ())), preferred_element_type=F32)


def dot_nt(a, b):
    return lax.dot_general(a, b, (((1,), (1,)), ((), ())), preferred_element_type=F32)


def dot_tn(a, b):
    return lax.dot_general(a, b, (((0,), (0,)), ((), ())), preferred_element_type=F32)


def row_stats(values):
    row_mean = jnp.mean(values, axis=-1, keepdims=True)
    centered = values - row_mean
    return row_mean, lax.rsqrt(jnp.mean(centered * centered, axis=-1, keepdims=True) + epsilon)


def gelu_and_slope(x):
    phi = 0.5 + 0.5 * lax.erf(x * 0.7071067811865476)
    return x * phi, phi + x * jnp.exp(x * x * -0.5) * 0.3989422804014327


def norm_backward(x, row_mean, row_scale, grad, gain):
    x_hat = (x - row_mean) * row_scale
    prod = grad * x_hat
    grad_gain = jnp.sum(prod, axis=0, keepdims=True)
    grad_shift = jnp.sum(grad, axis=0, keepdims=True)
    dx = grad * gain
    mean_one = jnp.mean(dx, axis=-1, keepdims=True)
    mean_two = jnp.mean(dx * x_hat, axis=-1, keepdims=True)
    return row_scale * (dx - mean_one - x_hat * mean_two), grad_gain, grad_shift


SMALL_ROWS = (
    ("ln1_gain", 0, 0, 24),
    ("ln1_bias", 0, 24, 24),
    ("proj_bias", 0, 48, 24),
    ("ln2_gain", 0, 72, 24),
    ("ln2_bias", 0, 96, 24),
    ("fc2_bias", 1, 0, 24),
    ("mask_embed", 1, 24, 24),
    ("qkv_bias", 1, 48, 72),
    ("fc1_bias", 2, 0, 96),
)


def spread_tables(lane0, width):
    count = 32 * width
    k = lax.broadcasted_iota(jnp.int32, (1, count), 1)
    pick = lax.broadcasted_iota(jnp.int32, (LANES, count), 0) == lax.rem(k, width) + lane0
    owner = lax.broadcasted_iota(jnp.int32, (32, count), 0) == lax.div(k, width)
    return jnp.where(pick, 1.0, 0.0).astype(BF16), owner


SCRATCH = dict(
    tok=((1024, 768), BF16),
    dm=((1024, 768), BF16),
    st=((1024, 8), F32),
    v24=((8, 768), F32),
    bqkv=((1, 2304), F32),
    bfc1=((1, 3072), F32),
    gv=((8, 768), F32),
    gbqkv=((1, 2304), F32),
    gbfc1=((1, 3072), F32),
    normed=((1024, 768), BF16),
    n2=((1024, 768), BF16),
    tr=((768, 1024), BF16),
    packed=((1024, 2304), BF16),
    att=((1024, 768), BF16),
    mid=((1024, 768), F32),
    hact=((1024, 3072), BF16),
    gp=((11, 768, COLS), BF16),
    dn=((1024, 768), F32),
    lse=((48, 256), F32),
    wa=((8, 768, COLS), BF16),
    w1=((8, 768, COLS), BF16),
    w2=((8, 768, COLS), BF16),
    g2=((8, 768, COLS), BF16),
    sv=((4, 4, 2, 8, LANES), F32),
    sg=((4, 4, 2, 8, LANES), F32),
    fs=((8, ROWS, COLS), F32),
    fr=((8, ROWS // 2, COLS), F32),
    l0=((RINGS["l0"], 4, 4, ROWS, COLS), BF16),
    l1=((RINGS["l1"], 4, CUT, COLS), BF16),
    lz=((RINGS["lz"], 4, ROWS - CUT, COLS), BF16),
    lt=((RINGS["lt"], ROWS - CUT, COLS), BF16),
    l2=((RINGS["l2"], 2, 4, ROWS, COLS), BF16),
    l3=((RINGS["l3"], 4, ROWS, COLS), BF16),
    l1s=((PIECES - SHORT, 4, ROWS, COLS), BF16),
    l3s=((PIECES - SHORT, 3, ROWS, COLS), BF16),
    s0=((4, 4, 8, LANES), F32),
    s1=((4, 8, LANES), F32),
    s2=((2, 4, 8, LANES), F32),
    s3=((4, 8, LANES), F32),
)
SEMS = dict(
    ld=pltpu.SemaphoreType.DMA((8,)),
    prep=pltpu.SemaphoreType.DMA((2,)),
    sent=pltpu.SemaphoreType.DMA((PIECES + 1, 14)),
    came=pltpu.SemaphoreType.DMA((PIECES + 1, 14)),
    credit=pltpu.SemaphoreType.REGULAR((26,)),
)


class Refs:
    pass


def fused_kernel(*refs):
    r = Refs()
    names = ["tok_in", "og_in", "mask", "pad", "small", "sq", "sp", "s1w", "s2w"]
    names += ["bo", "ig", "oq", "op", "o1", "o2", "osm"]
    names += list(SCRATCH) + list(SEMS)
    for name, ref in zip(names, refs):
        setattr(r, name, ref)

    me = lax.axis_index("fsdp")
    core = lax.rem(me, 2)
    other = 1 - core
    chip = lax.div(me, 2)
    xpos = lax.rem(chip, 2)
    ypos = lax.rem(lax.div(chip, 2), 2)
    zpos = lax.div(chip, 4)
    xy = lax.rem(chip, 4)
    xy_x = xy + 1 - 2 * xpos
    xy_y = xy + 2 - 4 * ypos
    xy_d = xy_x + 2 - 4 * ypos
    sib = me + 1 - 2 * core
    x_dev = me + 2 - 4 * xpos
    y_dev = me + 4 - 8 * ypos

    def z_of(k):
        return lax.rem(zpos + k, 4)

    def z_dev(k):
        return me + 8 * (z_of(k) - zpos)

    def remote(src, dst, ssem, rsem, dev):
        return pltpu.make_async_remote_copy(
            src_ref=src,
            dst_ref=dst,
            send_sem=ssem,
            recv_sem=rsem,
            device_id=(dev,),
            device_id_type=MESH_ID,
        )

    wa_v = r.wa.reshape(2, 4, 4, 4, ROWS, COLS)
    w1_v = r.w1.reshape(2, 4, 4, 4, ROWS, COLS)
    w2_v = r.w2.reshape(2, 4, 4, 2, 2, ROWS, COLS)
    w2_shard = r.w2.reshape(2, 4, 4, 2, 2 * ROWS, COLS)
    w2_m = r.w2.reshape(2, 3072, COLS)
    wa_m = r.wa.reshape(2, 4, 768, COLS)
    w1_m = r.w1.reshape(2, 4, 768, COLS)
    g2_v = r.g2.reshape(2, 4, 4, 2, 2, ROWS, COLS)
    g2_m = r.g2.reshape(2, 3072, COLS)
    ga_v = r.gp.reshape(11, 4, 4, ROWS, COLS)
    gp_m = r.gp.reshape(11 * 768, COLS)

    def weight_piece(p, half):
        if p == 0:
            return r.sv.at[:, :, half]
        if p <= 4:
            return wa_v.at[half, p - 1]
        if p <= 8:
            return w1_v.at[half, p - 5]
        return w2_v.at[(p - 9) % 2, :, :, half, (p - 9) // 2]

    def grad_piece(p, half):
        if p == 0:
            return r.sg.at[:, :, half]
        if p <= 4:
            return ga_v.at[half * 4 + p - 1]
        if p <= 8:
            return w1_v.at[half, p - 5]
        return g2_v.at[(p - 9) % 2, :, :, half, (p - 9) // 2]

    def ag_copy(p, i, src, dst, dev):
        return remote(src, dst, r.sent.at[p, i], r.came.at[p, i], dev)

    def rows_one(p):
        return pl.ds(0, CUT) if p else pl.ds(0, 8)

    def rs_rows_one(n):
        return pl.ds(0, ROWS) if SHORT <= n < PIECES else rows_one(order[n])

    rows_two = pl.ds(CUT, ROWS - CUT)

    def sides(p):
        along_x, along_y = (x_dev, xy_x), (y_dev, xy_y)
        return (along_x, along_y) if p % 2 == 0 else (along_y, along_x)

    at_start, at_end = zpos == 0, zpos == 3
    inside = jnp.logical_and(zpos > 0, zpos < 3)

    def along_z(p, fn):
        if p < DIRECT:
            for k in (1, 2, 3):
                fn(k)
        else:
            pl.when(jnp.logical_not(at_end))(lambda: fn(1))
            fn(2)
            pl.when(jnp.logical_not(at_start))(lambda: fn(3))

    def pass_to_end(p, fn):
        if p >= DIRECT:
            pl.when(zpos == 1)(lambda: fn(3, 3))
            pl.when(zpos == 2)(lambda: fn(0, 1))

    def ag_z(p, k, at):
        return ag_copy(p, k - 1, at, at, z_dev(k))

    def ag_z2(p, k, at):
        return ag_copy(p, 8 + k, at, at, z_dev(k))

    def ag_z_from(p, k, at, base=0):
        return ag_copy(p, base + k - 1, at, at, z_dev(k))

    def ag_pass(p, far, k, at, base=0):
        return ag_copy(p, base + (0 if k == 3 else 2), at, at, z_dev(k))

    def ag_x(p, k, v):
        at = v.at[z_of(4 - k), xy] if k else v.at[zpos, xy]
        return ag_copy(p, 4 if k else 3, at, at, x_dev)

    def ag_y(p, k, v):
        at = v.at[z_of(4 - k), xy] if k else v.at[zpos, xy]
        return ag_copy(p, 6 if k else 5, at, at, y_dev)

    def own_from(p, side, v):
        at = v.at[zpos, sides(p)[side][1]]
        return ag_copy(p, 3 if side == p % 2 else 5, at, at, sides(p)[side][0])

    def three_from(p, side, v):
        at = v.at[pl.ds(0, 3), sides(p)[side][1]]
        return ag_copy(p, 4 if side == p % 2 else 6, at, at, sides(p)[side][0])

    def ag_one(p, v, col):
        at = v.at[:, col, rows_one(p)]
        return ag_copy(p, 7, at, at, sides(p)[1][0])

    def ag_two(p, v, col):
        at = v.at[zpos, col, rows_two]
        return ag_copy(p, 8, at, at, sides(p)[0][0])

    def ag_a(p):
        v = weight_piece(p, core)
        along_z(p, lambda k: ag_z(p, k, v.at[zpos, xy]).start())
        ag_x(p, 0, v).start()
        ag_y(p, 0, v).start()

    def ag_b(p):
        v = weight_piece(p, core)
        for k in (1, 3):
            ag_z_from(p, k, v.at[z_of(4 - k), xy]).wait_recv()
            ag_x(p, k, v).start()
            ag_y(p, k, v).start()

    def ag_b2(p):
        v = weight_piece(p, core)
        ag_z_from(p, 2, v.at[z_of(2), xy]).wait_recv()
        pass_to_end(p, lambda far, k: ag_pass(p, far, k, v.at[far, xy]).start())
        ag_x(p, 2, v).start()
        ag_y(p, 2, v).start()

    def ag_c2(p):
        if p:
            v = weight_piece(p, core)
            own_from(p, 1, v).wait_recv()
            ag_two(p, v, sides(p)[1][1]).start()

    def ag_c3(p):
        if p:
            v = weight_piece(p, core)
            ag_two(p, v, xy_d).wait_recv()
            along_z(p, lambda k: ag_z2(p, k, v.at[zpos, xy_d, rows_two]).start())

    def ag_c1(p):
        v = weight_piece(p, core)
        own_from(p, 0, v).wait_recv()
        three_from(p, 0, v).wait_recv()
        ag_one(p, v, sides(p)[0][1]).start()

    def ag_c4(p):
        if p:
            v = weight_piece(p, core)
            ag_z_from(p, 2, v.at[z_of(2), xy_d, rows_two], 9).wait_recv()
            pass_to_end(
                p, lambda far, k: ag_pass(p, far, k, v.at[far, xy_d, rows_two], 9).start()
            )

    def ag_d(p):
        v = weight_piece(p, core)
        if p == 0:
            own_from(p, 1, v).wait_recv()
        three_from(p, 1, v).wait_recv()
        ag_one(p, v, xy_d).wait_recv()
        if p:
            for k in (1, 3):
                ag_z_from(p, k, v.at[z_of(4 - k), xy_d, rows_two], 9).wait_recv()
        ag_copy(p, 12, v, v, sib).start()

    def ag_e(p):
        v = weight_piece(p, other)
        ag_copy(p, 12, v, v, sib).wait_recv()

    def ag_f(p):
        v = weight_piece(p, core)
        along_z(p, lambda k: ag_z(p, k, v.at[zpos, xy]).wait_send())
        pass_to_end(p, lambda far, k: ag_pass(p, far, k, v.at[far, xy]).wait_send())
        ag_x(p, 0, v).wait_send()
        ag_y(p, 0, v).wait_send()
        three = v.at[pl.ds(0, 3), xy]
        ag_copy(p, 4, three, three, x_dev).wait_send()
        ag_copy(p, 6, three, three, y_dev).wait_send()
        ag_one(p, v, sides(p)[0][1]).wait_send()
        if p:
            ag_two(p, v, sides(p)[1][1]).wait_send()
            along_z(p, lambda k: ag_z2(p, k, v.at[zpos, xy_d, rows_two]).wait_send())
            pass_to_end(
                p, lambda far, k: ag_pass(p, far, k, v.at[far, xy_d, rows_two], 9).wait_send()
            )
        ag_copy(p, 12, v, v, sib).wait_send()

    ahead = 3

    def ag_step(s):
        for lag, stage in AG_STAGES:
            if 0 <= s - lag <= PIECES and not (lag < 0 and stage is ag_a and s - lag < ahead):
                stage(s - lag)

    AG_STAGES = (
        (-ahead, ag_a),
        (0, ag_b),
        (-1, ag_b2),
        (-1, ag_c2),
        (0, ag_c3),
        (1, ag_c1),
        (1, ag_c4),
        (2, ag_d),
    )

    order = [9, 10, 11, 12, 5, 6, 7, 8, 4, 1, 2, 3, 0]

    def rs_bufs(n):
        if n == PIECES:
            return r.s0, r.s1, r.s2, r.s3
        ring = [getattr(r, name).at[n % RINGS[name]] for name in ("l0", "l1", "l2", "l3")]
        if n >= SHORT:
            ring[1], ring[3] = r.l1s.at[n - SHORT], r.l3s.at[n - SHORT]
        return tuple(ring)

    def rs_copy(n, i, src, dst, dev):
        return remote(src, dst, r.sent.at[n, i], r.came.at[n, i], dev)

    def credit_wait(n, i):
        if RINGS[CREDIT_RINGS[i]] <= n < (PIECES if i in (0, 3, 4) else SHORT):
            pl.semaphore_wait(r.credit.at[2 * i + n % 2], 1)

    def credit_give(n, i, dev):
        if n < (PIECES if i in (0, 3, 4) else SHORT) - RINGS[CREDIT_RINGS[i]]:
            at = r.credit.at[2 * i + n % 2]
            pl.semaphore_signal(at, inc=1, device_id=(dev,), device_id_type=MESH_ID)

    def add_to(g, at, landed):
        g[at] = (g[at].astype(F32) + landed.astype(F32)).astype(g.dtype)

    def z_send(n, first, block, land, k):
        return rs_copy(n, first + k - 1, block(z_of(k)), land.at[k - 1], z_dev(k))

    def z_far(n, first, block, land, k):
        return rs_copy(n, first + 3, block(3 if k == 1 else 0), land.at[3], z_dev(k))

    def sum_z_start(n, first, credit, block, land):
        def near(k):
            credit_wait(n, credit + k - 1)
            z_send(n, first, block, land, k).start()

        def far(k):
            near(2)
            credit_wait(n, credit + 3)
            z_far(n, first, block, land, k).start()

        pl.when(jnp.logical_not(at_end))(lambda: near(1))
        pl.when(jnp.logical_not(at_start))(lambda: near(3))
        pl.when(at_start)(lambda: far(1))
        pl.when(at_end)(lambda: far(3))

    def sum_z_pass(n, first, credit, block, land):
        def go():
            z_far(n, first, block, land, 1).wait_recv()
            add_to(block(z_of(2)), Ellipsis, land[3])
            pl.when(zpos == 1)(lambda: credit_give(n, credit + 3, z_dev(3)))
            pl.when(zpos == 2)(lambda: credit_give(n, credit + 3, z_dev(1)))
            credit_wait(n, credit + 1)
            z_send(n, first, block, land, 2).start()

        pl.when(inside)(go)

    def sum_z_end(n, first, credit, block, land):
        z_send(n, first, block, land, 2).wait_recv()
        pl.when(jnp.logical_not(at_start))(lambda: z_send(n, first, block, land, 1).wait_recv())
        pl.when(jnp.logical_not(at_end))(lambda: z_send(n, first, block, land, 3).wait_recv())
        total = land[0].astype(F32) + land[1].astype(F32) + land[2].astype(F32)

        def give():
            credit_give(n, credit + 1, z_dev(2))
            pl.when(jnp.logical_not(at_start))(lambda: credit_give(n, credit, z_dev(3)))
            pl.when(jnp.logical_not(at_end))(lambda: credit_give(n, credit + 2, z_dev(1)))

        return total, give

    def sum_z_sent(n, first, block, land):
        z_send(n, first, block, land, 2).wait_send()
        pl.when(jnp.logical_not(at_end))(lambda: z_send(n, first, block, land, 1).wait_send())
        pl.when(jnp.logical_not(at_start))(lambda: z_send(n, first, block, land, 3).wait_send())
        pl.when(at_start)(lambda: z_far(n, first, block, land, 1).wait_send())
        pl.when(at_end)(lambda: z_far(n, first, block, land, 3).wait_send())

    def diagonal(n):
        g = grad_piece(order[n], core)
        return lambda z: g.at[z, xy_d, rows_two], r.lz.at[n % RINGS["lz"]]

    def own_line(n):
        g = grad_piece(order[n], core)
        return lambda z: g.at[z, xy], rs_bufs(n)[3]

    def rs_main(n):
        p = order[n]
        g, land = grad_piece(p, core), rs_bufs(n)[2]
        (a_dev, a), (b_dev, b) = sides(n)
        one = rs_rows_one(n)
        early, late_one, late_two = [], [], []
        if n < SHORT:
            early.append((7, g.at[:, a, rows_two], land.at[0, :, rows_two], a_dev))
        late_one.append((7, g.at[:, a, one], land.at[0, :, one], a_dev))
        early.append((8, g.at[:, b, one], land.at[1, :, one], b_dev))
        if n < SHORT:
            for k in (1, 2, 3):
                z = z_of(k)
                early.append((8, g.at[z, b, rows_two], land.at[1, z, rows_two], b_dev))
            late_two.append((8, g.at[zpos, b, rows_two], land.at[1, zpos, rows_two], b_dev))
        return [[rs_copy(n, *entry) for entry in group] for group in (early, late_one, late_two)]

    def rs_all(n):
        g, land = grad_piece(order[n], core), rs_bufs(n)[2]
        (a_dev, a), (b_dev, b) = sides(n)
        return [
            rs_copy(n, 7, g.at[:, a], land.at[0], a_dev),
            rs_copy(n, 8, g.at[:, b], land.at[1], b_dev),
        ]

    def rs_one(n):
        p = order[n]
        return rs_copy(
            n, 1, grad_piece(p, core).at[:, xy_d, rs_rows_one(n)], rs_bufs(n)[1], sides(n)[1][0]
        )

    def rs_two(n):
        p = order[n]
        return rs_copy(
            n,
            6,
            grad_piece(p, core).at[zpos, xy_d, rows_two],
            r.lt.at[n % RINGS["lt"]],
            sides(n)[0][0],
        )

    def rs_swap(n):
        p = order[n]
        half = pl.ds(pl.multiple_of(other * 24, 8), 24)
        return rs_copy(n, 13, r.fs.at[p - 1, half], r.fr.at[p - 1], sib)

    def rs_0(n):
        credit_wait(n, 0)
        rs_copy(n, 0, grad_piece(order[n], other), rs_bufs(n)[0], sib).start()

    def rs_1(n):
        p = order[n]
        l0 = rs_bufs(n)[0]
        g = grad_piece(p, core)
        rs_copy(n, 0, grad_piece(p, other), l0, sib).wait_recv()

        def body(i, carry):
            g[i] = (g[i].astype(F32) + l0[i].astype(F32)).astype(g.dtype)
            return carry

        lax.fori_loop(0, 4, body, 0)
        credit_give(n, 0, sib)
        credit_wait(n, 1)
        rs_one(n).start()
        if n < SHORT:
            sum_z_start(n, 2, 5, *diagonal(n))

    def rs_early(n):
        credit_wait(n, 3)
        credit_wait(n, 4)
        for copy in rs_main(n)[0]:
            copy.start()

    def rs_2(n):
        p = order[n]
        g, l1 = grad_piece(p, core), rs_bufs(n)[1]
        (a_dev, a), (b_dev, b) = sides(n)
        rs_one(n).wait_recv()
        for z in range(4):
            add_to(g, (z, a, rs_rows_one(n)), l1[z])
        credit_give(n, 1, b_dev)
        if n < SHORT:
            sum_z_pass(n, 2, 5, *diagonal(n))
        else:
            rs_early(n)
            for copy in rs_main(n)[1]:
                copy.start()

    def rs_3(n):
        p = order[n]
        if p:
            g = grad_piece(p, core)
            total, give = sum_z_end(n, 2, 5, *diagonal(n))
            add_to(g, (zpos, xy_d, rows_two), total)
            give()
            credit_wait(n, 2)
            rs_two(n).start()
            rs_early(n)
            for copy in rs_main(n)[1]:
                copy.start()

    def rs_4(n):
        p = order[n]
        if p:
            g = grad_piece(p, core)
            (a_dev, a), (b_dev, b) = sides(n)
            rs_two(n).wait_recv()
            add_to(g, (zpos, b, rows_two), r.lt[n % RINGS["lt"]])
            credit_give(n, 2, a_dev)
            for copy in rs_main(n)[2]:
                copy.start()

    def rs_5(n):
        p = order[n]
        g, l2 = grad_piece(p, core), rs_bufs(n)[2]
        (a_dev, a), (b_dev, b) = sides(n)
        for copy in rs_all(n):
            copy.wait_recv()
        for z in range(4):
            add_to(g, (z, xy), l2[0, z].astype(F32) + l2[1, z].astype(F32))
        credit_give(n, 3, a_dev)
        credit_give(n, 4, b_dev)
        if n < SHORT:
            sum_z_start(n, 9, 9, *own_line(n))
        else:
            for k in (1, 2, 3):
                z_send(n, 9, *own_line(n), k).start()

    def rs_6(n):
        sum_z_pass(n, 9, 9, *own_line(n))

    def rs_7(n):
        p = order[n]
        if n < SHORT:
            total, give = sum_z_end(n, 9, 9, *own_line(n))
        else:
            land = rs_bufs(n)[3]
            for k in (1, 2, 3):
                z_send(n, 9, *own_line(n), k).wait_recv()
            total = land[0].astype(F32) + land[1].astype(F32) + land[2].astype(F32)
        total = total + grad_piece(p, core)[zpos, xy].astype(F32)
        if p == 0:
            r.osm[...] = total
        elif p >= 9:
            i, j = (p - 9) // 2, (p - 9) % 2
            r.o2[ROWS * i : ROWS * (i + 1), COLS * j : COLS * (j + 1)] = total
        else:
            r.fs[p - 1] = total
            rs_swap(n).start()
        if n < SHORT:
            give()

    def rs_8(n):
        p = order[n]
        if p == 0 or p >= 9:
            return
        mine = pl.ds(pl.multiple_of(core * 24, 8), 24)
        rs_swap(n).wait_recv()
        out, first = (r.oq, 0) if p <= 3 else ((r.op, 0) if p == 4 else (r.o1, p - 5))
        for g in range(3):
            lanes = slice(LANES * g, LANES * (g + 1))
            base = 768 * g + 256 * (p - 1) if p <= 3 else 768 * first + 256 * g
            out[:, pl.ds(pl.multiple_of(base + LANES * core, LANES), LANES)] = r.fs[
                p - 1, mine, lanes
            ]
            out[:, pl.ds(pl.multiple_of(base + LANES * other, LANES), LANES)] = r.fr[
                p - 1, :, lanes
            ]

    def rs_9(n):
        p = order[n]
        rs_copy(n, 0, grad_piece(p, other), rs_bufs(n)[0], sib).wait_send()
        rs_one(n).wait_send()
        for copy in rs_all(n):
            copy.wait_send()
        if n < SHORT:
            sum_z_sent(n, 2, *diagonal(n))
            rs_two(n).wait_send()
            sum_z_sent(n, 9, *own_line(n))
        else:
            for k in (1, 2, 3):
                z_send(n, 9, *own_line(n), k).wait_send()
        if 1 <= p <= 8:
            rs_swap(n).wait_send()

    rs_long = list(zip((rs_0, rs_1, rs_2, rs_3, rs_4, rs_5, rs_6, rs_7, rs_8, rs_9), LONG_AT))
    rs_short = list(zip((rs_0, rs_1, rs_2, rs_5, rs_7, rs_8, rs_9), SHORT_AT))

    rs_small = list(zip((rs_0, rs_1, rs_2, rs_5, rs_7, rs_8, rs_9), SMALL_AT))

    def rs_tick(tick):
        for n in range(PIECES + 1):
            for stage, after in rs_long if n < SHORT else rs_short if n < PIECES else rs_small:
                if STARTS[n] + after == tick:
                    stage(n)

    def rows_of(f):
        return pl.ds(pl.multiple_of(f * WIN, WIN), WIN)

    def loop(count, body, ticks=()):
        def step(i, carry):
            body(i)
            for k, tick in enumerate(ticks):
                if tick is not None:
                    pl.when(i == k)(tick)
            return carry

        lax.fori_loop(0, count, step, 0)

    def steps(fn, *numbers):
        return [functools.partial(fn, s) if s is not None else None for s in numbers]

    def natural(ref, lead, rows):
        parts = []
        for g in range(3):
            for h in range(2):
                parts.append(ref[(h, *lead, rows, pl.ds(LANES * g, LANES))])
        return parts

    def put(ref, lead, rows, value):
        for g in range(3):
            for h in range(2):
                at = 256 * g + LANES * h
                ref[(h, *lead, rows, pl.ds(LANES * g, LANES))] = value[:, at : at + LANES]

    def put_a(piece, rows, value):
        for g in range(3):
            for h in range(2):
                at = 256 * g + LANES * h
                r.gp[4 * h + piece, rows, LANES * g : LANES * (g + 1)] = value[:, at : at + LANES]

    def pre_rows(t, h, s):
        return pl.ds(pl.multiple_of((2 * t + h) * 1024 + s.start, 8), s.stop - s.start)

    def pre_tile(t, s):
        return jnp.concatenate([gp_m[pre_rows(t, h, s), :] for h in range(2)], axis=1)

    def mixed_in(f):
        rw = rows_of(f)
        return jnp.where(r.st[rw, 0:1] > 0, r.v24[6:7, :], r.tok[rw, :].astype(F32))

    def masks():
        bits = jnp.transpose(r.mask[...].astype(F32))
        for j in range(8):
            keep = 1.0 - r.pad[j // 2].astype(F32)
            col = bits[:, j : j + 1]
            r.st[LANES * j : LANES * (j + 1), 0:1] = col
            r.st[LANES * j : LANES * (j + 1), 1:2] = col * keep

    def mask_grad(f):
        rw = rows_of(f)
        r.dm[rw, :] = (r.dm[rw, :].astype(F32) * r.st[rw, 1:2]).astype(BF16)

    def spread_small():
        table = r.sv[...].reshape(32, 8, LANES)
        rows = [table[:, i, :].astype(BF16) for i in range(3)]
        at = 0
        for name, row, lane0, width in SMALL_ROWS:
            pick, owner = spread_tables(lane0, width)
            full = jnp.sum(jnp.where(owner, dot_nn(rows[row], pick), 0.0), axis=0, keepdims=True)
            if name == "qkv_bias":
                for t in range(3):
                    for g in range(3):
                        at_piece, at_whole = 768 * t + 256 * g, 768 * g + 256 * t
                        r.bqkv[:, at_piece : at_piece + 256] = full[:, at_whole : at_whole + 256]
            elif name == "fc1_bias":
                r.bfc1[...] = full
            else:
                r.v24[at : at + 1, :] = full
                at += 1
        r.gv[...] = jnp.zeros_like(r.gv)

    def collect_small():
        table = [jnp.zeros((32, LANES), F32) for _ in range(3)]
        at = 0
        for name, row, lane0, width in SMALL_ROWS:
            pick, owner = spread_tables(lane0, width)
            if name == "qkv_bias":
                chunks = [768 * t + 256 * g for g in range(3) for t in range(3)]
                full = jnp.concatenate([r.gbqkv[:, c : c + 256] for c in chunks], axis=1)
            elif name == "fc1_bias":
                full = r.gbfc1[...]
            else:
                full = r.gv[at : at + 1, :]
                at += 1
            parts = jnp.where(owner, full, 0.0)
            for _ in range(3):
                high = parts.astype(BF16)
                table[row] = table[row] + dot_nt(high, pick)
                parts = parts - high.astype(F32)
        flat = r.sg.reshape(256, LANES)
        r.sg[...] = jnp.zeros_like(r.sg)
        for i in range(3):
            flat[pl.ds(i, 32, stride=8), :] = table[i]

    def ln1(f):
        rw = rows_of(f)
        x = mixed_in(f)
        row_mean, row_scale = row_stats(x)
        r.st[rw, 2:3] = row_mean
        r.st[rw, 3:4] = row_scale
        r.normed[rw, :] = ((x - row_mean) * row_scale * r.v24[0:1, :] + r.v24[1:2, :]).astype(BF16)

    def qkv(t):
        w = jnp.concatenate(natural(wa_m, (t,), pl.ds(0, 768)), axis=1)
        cols = tile(t)
        bias = r.bqkv[:, cols]
        for i in range(4):
            s = slice(WIN * i, WIN * (i + 1))
            r.packed[s, cols] = (dot_nn(r.normed[s, :], w) + bias).astype(BF16)

    def part(t, i, pair):
        return pl.ds(pl.multiple_of(768 * t + 256 * i + LANES * pair, LANES), LANES)

    def head_cols(t, pair):
        return pl.ds(pl.multiple_of(256 * t + LANES * pair, LANES), LANES)

    low_lanes = lax.broadcasted_iota(jnp.int32, (WIN, LANES), 1) < HEAD_DIM

    def two_heads(a):
        z = jnp.zeros_like(a)
        return jnp.concatenate([jnp.where(low_lanes, a, z), jnp.where(low_lanes, z, a)], axis=0)

    def attention(t, f, pair):
        rw = rows_of(f)
        q2 = r.packed[rw, part(t, 0, pair)] * jnp.asarray(0.125, BF16)
        k2 = r.packed[rw, part(t, 1, pair)]
        v2 = r.packed[rw, part(t, 2, pair)]
        scores = dot_nt(two_heads(q2), k2)
        row_max = jnp.max(scores, axis=1, keepdims=True)
        e = jnp.exp(scores - row_max)
        total = jnp.sum(e, axis=1, keepdims=True)
        inv = 1.0 / total
        log_total = row_max + jnp.log(total)
        for h in range(2):
            col = jnp.broadcast_to(log_total[WIN * h : WIN * (h + 1)], (WIN, 8))
            r.lse[pl.ds(f * 12 + 4 * t + 2 * pair + h, 1), :] = jnp.transpose(col)[0:1]
        e = e.astype(BF16)
        out = dot_nn(jnp.concatenate([e[:WIN], e[WIN:]], axis=1), two_heads(v2))
        scale = jnp.where(
            low_lanes,
            jnp.broadcast_to(inv[:WIN], (WIN, LANES)),
            jnp.broadcast_to(inv[WIN:], (WIN, LANES)),
        )
        r.att[rw, head_cols(t, pair)] = (out * scale).astype(BF16)

    def heads_forward(t, between):
        qkv(t)
        for f in range(4):
            for pair in range(2):
                attention(t, f, pair)
            if f == 1:
                for k, tick in enumerate(between):
                    if tick is not None:
                        pl.when(t == k)(tick)

    def project(f):
        rw = rows_of(f)
        w = jnp.concatenate(natural(wa_m, (3,), pl.ds(0, 768)), axis=1)
        middle = mixed_in(f) + (dot_nn(r.att[rw, :], w) + r.v24[2:3, :])
        r.mid[rw, :] = middle
        row_mean, row_scale = row_stats(middle)
        r.st[rw, 4:5] = row_mean
        r.st[rw, 5:6] = row_scale
        r.n2[rw, :] = ((middle - row_mean) * row_scale * r.v24[3:4, :] + r.v24[4:5, :]).astype(BF16)

    def tile(t):
        return pl.ds(pl.multiple_of(t * 768, 768), 768)

    def fc1(t):
        w = jnp.concatenate(natural(w1_m, (t,), pl.ds(0, 768)), axis=1)
        cols = tile(t)
        bias = r.bfc1[:, cols]
        for i in range(4):
            s = slice(WIN * i, WIN * (i + 1))
            act, slope = gelu_and_slope(dot_nn(r.n2[s, :], w) + bias)
            r.hact[s, cols] = act.astype(BF16)
            slope = slope.astype(BF16)
            gp_m[pre_rows(t, 0, s), :] = slope[:, :COLS]
            gp_m[pre_rows(t, 1, s), :] = slope[:, COLS:]

    def turn(src):
        def body(f):
            rw = rows_of(f)
            r.tr[:, rw] = r.normed[rw, :].T if src == 0 else r.n2[rw, :].T

        return body

    def fc2(n):
        cols = pl.ds(pl.multiple_of(n * 256, 256), 256)
        parts = []
        for i in range(2):
            g = 2 * n + i
            lanes = pl.ds(pl.multiple_of(lax.rem(g, 3) * LANES, LANES), LANES)
            parts.append(w2_m[lax.div(g, 3), :, lanes])
        w = jnp.concatenate(parts, axis=1)
        for i in range(4):
            s = slice(WIN * i, WIN * (i + 1))
            r.n2[s, cols] = (
                dot_nn(r.hact[s, :], w) + (r.mid[s, cols] + r.v24[5:6, cols])
            ).astype(BF16)

    def grad_fc2(t):
        cols = tile(t)
        g = dot_tn(r.hact[:, cols], r.dm[...]).astype(BF16)
        g2_m[0, cols, :] = g[:, :COLS]
        g2_m[1, cols, :] = g[:, COLS:]

    def grad_pre(t):
        cols = tile(t)
        w = jnp.concatenate([w2_m[0, cols, :], w2_m[1, cols, :]], axis=1)
        sums = jnp.zeros((1, 768), F32)
        for i in range(4):
            s = slice(WIN * i, WIN * (i + 1))
            d = (dot_nt(r.dm[s, :], w) * pre_tile(t, s).astype(F32)).astype(BF16)
            gp_m[pre_rows(t, 0, s), :] = d[:, :COLS]
            gp_m[pre_rows(t, 1, s), :] = d[:, COLS:]
            sums = sums + jnp.sum(d.astype(F32), axis=0, keepdims=True)
        r.gbfc1[:, cols] = sums

    def grad_fc1(t):
        put(w1_m, (t,), pl.ds(0, 768), dot_nn(r.tr[...], pre_tile(t, slice(0, 1024))).astype(BF16))

    def grad_norm_two(n):
        rw = rows_of(n)
        parts = []
        for t in range(4):
            parts += natural(w1_m, (t,), rw)
        w = jnp.concatenate(parts, axis=1)
        for i in range(4):
            s = slice(WIN * i, WIN * (i + 1))
            pre = jnp.concatenate([pre_tile(t, s) for t in range(4)], axis=1)
            r.dn[s, rw] = dot_nt(pre, w)

    def grad_middle(f):
        rw = rows_of(f)
        dy = r.dm[rw, :].astype(F32)
        dx, gain, shift = norm_backward(
            r.mid[rw, :], r.st[rw, 4:5], r.st[rw, 5:6], r.dn[rw, :], r.v24[3:4, :]
        )
        d = dy + dx
        low = d.astype(BF16)
        r.mid[rw, :] = d
        r.dm[rw, :] = low
        r.gv[3:4, :] += gain
        r.gv[4:5, :] += shift
        r.gv[5:6, :] += jnp.sum(dy, axis=0, keepdims=True)
        r.gv[2:3, :] += jnp.sum(low.astype(F32), axis=0, keepdims=True)

    def grad_proj(j):
        rw = rows_of(j)
        put_a(3, rw, dot_tn(r.att[:, rw], r.dm[...]).astype(BF16))

    def grad_att(f):
        rw = rows_of(f)
        w = jnp.concatenate(natural(wa_m, (3,), pl.ds(0, 768)), axis=1)
        r.n2[rw, :] = dot_nt(r.dm[rw, :], w).astype(BF16)

    def attention_backward(t, f, pair):
        rw = rows_of(f)
        q2 = r.packed[rw, part(t, 0, pair)] * jnp.asarray(0.125, BF16)
        k2 = r.packed[rw, part(t, 1, pair)]
        v2 = r.packed[rw, part(t, 2, pair)]
        qs, ds, ks = two_heads(q2), two_heads(r.n2[rw, head_cols(t, pair)]), two_heads(k2)
        at = f * 12 + 4 * t + 2 * pair
        log_total = jnp.concatenate([r.lse[pl.ds(at + h, 1), :] for h in range(2)], axis=1)
        probs = jnp.exp(dot_nt(k2, qs) - log_total)
        prod = probs * dot_nt(v2, ds)
        row_dot = jnp.sum(prod, axis=0, keepdims=True)
        d_scores = (prod - probs * row_dot).astype(BF16)
        r.packed[rw, part(t, 2, pair)] = dot_nn(probs.astype(BF16), ds).astype(BF16)
        r.packed[rw, part(t, 1, pair)] = dot_nn(d_scores, qs).astype(BF16)
        stacked = jnp.concatenate([d_scores[:, :WIN], d_scores[:, WIN:]], axis=0)
        r.packed[rw, part(t, 0, pair)] = (dot_tn(stacked, ks) * 0.125).astype(BF16)

    def heads_backward(t):
        def body(f):
            for pair in range(2):
                attention_backward(t, f, pair)

        return body

    def grad_qkv(t):
        cols = tile(t)
        d = r.packed[:, cols]
        put_a(t, slice(None), dot_nn(r.tr[...], d).astype(BF16))
        r.gbqkv[:, cols] = jnp.sum(d.astype(F32), axis=0, keepdims=True)

    def grad_norm_one(n):
        rw = rows_of(n)
        parts = []
        for t in range(3):
            parts += natural(wa_m, (t,), rw)
        w = jnp.concatenate(parts, axis=1)
        for i in range(4):
            s = slice(WIN * i, WIN * (i + 1))
            r.dn[s, rw] = dot_nt(r.packed[s, :], w)

    def grad_mixed(f):
        rw = rows_of(f)
        dx, gain, shift = norm_backward(
            mixed_in(f), r.st[rw, 2:3], r.st[rw, 3:4], r.dn[rw, :], r.v24[0:1, :]
        )
        d = r.mid[rw, :] + dx
        chosen = r.st[rw, 0:1] > 0
        r.dn[rw, :] = jnp.where(chosen, 0.0, d)
        r.gv[0:1, :] += gain
        r.gv[1:2, :] += shift
        r.gv[6:7, :] += jnp.sum(jnp.where(chosen, d, 0.0), axis=0, keepdims=True)

    loads = [
        pltpu.make_async_copy(r.og_in, r.dm, r.ld.at[0]),
        pltpu.make_async_copy(r.tok_in, r.tok, r.ld.at[1]),
    ]
    for q in range(2):
        loads.append(
            pltpu.make_async_copy(
                r.s2w.at[:, pl.ds(COLS * q, COLS)], w2_shard.at[q, zpos, xy, core], r.ld.at[2 + q]
            )
        )
    loads.append(pltpu.make_async_copy(r.small, r.sv.at[zpos, xy, core], r.ld.at[4]))
    for copy in loads:
        copy.start()

    for land in (r.lz, r.l3):
        for slot in range(land.shape[0]):
            land[slot, 0] = jnp.zeros_like(land[slot, 0])
            land[slot, 2] = jnp.zeros_like(land[slot, 2])

    barrier = pltpu.get_barrier_semaphore()
    peers = [sib, x_dev, y_dev, z_dev(1), z_dev(2), z_dev(3)]
    for dev in peers:
        pl.semaphore_signal(barrier, inc=1, device_id=(dev,), device_id_type=MESH_ID)

    def shard_half(t, half):
        ref, first = (r.sq, 0) if t < 3 else ((r.sp, 0) if t == 3 else (r.s1w, t - 4))
        parts = []
        for g in range(3):
            base = 768 * g + 256 * t if t < 3 else 768 * first + 256 * g
            a = ref[:, base : base + LANES].astype(F32)
            b = ref[:, base + LANES : base + 2 * LANES].astype(F32)
            parts.append(jnp.where(half == 0, a, b))
        return jnp.concatenate(parts, axis=1)

    for t in range(8):
        away = jnp.concatenate([shard_half(t, other), jnp.zeros((8, COLS), F32)], axis=0)
        r.l0[0, t // 4, t % 4, 0:32] = away.astype(BF16)
    pl.semaphore_wait(barrier, len(peers))
    away, came = [r.l0.at[i, pl.ds(0, 2), :, pl.ds(0, 32)] for i in range(2)]
    swap = remote(away, came, r.prep.at[0], r.prep.at[1], sib)
    swap.start()
    loads[4].wait()
    ag_a(0)
    swap.wait()
    for t in range(8):
        here = shard_half(t, core)
        there = r.l0[1, t // 4, t % 4, 0:32].astype(F32)[:24]
        block = jnp.concatenate(
            [jnp.where(core == 0, here, there), jnp.where(core == 0, there, here)], axis=0
        ).astype(BF16)
        if t < 4:
            wa_v[core, t, zpos, xy] = block
        else:
            w1_v[core, t - 4, zpos, xy] = block
        if t + 1 < ahead:
            ag_a(t + 1)
    ag_step(-1)
    loads[2].wait()
    loads[3].wait()
    def ag(*numbers):
        def go():
            for s in numbers:
                ag_step(s)

        return go

    def rs(*numbers):
        def go():
            for s in numbers:
                rs_tick(s)

        return go

    def arrive(p, *numbers):
        def go():
            ag(*numbers)()
            ag_e(p)

        return go

    ag_step(0)
    masks()
    ag_step(1)
    loads[0].wait()
    loop(4, mask_grad)
    ag_step(2)
    ag_e(0)
    ag_step(3)
    loads[1].wait()
    spread_small()
    loop(4, ln1)
    ag_e(1)
    loop(
        3,
        functools.partial(heads_forward, between=[ag(4), ag(6), ag(8)]),
        [arrive(2, 5), arrive(3, 7), arrive(4, 9)],
    )
    loop(4, project, [None, ag(10), None, None])
    keep_middle = pltpu.make_async_copy(r.mid, r.ig, r.ld.at[5])
    keep_middle.start()
    ag_e(5)
    loop(4, fc1, [arrive(6, 11), arrive(7), arrive(8, 12), ag(13)])
    loop(4, turn(1))
    for p in range(9):
        ag_f(p)
    loop(4, grad_fc2, [None, ag(14), None, None])
    rs_tick(0)
    for p in range(9, PIECES + 1):
        ag_e(p)
        ag_f(p)
    loop(4, grad_pre, [rs(1), rs(2), rs(3), rs(4)])
    loop(3, grad_norm_two, [rs(5), rs(6), rs(7)])
    loop(4, grad_fc1, [rs(8), rs(9), rs(10), rs(11)])
    keep_middle.wait()
    loop(4, grad_middle, [None, rs(12), None, rs(13)])
    loop(3, grad_proj)
    rs_tick(14)
    loop(4, grad_att)
    rs_tick(15)
    loop(4, turn(0))
    loop(4, heads_backward(0), [rs(16), rs(17), rs(18), rs(19)])
    grad_qkv(0)
    rs_tick(20)
    loop(4, heads_backward(1), [rs(21), rs(22), rs(23), rs(24)])
    grad_qkv(1)
    rs_tick(25)
    loop(4, heads_backward(2), [rs(26), rs(27), rs(28), rs(29)])
    grad_qkv(2)
    rs_tick(30)
    loop(3, grad_norm_one, [rs(31), rs(32), rs(33)])
    loop(4, grad_mixed, [None, rs(34), None, rs(35)])
    load_middle = pltpu.make_async_copy(r.ig, r.mid, r.ld.at[6])
    load_middle.start()
    collect_small()
    rs_tick(36)
    load_middle.wait()
    write_grad = pltpu.make_async_copy(r.dn, r.ig, r.ld.at[7])
    write_grad.start()
    rs_tick(37)
    loop(3, fc2, [rs(38, 39), rs(40, 41), rs(42, 43)])
    write_out = pltpu.make_async_copy(r.n2, r.bo, r.ld.at[0])
    write_out.start()
    last = max(at + (LONG_AT if n < SHORT else SHORT_AT)[-1] for n, at in enumerate(STARTS))
    for tick in range(44, last + 1):
        rs_tick(tick)
    write_grad.wait()
    write_out.wait()


HAND_PARTS = 4


def hand_over(*refs):
    arrays, small, outs = refs[:6], refs[6], refs[7:13]
    vectors, held, (in_sems, out_sems) = refs[13:-8], refs[-8:-2], refs[-2:]
    loads, stores = [], []
    for src, buf, dst in zip(arrays, held, outs):
        parts = HAND_PARTS if src.shape[0] == 1024 else 1
        rows = src.shape[0] // parts
        for i in range(parts):
            at, n = pl.ds(rows * i, rows), len(loads)
            loads.append(pltpu.make_async_copy(src.at[at], buf.at[at], in_sems.at[n]))
            stores.append(pltpu.make_async_copy(buf.at[at], dst.at[at], out_sems.at[n]))
    for copy in loads:
        copy.start()
    for ref, (_, row, lane0, width) in zip(vectors, SMALL_ROWS):
        ref[...] = small[row : row + 1, lane0 : lane0 + width]
    for load, store in zip(loads, stores):
        load.wait()
        store.start()
    for copy in stores:
        copy.wait()


def fused_device(
    tokens,
    mask_bits,
    pad_flags,
    ln1_gain,
    ln1_bias,
    qkv_weight,
    qkv_bias,
    proj_weight,
    proj_bias,
    ln2_gain,
    ln2_bias,
    fc1_weight,
    fc1_bias,
    fc2_weight,
    fc2_bias,
    mask_embed,
    out_grad,
):
    held = dict(
        ln1_gain=ln1_gain,
        ln1_bias=ln1_bias,
        proj_bias=proj_bias,
        ln2_gain=ln2_gain,
        ln2_bias=ln2_bias,
        fc2_bias=fc2_bias,
        mask_embed=mask_embed,
        qkv_bias=qkv_bias,
        fc1_bias=fc1_bias,
    )
    small = jnp.zeros((8 * LANES,), F32)
    for name, row, lane0, width in SMALL_ROWS:
        first = row * LANES + lane0
        small = small + jnp.pad(held[name].astype(F32), (first, 8 * LANES - first - width))
    small = small.reshape(8, LANES)
    any_spec = pl.BlockSpec(memory_space=pl.ANY)
    vmem = pl.BlockSpec(memory_space=pltpu.VMEM)
    smem = pl.BlockSpec(memory_space=pltpu.SMEM)
    shape = jax.ShapeDtypeStruct
    outs = pl.pallas_call(
        fused_kernel,
        out_shape=(
            shape((1024, 768), BF16),
            shape((1024, 768), F32),
            shape((24, 2304), F32),
            shape((24, 768), F32),
            shape((24, 3072), F32),
            shape((96, 768), F32),
            shape((8, LANES), F32),
        ),
        in_specs=[any_spec, any_spec, vmem, smem, any_spec, vmem, vmem, vmem, any_spec],
        out_specs=(any_spec, any_spec, vmem, vmem, vmem, vmem, vmem),
        scratch_shapes=[pltpu.VMEM(*spec) for spec in SCRATCH.values()] + list(SEMS.values()),
        compiler_params=pltpu.CompilerParams(
            collective_id=0, has_side_effects=True, vmem_limit_bytes=64 * 2**20
        ),
    )(
        tokens,
        out_grad,
        mask_bits.reshape(8, LANES),
        pad_flags,
        small,
        qkv_weight,
        proj_weight,
        fc1_weight,
        fc2_weight,
    )
    held = pl.pallas_call(
        hand_over,
        out_shape=tuple(shape(o.shape, o.dtype) for o in outs[:6])
        + tuple(shape((1, width), F32) for _, _, _, width in SMALL_ROWS),
        in_specs=[any_spec] * 6 + [vmem],
        out_specs=(any_spec,) * 6 + (vmem,) * len(SMALL_ROWS),
        scratch_shapes=[pltpu.VMEM(o.shape, o.dtype) for o in outs[:6]]
        + [pltpu.SemaphoreType.DMA((6 * HAND_PARTS,)), pltpu.SemaphoreType.DMA((6 * HAND_PARTS,))],
        compiler_params=pltpu.CompilerParams(vmem_limit_bytes=63 * 2**20),
    )(*outs)
    block_out, input_grad, gq, gpj, g1, g2 = held[:6]
    v = {entry[0]: vec.reshape(entry[3]) for entry, vec in zip(SMALL_ROWS, held[6:])}
    return (
        block_out,
        input_grad,
        v["ln1_gain"],
        v["ln1_bias"],
        gq,
        v["qkv_bias"],
        gpj,
        v["proj_bias"],
        v["ln2_gain"],
        v["ln2_bias"],
        g1,
        v["fc1_bias"],
        g2,
        v["fc2_bias"],
        v["mask_embed"],
    )


def solution(mesh):
    placed = (
        P("fsdp", None),
        P("fsdp"),
        P("fsdp"),
        P("fsdp"),
        P("fsdp"),
        P("fsdp", None),
        P("fsdp"),
        P("fsdp", None),
        P("fsdp"),
        P("fsdp"),
        P("fsdp"),
        P("fsdp", None),
        P("fsdp"),
        P("fsdp", None),
        P("fsdp"),
        P("fsdp"),
        P("fsdp", None),
    )
    return jax.shard_map(
        fused_device if mesh.shape["fsdp"] == 32 else per_device,
        mesh=mesh,
        in_specs=placed,
        out_specs=(
            P("fsdp", None),
            P("fsdp", None),
            P("fsdp"),
            P("fsdp"),
            P("fsdp", None),
            P("fsdp"),
            P("fsdp", None),
            P("fsdp"),
            P("fsdp"),
            P("fsdp"),
            P("fsdp", None),
            P("fsdp"),
            P("fsdp", None),
            P("fsdp"),
            P("fsdp"),
        ),
        check_vma=False,
    )
```

```python
import functools

import jax
import jax.numpy as jnp
from jax import lax
from jax.experimental import pallas as pl
from jax.experimental.pallas import tpu as pltpu
from jax.sharding import PartitionSpec as P

HEADS = 12
HEAD_DIM = 64
WIN = 256


epsilon = 1e-06


def norm_rows(values, gain_vec, shift_vec):
    row_mean = jnp.mean(values, axis=-1, keepdims=True)
    centered = values - row_mean
    variance = jnp.mean(centered * centered, axis=-1, keepdims=True)
    return centered * lax.rsqrt(variance + epsilon) * gain_vec + shift_vec


def gelu_exact(values):
    return jax.nn.gelu(values, approximate=False)


def forward_pass(full, tok_rows, masked):
    (
        gain_one,
        shift_one,
        qkv_w,
        qkv_b,
        proj_w,
        proj_b,
        gain_two,
        shift_two,
        up_w,
        up_b,
        down_w,
        down_b,
        mask_vec,
    ) = full
    row_count = tok_rows.shape[0]
    width = tok_rows.shape[1]
    frames = row_count // WIN
    mixed_in = jnp.where(
        masked[:, None] > 0, mask_vec.astype(jnp.float32)[None, :], tok_rows.astype(jnp.float32)
    )
    normed = norm_rows(
        mixed_in, gain_one.astype(jnp.float32), shift_one.astype(jnp.float32)
    ).astype(jnp.bfloat16)
    packed = (
        jnp.dot(normed, qkv_w, preferred_element_type=jnp.float32) + qkv_b.astype(jnp.float32)
    ).astype(jnp.bfloat16)
    heads_view = packed.reshape(frames, WIN, 3, HEADS, HEAD_DIM)
    scores = jnp.einsum(
        "fqhd,fkhd->fhqk",
        heads_view[:, :, 0],
        heads_view[:, :, 1],
        preferred_element_type=jnp.float32,
    ) * HEAD_DIM ** (-0.5)
    row_max = jnp.max(scores, axis=-1, keepdims=True)
    exp_terms = jnp.exp(scores - row_max)
    row_total = jnp.sum(exp_terms, axis=-1, keepdims=True)
    probs_low = (exp_terms / row_total).astype(jnp.bfloat16)
    log_total = row_max + jnp.log(row_total)
    attended = jnp.einsum(
        "fhqk,fkhd->fqhd", probs_low, heads_view[:, :, 2], preferred_element_type=jnp.float32
    )
    attended = attended.reshape(row_count, width).astype(jnp.bfloat16)
    middle = (
        mixed_in
        + jnp.dot(attended, proj_w, preferred_element_type=jnp.float32)
        + proj_b.astype(jnp.float32)
    )
    normed_two = norm_rows(
        middle, gain_two.astype(jnp.float32), shift_two.astype(jnp.float32)
    ).astype(jnp.bfloat16)
    hidden_pre = jnp.dot(normed_two, up_w, preferred_element_type=jnp.float32) + up_b.astype(
        jnp.float32
    )
    hidden_act = gelu_exact(hidden_pre).astype(jnp.bfloat16)
    result = (
        middle
        + jnp.dot(hidden_act, down_w, preferred_element_type=jnp.float32)
        + down_b.astype(jnp.float32)
    )
    saved = (
        mixed_in,
        normed,
        packed,
        log_total,
        attended,
        middle,
        normed_two,
        hidden_pre,
        hidden_act,
    )
    return (result, saved)


def mlp_backward(full, saved, cotangent):
    (
        gain_one,
        shift_one,
        qkv_w,
        qkv_b,
        proj_w,
        proj_b,
        gain_two,
        shift_two,
        up_w,
        up_b,
        down_w,
        down_b,
        mask_vec,
    ) = full
    mixed_in, normed, packed, log_total, attended, middle, normed_two, hidden_pre, hidden_act = (
        saved
    )
    down_in = cotangent.astype(jnp.bfloat16)
    grad_down = jnp.einsum("tf,td->fd", hidden_act, down_in, preferred_element_type=jnp.float32)
    grad_down_b = jnp.sum(down_in.astype(jnp.float32), axis=0)
    grad_act = jnp.einsum("td,fd->tf", down_in, down_w, preferred_element_type=jnp.float32)
    gelu_value, gelu_pull = jax.vjp(gelu_exact, hidden_pre)
    grad_pre = gelu_pull(grad_act)[0].astype(jnp.bfloat16)
    grad_up = jnp.einsum("td,tf->df", normed_two, grad_pre, preferred_element_type=jnp.float32)
    grad_up_b = jnp.sum(grad_pre.astype(jnp.float32), axis=0)
    grad_norm_two = jnp.einsum("tf,df->td", grad_pre, up_w, preferred_element_type=jnp.float32)
    norm_value, norm_pull = jax.vjp(
        norm_rows, middle, gain_two.astype(jnp.float32), shift_two.astype(jnp.float32)
    )
    grad_middle, grad_gain_two, grad_shift_two = norm_pull(grad_norm_two)
    grad_middle = grad_middle + cotangent
    return (
        grad_middle,
        (grad_gain_two, grad_shift_two, grad_up, grad_up_b, grad_down, grad_down_b),
    )


def attn_backward(full, saved, grad_middle, masked):
    (
        gain_one,
        shift_one,
        qkv_w,
        qkv_b,
        proj_w,
        proj_b,
        gain_two,
        shift_two,
        up_w,
        up_b,
        down_w,
        down_b,
        mask_vec,
    ) = full
    mixed_in, normed, packed, log_total, attended, middle, normed_two, hidden_pre, hidden_act = (
        saved
    )
    row_count = grad_middle.shape[0]
    width = grad_middle.shape[1]
    frames = row_count // WIN
    proj_in = grad_middle.astype(jnp.bfloat16)
    grad_proj = jnp.einsum("td,te->de", attended, proj_in, preferred_element_type=jnp.float32)
    grad_proj_b = jnp.sum(proj_in.astype(jnp.float32), axis=0)
    grad_att = jnp.einsum("te,de->td", proj_in, proj_w, preferred_element_type=jnp.float32).astype(
        jnp.bfloat16
    )
    grad_att = grad_att.reshape(frames, WIN, HEADS, HEAD_DIM)
    heads_view = packed.reshape(frames, WIN, 3, HEADS, HEAD_DIM)
    query_part = heads_view[:, :, 0]
    key_part = heads_view[:, :, 1]
    value_part = heads_view[:, :, 2]
    score_scale = HEAD_DIM ** (-0.5)
    scores = (
        jnp.einsum("fqhd,fkhd->fhqk", query_part, key_part, preferred_element_type=jnp.float32)
        * score_scale
    )
    probs_full = jnp.exp(scores - log_total)
    probs_low = probs_full.astype(jnp.bfloat16)
    grad_value = jnp.einsum(
        "fhqk,fqhd->fkhd", probs_low, grad_att, preferred_element_type=jnp.float32
    )
    grad_probs = jnp.einsum(
        "fqhd,fkhd->fhqk", grad_att, value_part, preferred_element_type=jnp.float32
    )
    row_dot = jnp.sum(grad_probs * probs_full, axis=-1, keepdims=True)
    grad_scores = (probs_full * (grad_probs - row_dot)).astype(jnp.bfloat16)
    grad_query = (
        jnp.einsum("fhqk,fkhd->fqhd", grad_scores, key_part, preferred_element_type=jnp.float32)
        * score_scale
    )
    grad_key = (
        jnp.einsum("fhqk,fqhd->fkhd", grad_scores, query_part, preferred_element_type=jnp.float32)
        * score_scale
    )
    grad_packed = (
        jnp.stack([grad_query, grad_key, grad_value], axis=2)
        .reshape(row_count, 3 * width)
        .astype(jnp.bfloat16)
    )
    grad_qkv = jnp.einsum("td,te->de", normed, grad_packed, preferred_element_type=jnp.float32)
    grad_qkv_b = jnp.sum(grad_packed.astype(jnp.float32), axis=0)
    grad_normed = jnp.einsum("te,de->td", grad_packed, qkv_w, preferred_element_type=jnp.float32)
    first_value, first_pull = jax.vjp(
        norm_rows, mixed_in, gain_one.astype(jnp.float32), shift_one.astype(jnp.float32)
    )
    grad_mixed, grad_gain_one, grad_shift_one = first_pull(grad_normed)
    grad_mixed = grad_mixed + grad_middle
    chosen = masked[:, None] > 0
    tok_grad = jnp.where(chosen, 0.0, grad_mixed)
    grad_mask = jnp.sum(jnp.where(chosen, grad_mixed, 0.0), axis=0)
    return (
        tok_grad,
        (grad_gain_one, grad_shift_one, grad_qkv, grad_qkv_b, grad_proj, grad_proj_b, grad_mask),
    )


def per_device(
    tokens,
    mask_bits,
    pad_flags,
    ln1_gain,
    ln1_bias,
    qkv_weight,
    qkv_bias,
    proj_weight,
    proj_bias,
    ln2_gain,
    ln2_bias,
    fc1_weight,
    fc1_bias,
    fc2_weight,
    fc2_bias,
    mask_embed,
    out_grad,
):
    full = (
        lax.all_gather(ln1_gain, "fsdp", axis=0, tiled=True),
        lax.all_gather(ln1_bias, "fsdp", axis=0, tiled=True),
        lax.all_gather(qkv_weight, "fsdp", axis=0, tiled=True),
        lax.all_gather(qkv_bias, "fsdp", axis=0, tiled=True),
        lax.all_gather(proj_weight, "fsdp", axis=0, tiled=True),
        lax.all_gather(proj_bias, "fsdp", axis=0, tiled=True),
        lax.all_gather(ln2_gain, "fsdp", axis=0, tiled=True),
        lax.all_gather(ln2_bias, "fsdp", axis=0, tiled=True),
        lax.all_gather(fc1_weight, "fsdp", axis=0, tiled=True),
        lax.all_gather(fc1_bias, "fsdp", axis=0, tiled=True),
        lax.all_gather(fc2_weight, "fsdp", axis=0, tiled=True),
        lax.all_gather(fc2_bias, "fsdp", axis=0, tiled=True),
        lax.all_gather(mask_embed, "fsdp", axis=0, tiled=True),
    )
    result, saved = forward_pass(full, tokens, mask_bits)
    full_back = (
        lax.all_gather(ln1_gain, "fsdp", axis=0, tiled=True),
        lax.all_gather(ln1_bias, "fsdp", axis=0, tiled=True),
        lax.all_gather(qkv_weight, "fsdp", axis=0, tiled=True),
        lax.all_gather(qkv_bias, "fsdp", axis=0, tiled=True),
        lax.all_gather(proj_weight, "fsdp", axis=0, tiled=True),
        lax.all_gather(proj_bias, "fsdp", axis=0, tiled=True),
        lax.all_gather(ln2_gain, "fsdp", axis=0, tiled=True),
        lax.all_gather(ln2_bias, "fsdp", axis=0, tiled=True),
        lax.all_gather(fc1_weight, "fsdp", axis=0, tiled=True),
        lax.all_gather(fc1_bias, "fsdp", axis=0, tiled=True),
        lax.all_gather(fc2_weight, "fsdp", axis=0, tiled=True),
        lax.all_gather(fc2_bias, "fsdp", axis=0, tiled=True),
        lax.all_gather(mask_embed, "fsdp", axis=0, tiled=True),
    )
    kept_acts = forward_pass(full_back, tokens, mask_bits)[1]
    row_count = tokens.shape[0]
    frames = row_count // WIN
    frame_keep = (1 - pad_flags).astype(jnp.float32)
    tok_weight = (mask_bits.astype(jnp.float32).reshape(frames, WIN) * frame_keep[:, None]).reshape(
        row_count
    )
    cotangent = out_grad.astype(jnp.float32) * tok_weight[:, None]
    grad_middle, mlp_grads = mlp_backward(full_back, kept_acts, cotangent)
    tok_grad, attn_grads = attn_backward(full_back, kept_acts, grad_middle, mask_bits)
    shares = (
        lax.psum_scatter(attn_grads[0], "fsdp", scatter_dimension=0, tiled=True),
        lax.psum_scatter(attn_grads[1], "fsdp", scatter_dimension=0, tiled=True),
        lax.psum_scatter(attn_grads[2], "fsdp", scatter_dimension=0, tiled=True),
        lax.psum_scatter(attn_grads[3], "fsdp", scatter_dimension=0, tiled=True),
        lax.psum_scatter(attn_grads[4], "fsdp", scatter_dimension=0, tiled=True),
        lax.psum_scatter(attn_grads[5], "fsdp", scatter_dimension=0, tiled=True),
        lax.psum_scatter(mlp_grads[0], "fsdp", scatter_dimension=0, tiled=True),
        lax.psum_scatter(mlp_grads[1], "fsdp", scatter_dimension=0, tiled=True),
        lax.psum_scatter(mlp_grads[2], "fsdp", scatter_dimension=0, tiled=True),
        lax.psum_scatter(mlp_grads[3], "fsdp", scatter_dimension=0, tiled=True),
        lax.psum_scatter(mlp_grads[4], "fsdp", scatter_dimension=0, tiled=True),
        lax.psum_scatter(mlp_grads[5], "fsdp", scatter_dimension=0, tiled=True),
        lax.psum_scatter(attn_grads[6], "fsdp", scatter_dimension=0, tiled=True),
    )
    return (
        result.astype(jnp.bfloat16),
        tok_grad,
        shares[0],
        shares[1],
        shares[2],
        shares[3],
        shares[4],
        shares[5],
        shares[6],
        shares[7],
        shares[8],
        shares[9],
        shares[10],
        shares[11],
        shares[12],
    )


F32 = jnp.float32
BF16 = jnp.bfloat16
LANES = 128
ROWS = 48
COLS = 384
PIECES = 12
CUT = 16
RINGS = dict(l0=2, l1=4, lz=4, lt=4, l2=4, l3=4)
CREDIT_RINGS = ["l0", "l1", "lt", "l2", "l2"] + ["lz"] * 4 + ["l3"] * 4
SHORT = 11
DIRECT = 1
LONG_AT = (0, 2, 5, 8, 11, 14, 17, 20, 22, 23)
SHORT_AT = (0, 2, 5, 8, 11, 13, 14)
SMALL_AT = (0, 1, 3, 5, 7, 8, 9)
STARTS = (0, 2, 4, 6, 9, 11, 14, 17, 20, 23, 26, 30, 36)
MESH_ID = pl.DeviceIdType.MESH


def dot_nn(a, b):
    return lax.dot_general(a, b, (((1,), (0,)), ((), ())), preferred_element_type=F32)


def dot_nt(a, b):
    return lax.dot_general(a, b, (((1,), (1,)), ((), ())), preferred_element_type=F32)


def dot_tn(a, b):
    return lax.dot_general(a, b, (((0,), (0,)), ((), ())), preferred_element_type=F32)


def row_stats(values):
    row_mean = jnp.mean(values, axis=-1, keepdims=True)
    centered = values - row_mean
    return row_mean, lax.rsqrt(jnp.mean(centered * centered, axis=-1, keepdims=True) + epsilon)


def gelu_and_slope(x):
    phi = 0.5 + 0.5 * lax.erf(x * 0.7071067811865476)
    return x * phi, phi + x * jnp.exp(x * x * -0.5) * 0.3989422804014327


def norm_backward(x, row_mean, row_scale, grad, gain):
    x_hat = (x - row_mean) * row_scale
    prod = grad * x_hat
    grad_gain = jnp.sum(prod, axis=0, keepdims=True)
    grad_shift = jnp.sum(grad, axis=0, keepdims=True)
    dx = grad * gain
    mean_one = jnp.mean(dx, axis=-1, keepdims=True)
    mean_two = jnp.mean(dx * x_hat, axis=-1, keepdims=True)
    return row_scale * (dx - mean_one - x_hat * mean_two), grad_gain, grad_shift


SMALL_ROWS = (
    ("ln1_gain", 0, 0, 24),
    ("ln1_bias", 0, 24, 24),
    ("proj_bias", 0, 48, 24),
    ("ln2_gain", 0, 72, 24),
    ("ln2_bias", 0, 96, 24),
    ("fc2_bias", 1, 0, 24),
    ("mask_embed", 1, 24, 24),
    ("qkv_bias", 1, 48, 72),
    ("fc1_bias", 2, 0, 96),
)


def spread_tables(lane0, width):
    count = 32 * width
    k = lax.broadcasted_iota(jnp.int32, (1, count), 1)
    pick = lax.broadcasted_iota(jnp.int32, (LANES, count), 0) == lax.rem(k, width) + lane0
    owner = lax.broadcasted_iota(jnp.int32, (32, count), 0) == lax.div(k, width)
    return jnp.where(pick, 1.0, 0.0).astype(BF16), owner


SCRATCH = dict(
    tok=((1024, 768), BF16),
    dm=((1024, 768), BF16),
    st=((1024, 8), F32),
    v24=((8, 768), F32),
    bqkv=((1, 2304), F32),
    bfc1=((1, 3072), F32),
    gv=((8, 768), F32),
    gbqkv=((1, 2304), F32),
    gbfc1=((1, 3072), F32),
    normed=((1024, 768), BF16),
    n2=((1024, 768), BF16),
    tr=((768, 1024), BF16),
    packed=((1024, 2304), BF16),
    att=((1024, 768), BF16),
    mid=((1024, 768), F32),
    hact=((1024, 3072), BF16),
    gp=((11, 768, COLS), BF16),
    dn=((1024, 768), F32),
    lse=((48, 256), F32),
    wa=((8, 768, COLS), BF16),
    w1=((8, 768, COLS), BF16),
    w2=((8, 768, COLS), BF16),
    g2=((8, 768, COLS), BF16),
    sv=((4, 4, 2, 8, LANES), F32),
    sg=((4, 4, 2, 8, LANES), F32),
    fs=((8, ROWS, COLS), F32),
    fr=((8, ROWS // 2, COLS), F32),
    l0=((RINGS["l0"], 4, 4, ROWS, COLS), BF16),
    l1=((RINGS["l1"], 4, CUT, COLS), BF16),
    lz=((RINGS["lz"], 4, ROWS - CUT, COLS), BF16),
    lt=((RINGS["lt"], ROWS - CUT, COLS), BF16),
    l2=((RINGS["l2"], 2, 4, ROWS, COLS), BF16),
    l3=((RINGS["l3"], 4, ROWS, COLS), BF16),
    l1s=((PIECES - SHORT, 4, ROWS, COLS), BF16),
    l3s=((PIECES - SHORT, 3, ROWS, COLS), BF16),
    s0=((4, 4, 8, LANES), F32),
    s1=((4, 8, LANES), F32),
    s2=((2, 4, 8, LANES), F32),
    s3=((4, 8, LANES), F32),
)
SEMS = dict(
    ld=pltpu.SemaphoreType.DMA((8,)),
    prep=pltpu.SemaphoreType.DMA((2,)),
    sent=pltpu.SemaphoreType.DMA((PIECES + 1, 14)),
    came=pltpu.SemaphoreType.DMA((PIECES + 1, 14)),
    credit=pltpu.SemaphoreType.REGULAR((26,)),
)


class Refs:
    pass


def fused_kernel(*refs):
    r = Refs()
    names = ["tok_in", "og_in", "mask", "pad", "small", "sq", "sp", "s1w", "s2w"]
    names += ["bo", "ig", "oq", "op", "o1", "o2", "osm"]
    names += list(SCRATCH) + list(SEMS)
    for name, ref in zip(names, refs):
        setattr(r, name, ref)

    me = lax.axis_index("fsdp")
    core = lax.rem(me, 2)
    other = 1 - core
    chip = lax.div(me, 2)
    xpos = lax.rem(chip, 2)
    ypos = lax.rem(lax.div(chip, 2), 2)
    zpos = lax.div(chip, 4)
    xy = lax.rem(chip, 4)
    xy_x = xy + 1 - 2 * xpos
    xy_y = xy + 2 - 4 * ypos
    xy_d = xy_x + 2 - 4 * ypos
    sib = me + 1 - 2 * core
    x_dev = me + 2 - 4 * xpos
    y_dev = me + 4 - 8 * ypos

    def z_of(k):
        return lax.rem(zpos + k, 4)

    def z_dev(k):
        return me + 8 * (z_of(k) - zpos)

    def remote(src, dst, ssem, rsem, dev):
        return pltpu.make_async_remote_copy(
            src_ref=src,
            dst_ref=dst,
            send_sem=ssem,
            recv_sem=rsem,
            device_id=(dev,),
            device_id_type=MESH_ID,
        )

    wa_v = r.wa.reshape(2, 4, 4, 4, ROWS, COLS)
    w1_v = r.w1.reshape(2, 4, 4, 4, ROWS, COLS)
    w2_v = r.w2.reshape(2, 4, 4, 2, 2, ROWS, COLS)
    w2_shard = r.w2.reshape(2, 4, 4, 2, 2 * ROWS, COLS)
    w2_m = r.w2.reshape(2, 3072, COLS)
    wa_m = r.wa.reshape(2, 4, 768, COLS)
    w1_m = r.w1.reshape(2, 4, 768, COLS)
    g2_v = r.g2.reshape(2, 4, 4, 2, 2, ROWS, COLS)
    g2_m = r.g2.reshape(2, 3072, COLS)
    ga_v = r.gp.reshape(11, 4, 4, ROWS, COLS)
    gp_m = r.gp.reshape(11 * 768, COLS)

    def weight_piece(p, half):
        if p == 0:
            return r.sv.at[:, :, half]
        if p <= 4:
            return wa_v.at[half, p - 1]
        if p <= 8:
            return w1_v.at[half, p - 5]
        return w2_v.at[(p - 9) % 2, :, :, half, (p - 9) // 2]

    def grad_piece(p, half):
        if p == 0:
            return r.sg.at[:, :, half]
        if p <= 4:
            return ga_v.at[half * 4 + p - 1]
        if p <= 8:
            return w1_v.at[half, p - 5]
        return g2_v.at[(p - 9) % 2, :, :, half, (p - 9) // 2]

    def ag_copy(p, i, src, dst, dev):
        return remote(src, dst, r.sent.at[p, i], r.came.at[p, i], dev)

    def rows_one(p):
        return pl.ds(0, CUT) if p else pl.ds(0, 8)

    def rs_rows_one(n):
        return pl.ds(0, ROWS) if SHORT <= n < PIECES else rows_one(order[n])

    rows_two = pl.ds(CUT, ROWS - CUT)

    def sides(p):
        along_x, along_y = (x_dev, xy_x), (y_dev, xy_y)
        return (along_x, along_y) if p % 2 == 0 else (along_y, along_x)

    at_start, at_end = zpos == 0, zpos == 3
    inside = jnp.logical_and(zpos > 0, zpos < 3)

    def along_z(p, fn):
        if p < DIRECT:
            for k in (1, 2, 3):
                fn(k)
        else:
            pl.when(jnp.logical_not(at_end))(lambda: fn(1))
            fn(2)
            pl.when(jnp.logical_not(at_start))(lambda: fn(3))

    def pass_to_end(p, fn):
        if p >= DIRECT:
            pl.when(zpos == 1)(lambda: fn(3, 3))
            pl.when(zpos == 2)(lambda: fn(0, 1))

    def ag_z(p, k, at):
        return ag_copy(p, k - 1, at, at, z_dev(k))

    def ag_z2(p, k, at):
        return ag_copy(p, 8 + k, at, at, z_dev(k))

    def ag_z_from(p, k, at, base=0):
        return ag_copy(p, base + k - 1, at, at, z_dev(k))

    def ag_pass(p, far, k, at, base=0):
        return ag_copy(p, base + (0 if k == 3 else 2), at, at, z_dev(k))

    def ag_x(p, k, v):
        at = v.at[z_of(4 - k), xy] if k else v.at[zpos, xy]
        return ag_copy(p, 4 if k else 3, at, at, x_dev)

    def ag_y(p, k, v):
        at = v.at[z_of(4 - k), xy] if k else v.at[zpos, xy]
        return ag_copy(p, 6 if k else 5, at, at, y_dev)

    def own_from(p, side, v):
        at = v.at[zpos, sides(p)[side][1]]
        return ag_copy(p, 3 if side == p % 2 else 5, at, at, sides(p)[side][0])

    def three_from(p, side, v):
        at = v.at[pl.ds(0, 3), sides(p)[side][1]]
        return ag_copy(p, 4 if side == p % 2 else 6, at, at, sides(p)[side][0])

    def ag_one(p, v, col):
        at = v.at[:, col, rows_one(p)]
        return ag_copy(p, 7, at, at, sides(p)[1][0])

    def ag_two(p, v, col):
        at = v.at[zpos, col, rows_two]
        return ag_copy(p, 8, at, at, sides(p)[0][0])

    def ag_a(p):
        v = weight_piece(p, core)
        along_z(p, lambda k: ag_z(p, k, v.at[zpos, xy]).start())
        ag_x(p, 0, v).start()
        ag_y(p, 0, v).start()

    def ag_b(p):
        v = weight_piece(p, core)
        for k in (1, 3):
            ag_z_from(p, k, v.at[z_of(4 - k), xy]).wait_recv()
            ag_x(p, k, v).start()
            ag_y(p, k, v).start()

    def ag_b2(p):
        v = weight_piece(p, core)
        ag_z_from(p, 2, v.at[z_of(2), xy]).wait_recv()
        pass_to_end(p, lambda far, k: ag_pass(p, far, k, v.at[far, xy]).start())
        ag_x(p, 2, v).start()
        ag_y(p, 2, v).start()

    def ag_c2(p):
        if p:
            v = weight_piece(p, core)
            own_from(p, 1, v).wait_recv()
            ag_two(p, v, sides(p)[1][1]).start()

    def ag_c3(p):
        if p:
            v = weight_piece(p, core)
            ag_two(p, v, xy_d).wait_recv()
            along_z(p, lambda k: ag_z2(p, k, v.at[zpos, xy_d, rows_two]).start())

    def ag_c1(p):
        v = weight_piece(p, core)
        own_from(p, 0, v).wait_recv()
        three_from(p, 0, v).wait_recv()
        ag_one(p, v, sides(p)[0][1]).start()

    def ag_c4(p):
        if p:
            v = weight_piece(p, core)
            ag_z_from(p, 2, v.at[z_of(2), xy_d, rows_two], 9).wait_recv()
            pass_to_end(
                p, lambda far, k: ag_pass(p, far, k, v.at[far, xy_d, rows_two], 9).start()
            )

    def ag_d(p):
        v = weight_piece(p, core)
        if p == 0:
            own_from(p, 1, v).wait_recv()
        three_from(p, 1, v).wait_recv()
        ag_one(p, v, xy_d).wait_recv()
        if p:
            for k in (1, 3):
                ag_z_from(p, k, v.at[z_of(4 - k), xy_d, rows_two], 9).wait_recv()
        ag_copy(p, 12, v, v, sib).start()

    def ag_e(p):
        v = weight_piece(p, other)
        ag_copy(p, 12, v, v, sib).wait_recv()

    def ag_f(p):
        v = weight_piece(p, core)
        along_z(p, lambda k: ag_z(p, k, v.at[zpos, xy]).wait_send())
        pass_to_end(p, lambda far, k: ag_pass(p, far, k, v.at[far, xy]).wait_send())
        ag_x(p, 0, v).wait_send()
        ag_y(p, 0, v).wait_send()
        three = v.at[pl.ds(0, 3), xy]
        ag_copy(p, 4, three, three, x_dev).wait_send()
        ag_copy(p, 6, three, three, y_dev).wait_send()
        ag_one(p, v, sides(p)[0][1]).wait_send()
        if p:
            ag_two(p, v, sides(p)[1][1]).wait_send()
            along_z(p, lambda k: ag_z2(p, k, v.at[zpos, xy_d, rows_two]).wait_send())
            pass_to_end(
                p, lambda far, k: ag_pass(p, far, k, v.at[far, xy_d, rows_two], 9).wait_send()
            )
        ag_copy(p, 12, v, v, sib).wait_send()

    ahead = 3

    def ag_step(s):
        for lag, stage in AG_STAGES:
            if 0 <= s - lag <= PIECES and not (lag < 0 and stage is ag_a and s - lag < ahead):
                stage(s - lag)

    AG_STAGES = (
        (-ahead, ag_a),
        (0, ag_b),
        (-1, ag_b2),
        (-1, ag_c2),
        (0, ag_c3),
        (1, ag_c1),
        (1, ag_c4),
        (2, ag_d),
    )

    order = [9, 10, 11, 12, 5, 6, 7, 8, 4, 1, 2, 3, 0]

    def rs_bufs(n):
        if n == PIECES:
            return r.s0, r.s1, r.s2, r.s3
        ring = [getattr(r, name).at[n % RINGS[name]] for name in ("l0", "l1", "l2", "l3")]
        if n >= SHORT:
            ring[1], ring[3] = r.l1s.at[n - SHORT], r.l3s.at[n - SHORT]
        return tuple(ring)

    def rs_copy(n, i, src, dst, dev):
        return remote(src, dst, r.sent.at[n, i], r.came.at[n, i], dev)

    def credit_wait(n, i):
        if RINGS[CREDIT_RINGS[i]] <= n < (PIECES if i in (0, 3, 4) else SHORT):
            pl.semaphore_wait(r.credit.at[2 * i + n % 2], 1)

    def credit_give(n, i, dev):
        if n < (PIECES if i in (0, 3, 4) else SHORT) - RINGS[CREDIT_RINGS[i]]:
            at = r.credit.at[2 * i + n % 2]
            pl.semaphore_signal(at, inc=1, device_id=(dev,), device_id_type=MESH_ID)

    def add_to(g, at, landed):
        g[at] = (g[at].astype(F32) + landed.astype(F32)).astype(g.dtype)

    def z_send(n, first, block, land, k):
        return rs_copy(n, first + k - 1, block(z_of(k)), land.at[k - 1], z_dev(k))

    def z_far(n, first, block, land, k):
        return rs_copy(n, first + 3, block(3 if k == 1 else 0), land.at[3], z_dev(k))

    def sum_z_start(n, first, credit, block, land):
        def near(k):
            credit_wait(n, credit + k - 1)
            z_send(n, first, block, land, k).start()

        def far(k):
            near(2)
            credit_wait(n, credit + 3)
            z_far(n, first, block, land, k).start()

        pl.when(jnp.logical_not(at_end))(lambda: near(1))
        pl.when(jnp.logical_not(at_start))(lambda: near(3))
        pl.when(at_start)(lambda: far(1))
        pl.when(at_end)(lambda: far(3))

    def sum_z_pass(n, first, credit, block, land):
        def go():
            z_far(n, first, block, land, 1).wait_recv()
            add_to(block(z_of(2)), Ellipsis, land[3])
            pl.when(zpos == 1)(lambda: credit_give(n, credit + 3, z_dev(3)))
            pl.when(zpos == 2)(lambda: credit_give(n, credit + 3, z_dev(1)))
            credit_wait(n, credit + 1)
            z_send(n, first, block, land, 2).start()

        pl.when(inside)(go)

    def sum_z_end(n, first, credit, block, land):
        z_send(n, first, block, land, 2).wait_recv()
        pl.when(jnp.logical_not(at_start))(lambda: z_send(n, first, block, land, 1).wait_recv())
        pl.when(jnp.logical_not(at_end))(lambda: z_send(n, first, block, land, 3).wait_recv())
        total = land[0].astype(F32) + land[1].astype(F32) + land[2].astype(F32)

        def give():
            credit_give(n, credit + 1, z_dev(2))
            pl.when(jnp.logical_not(at_start))(lambda: credit_give(n, credit, z_dev(3)))
            pl.when(jnp.logical_not(at_end))(lambda: credit_give(n, credit + 2, z_dev(1)))

        return total, give

    def sum_z_sent(n, first, block, land):
        z_send(n, first, block, land, 2).wait_send()
        pl.when(jnp.logical_not(at_end))(lambda: z_send(n, first, block, land, 1).wait_send())
        pl.when(jnp.logical_not(at_start))(lambda: z_send(n, first, block, land, 3).wait_send())
        pl.when(at_start)(lambda: z_far(n, first, block, land, 1).wait_send())
        pl.when(at_end)(lambda: z_far(n, first, block, land, 3).wait_send())

    def diagonal(n):
        g = grad_piece(order[n], core)
        return lambda z: g.at[z, xy_d, rows_two], r.lz.at[n % RINGS["lz"]]

    def own_line(n):
        g = grad_piece(order[n], core)
        return lambda z: g.at[z, xy], rs_bufs(n)[3]

    def rs_main(n):
        p = order[n]
        g, land = grad_piece(p, core), rs_bufs(n)[2]
        (a_dev, a), (b_dev, b) = sides(n)
        one = rs_rows_one(n)
        early, late_one, late_two = [], [], []
        if n < SHORT:
            early.append((7, g.at[:, a, rows_two], land.at[0, :, rows_two], a_dev))
        late_one.append((7, g.at[:, a, one], land.at[0, :, one], a_dev))
        early.append((8, g.at[:, b, one], land.at[1, :, one], b_dev))
        if n < SHORT:
            for k in (1, 2, 3):
                z = z_of(k)
                early.append((8, g.at[z, b, rows_two], land.at[1, z, rows_two], b_dev))
            late_two.append((8, g.at[zpos, b, rows_two], land.at[1, zpos, rows_two], b_dev))
        return [[rs_copy(n, *entry) for entry in group] for group in (early, late_one, late_two)]

    def rs_all(n):
        g, land = grad_piece(order[n], core), rs_bufs(n)[2]
        (a_dev, a), (b_dev, b) = sides(n)
        return [
            rs_copy(n, 7, g.at[:, a], land.at[0], a_dev),
            rs_copy(n, 8, g.at[:, b], land.at[1], b_dev),
        ]

    def rs_one(n):
        p = order[n]
        return rs_copy(
            n, 1, grad_piece(p, core).at[:, xy_d, rs_rows_one(n)], rs_bufs(n)[1], sides(n)[1][0]
        )

    def rs_two(n):
        p = order[n]
        return rs_copy(
            n,
            6,
            grad_piece(p, core).at[zpos, xy_d, rows_two],
            r.lt.at[n % RINGS["lt"]],
            sides(n)[0][0],
        )

    def rs_swap(n):
        p = order[n]
        half = pl.ds(pl.multiple_of(other * 24, 8), 24)
        return rs_copy(n, 13, r.fs.at[p - 1, half], r.fr.at[p - 1], sib)

    def rs_0(n):
        credit_wait(n, 0)
        rs_copy(n, 0, grad_piece(order[n], other), rs_bufs(n)[0], sib).start()

    def rs_1(n):
        p = order[n]
        l0 = rs_bufs(n)[0]
        g = grad_piece(p, core)
        rs_copy(n, 0, grad_piece(p, other), l0, sib).wait_recv()

        def body(i, carry):
            g[i] = (g[i].astype(F32) + l0[i].astype(F32)).astype(g.dtype)
            return carry

        lax.fori_loop(0, 4, body, 0)
        credit_give(n, 0, sib)
        credit_wait(n, 1)
        rs_one(n).start()
        if n < SHORT:
            sum_z_start(n, 2, 5, *diagonal(n))

    def rs_early(n):
        credit_wait(n, 3)
        credit_wait(n, 4)
        for copy in rs_main(n)[0]:
            copy.start()

    def rs_2(n):
        p = order[n]
        g, l1 = grad_piece(p, core), rs_bufs(n)[1]
        (a_dev, a), (b_dev, b) = sides(n)
        rs_one(n).wait_recv()
        for z in range(4):
            add_to(g, (z, a, rs_rows_one(n)), l1[z])
        credit_give(n, 1, b_dev)
        if n < SHORT:
            sum_z_pass(n, 2, 5, *diagonal(n))
        else:
            rs_early(n)
            for copy in rs_main(n)[1]:
                copy.start()

    def rs_3(n):
        p = order[n]
        if p:
            g = grad_piece(p, core)
            total, give = sum_z_end(n, 2, 5, *diagonal(n))
            add_to(g, (zpos, xy_d, rows_two), total)
            give()
            credit_wait(n, 2)
            rs_two(n).start()
            rs_early(n)
            for copy in rs_main(n)[1]:
                copy.start()

    def rs_4(n):
        p = order[n]
        if p:
            g = grad_piece(p, core)
            (a_dev, a), (b_dev, b) = sides(n)
            rs_two(n).wait_recv()
            add_to(g, (zpos, b, rows_two), r.lt[n % RINGS["lt"]])
            credit_give(n, 2, a_dev)
            for copy in rs_main(n)[2]:
                copy.start()

    def rs_5(n):
        p = order[n]
        g, l2 = grad_piece(p, core), rs_bufs(n)[2]
        (a_dev, a), (b_dev, b) = sides(n)
        for copy in rs_all(n):
            copy.wait_recv()
        for z in range(4):
            add_to(g, (z, xy), l2[0, z].astype(F32) + l2[1, z].astype(F32))
        credit_give(n, 3, a_dev)
        credit_give(n, 4, b_dev)
        if n < SHORT:
            sum_z_start(n, 9, 9, *own_line(n))
        else:
            for k in (1, 2, 3):
                z_send(n, 9, *own_line(n), k).start()

    def rs_6(n):
        sum_z_pass(n, 9, 9, *own_line(n))

    def rs_7(n):
        p = order[n]
        if n < SHORT:
            total, give = sum_z_end(n, 9, 9, *own_line(n))
        else:
            land = rs_bufs(n)[3]
            for k in (1, 2, 3):
                z_send(n, 9, *own_line(n), k).wait_recv()
            total = land[0].astype(F32) + land[1].astype(F32) + land[2].astype(F32)
        total = total + grad_piece(p, core)[zpos, xy].astype(F32)
        if p == 0:
            r.osm[...] = total
        elif p >= 9:
            i, j = (p - 9) // 2, (p - 9) % 2
            r.o2[ROWS * i : ROWS * (i + 1), COLS * j : COLS * (j + 1)] = total
        else:
            r.fs[p - 1] = total
            rs_swap(n).start()
        if n < SHORT:
            give()

    def rs_8(n):
        p = order[n]
        if p == 0 or p >= 9:
            return
        mine = pl.ds(pl.multiple_of(core * 24, 8), 24)
        rs_swap(n).wait_recv()
        out, first = (r.oq, 0) if p <= 3 else ((r.op, 0) if p == 4 else (r.o1, p - 5))
        for g in range(3):
            lanes = slice(LANES * g, LANES * (g + 1))
            base = 768 * g + 256 * (p - 1) if p <= 3 else 768 * first + 256 * g
            out[:, pl.ds(pl.multiple_of(base + LANES * core, LANES), LANES)] = r.fs[
                p - 1, mine, lanes
            ]
            out[:, pl.ds(pl.multiple_of(base + LANES * other, LANES), LANES)] = r.fr[
                p - 1, :, lanes
            ]

    def rs_9(n):
        p = order[n]
        rs_copy(n, 0, grad_piece(p, other), rs_bufs(n)[0], sib).wait_send()
        rs_one(n).wait_send()
        for copy in rs_all(n):
            copy.wait_send()
        if n < SHORT:
            sum_z_sent(n, 2, *diagonal(n))
            rs_two(n).wait_send()
            sum_z_sent(n, 9, *own_line(n))
        else:
            for k in (1, 2, 3):
                z_send(n, 9, *own_line(n), k).wait_send()
        if 1 <= p <= 8:
            rs_swap(n).wait_send()

    rs_long = list(zip((rs_0, rs_1, rs_2, rs_3, rs_4, rs_5, rs_6, rs_7, rs_8, rs_9), LONG_AT))
    rs_short = list(zip((rs_0, rs_1, rs_2, rs_5, rs_7, rs_8, rs_9), SHORT_AT))

    rs_small = list(zip((rs_0, rs_1, rs_2, rs_5, rs_7, rs_8, rs_9), SMALL_AT))

    def rs_tick(tick):
        for n in range(PIECES + 1):
            for stage, after in rs_long if n < SHORT else rs_short if n < PIECES else rs_small:
                if STARTS[n] + after == tick:
                    stage(n)

    def rows_of(f):
        return pl.ds(pl.multiple_of(f * WIN, WIN), WIN)

    def loop(count, body, ticks=()):
        def step(i, carry):
            body(i)
            for k, tick in enumerate(ticks):
                if tick is not None:
                    pl.when(i == k)(tick)
            return carry

        lax.fori_loop(0, count, step, 0)

    def steps(fn, *numbers):
        return [functools.partial(fn, s) if s is not None else None for s in numbers]

    def natural(ref, lead, rows):
        parts = []
        for g in range(3):
            for h in range(2):
                parts.append(ref[(h, *lead, rows, pl.ds(LANES * g, LANES))])
        return parts

    def put(ref, lead, rows, value):
        for g in range(3):
            for h in range(2):
                at = 256 * g + LANES * h
                ref[(h, *lead, rows, pl.ds(LANES * g, LANES))] = value[:, at : at + LANES]

    def put_a(piece, rows, value):
        for g in range(3):
            for h in range(2):
                at = 256 * g + LANES * h
                r.gp[4 * h + piece, rows, LANES * g : LANES * (g + 1)] = value[:, at : at + LANES]

    def pre_rows(t, h, s):
        return pl.ds(pl.multiple_of((2 * t + h) * 1024 + s.start, 8), s.stop - s.start)

    def pre_tile(t, s):
        return jnp.concatenate([gp_m[pre_rows(t, h, s), :] for h in range(2)], axis=1)

    def mixed_in(f):
        rw = rows_of(f)
        return jnp.where(r.st[rw, 0:1] > 0, r.v24[6:7, :], r.tok[rw, :].astype(F32))

    def masks():
        bits = jnp.transpose(r.mask[...].astype(F32))
        for j in range(8):
            keep = 1.0 - r.pad[j // 2].astype(F32)
            col = bits[:, j : j + 1]
            r.st[LANES * j : LANES * (j + 1), 0:1] = col
            r.st[LANES * j : LANES * (j + 1), 1:2] = col * keep

    def mask_grad(f):
        rw = rows_of(f)
        r.dm[rw, :] = (r.dm[rw, :].astype(F32) * r.st[rw, 1:2]).astype(BF16)

    def spread_small():
        table = r.sv[...].reshape(32, 8, LANES)
        rows = [table[:, i, :].astype(BF16) for i in range(3)]
        at = 0
        for name, row, lane0, width in SMALL_ROWS:
            pick, owner = spread_tables(lane0, width)
            full = jnp.sum(jnp.where(owner, dot_nn(rows[row], pick), 0.0), axis=0, keepdims=True)
            if name == "qkv_bias":
                for t in range(3):
                    for g in range(3):
                        at_piece, at_whole = 768 * t + 256 * g, 768 * g + 256 * t
                        r.bqkv[:, at_piece : at_piece + 256] = full[:, at_whole : at_whole + 256]
            elif name == "fc1_bias":
                r.bfc1[...] = full
            else:
                r.v24[at : at + 1, :] = full
                at += 1
        r.gv[...] = jnp.zeros_like(r.gv)

    def collect_small():
        table = [jnp.zeros((32, LANES), F32) for _ in range(3)]
        at = 0
        for name, row, lane0, width in SMALL_ROWS:
            pick, owner = spread_tables(lane0, width)
            if name == "qkv_bias":
                chunks = [768 * t + 256 * g for g in range(3) for t in range(3)]
                full = jnp.concatenate([r.gbqkv[:, c : c + 256] for c in chunks], axis=1)
            elif name == "fc1_bias":
                full = r.gbfc1[...]
            else:
                full = r.gv[at : at + 1, :]
                at += 1
            parts = jnp.where(owner, full, 0.0)
            for _ in range(3):
                high = parts.astype(BF16)
                table[row] = table[row] + dot_nt(high, pick)
                parts = parts - high.astype(F32)
        flat = r.sg.reshape(256, LANES)
        r.sg[...] = jnp.zeros_like(r.sg)
        for i in range(3):
            flat[pl.ds(i, 32, stride=8), :] = table[i]

    def ln1(f):
        rw = rows_of(f)
        x = mixed_in(f)
        row_mean, row_scale = row_stats(x)
        r.st[rw, 2:3] = row_mean
        r.st[rw, 3:4] = row_scale
        r.normed[rw, :] = ((x - row_mean) * row_scale * r.v24[0:1, :] + r.v24[1:2, :]).astype(BF16)

    def qkv(t):
        w = jnp.concatenate(natural(wa_m, (t,), pl.ds(0, 768)), axis=1)
        cols = tile(t)
        bias = r.bqkv[:, cols]
        for i in range(4):
            s = slice(WIN * i, WIN * (i + 1))
            r.packed[s, cols] = (dot_nn(r.normed[s, :], w) + bias).astype(BF16)

    def part(t, i, pair):
        return pl.ds(pl.multiple_of(768 * t + 256 * i + LANES * pair, LANES), LANES)

    def head_cols(t, pair):
        return pl.ds(pl.multiple_of(256 * t + LANES * pair, LANES), LANES)

    low_lanes = lax.broadcasted_iota(jnp.int32, (WIN, LANES), 1) < HEAD_DIM

    def two_heads(a):
        z = jnp.zeros_like(a)
        return jnp.concatenate([jnp.where(low_lanes, a, z), jnp.where(low_lanes, z, a)], axis=0)

    def attention(t, f, pair):
        rw = rows_of(f)
        q2 = r.packed[rw, part(t, 0, pair)] * jnp.asarray(0.125, BF16)
        k2 = r.packed[rw, part(t, 1, pair)]
        v2 = r.packed[rw, part(t, 2, pair)]
        scores = dot_nt(two_heads(q2), k2)
        row_max = jnp.max(scores, axis=1, keepdims=True)
        e = jnp.exp(scores - row_max)
        total = jnp.sum(e, axis=1, keepdims=True)
        inv = 1.0 / total
        log_total = row_max + jnp.log(total)
        for h in range(2):
            col = jnp.broadcast_to(log_total[WIN * h : WIN * (h + 1)], (WIN, 8))
            r.lse[pl.ds(f * 12 + 4 * t + 2 * pair + h, 1), :] = jnp.transpose(col)[0:1]
        e = e.astype(BF16)
        out = dot_nn(jnp.concatenate([e[:WIN], e[WIN:]], axis=1), two_heads(v2))
        scale = jnp.where(
            low_lanes,
            jnp.broadcast_to(inv[:WIN], (WIN, LANES)),
            jnp.broadcast_to(inv[WIN:], (WIN, LANES)),
        )
        r.att[rw, head_cols(t, pair)] = (out * scale).astype(BF16)

    def heads_forward(t, between):
        qkv(t)
        for f in range(4):
            for pair in range(2):
                attention(t, f, pair)
            if f == 1:
                for k, tick in enumerate(between):
                    if tick is not None:
                        pl.when(t == k)(tick)

    def project(f):
        rw = rows_of(f)
        w = jnp.concatenate(natural(wa_m, (3,), pl.ds(0, 768)), axis=1)
        middle = mixed_in(f) + (dot_nn(r.att[rw, :], w) + r.v24[2:3, :])
        r.mid[rw, :] = middle
        row_mean, row_scale = row_stats(middle)
        r.st[rw, 4:5] = row_mean
        r.st[rw, 5:6] = row_scale
        r.n2[rw, :] = ((middle - row_mean) * row_scale * r.v24[3:4, :] + r.v24[4:5, :]).astype(BF16)

    def tile(t):
        return pl.ds(pl.multiple_of(t * 768, 768), 768)

    def fc1(t):
        w = jnp.concatenate(natural(w1_m, (t,), pl.ds(0, 768)), axis=1)
        cols = tile(t)
        bias = r.bfc1[:, cols]
        for i in range(4):
            s = slice(WIN * i, WIN * (i + 1))
            act, slope = gelu_and_slope(dot_nn(r.n2[s, :], w) + bias)
            r.hact[s, cols] = act.astype(BF16)
            slope = slope.astype(BF16)
            gp_m[pre_rows(t, 0, s), :] = slope[:, :COLS]
            gp_m[pre_rows(t, 1, s), :] = slope[:, COLS:]

    def turn(src):
        def body(f):
            rw = rows_of(f)
            r.tr[:, rw] = r.normed[rw, :].T if src == 0 else r.n2[rw, :].T

        return body

    def fc2(n):
        cols = pl.ds(pl.multiple_of(n * 256, 256), 256)
        parts = []
        for i in range(2):
            g = 2 * n + i
            lanes = pl.ds(pl.multiple_of(lax.rem(g, 3) * LANES, LANES), LANES)
            parts.append(w2_m[lax.div(g, 3), :, lanes])
        w = jnp.concatenate(parts, axis=1)
        for i in range(4):
            s = slice(WIN * i, WIN * (i + 1))
            r.n2[s, cols] = (
                dot_nn(r.hact[s, :], w) + (r.mid[s, cols] + r.v24[5:6, cols])
            ).astype(BF16)

    def grad_fc2(t):
        cols = tile(t)
        g = dot_tn(r.hact[:, cols], r.dm[...]).astype(BF16)
        g2_m[0, cols, :] = g[:, :COLS]
        g2_m[1, cols, :] = g[:, COLS:]

    def grad_pre(t):
        cols = tile(t)
        w = jnp.concatenate([w2_m[0, cols, :], w2_m[1, cols, :]], axis=1)
        sums = jnp.zeros((1, 768), F32)
        for i in range(4):
            s = slice(WIN * i, WIN * (i + 1))
            d = (dot_nt(r.dm[s, :], w) * pre_tile(t, s).astype(F32)).astype(BF16)
            gp_m[pre_rows(t, 0, s), :] = d[:, :COLS]
            gp_m[pre_rows(t, 1, s), :] = d[:, COLS:]
            sums = sums + jnp.sum(d.astype(F32), axis=0, keepdims=True)
        r.gbfc1[:, cols] = sums

    def grad_fc1(t):
        put(w1_m, (t,), pl.ds(0, 768), dot_nn(r.tr[...], pre_tile(t, slice(0, 1024))).astype(BF16))

    def grad_norm_two(n):
        rw = rows_of(n)
        parts = []
        for t in range(4):
            parts += natural(w1_m, (t,), rw)
        w = jnp.concatenate(parts, axis=1)
        for i in range(4):
            s = slice(WIN * i, WIN * (i + 1))
            pre = jnp.concatenate([pre_tile(t, s) for t in range(4)], axis=1)
            r.dn[s, rw] = dot_nt(pre, w)

    def grad_middle(f):
        rw = rows_of(f)
        dy = r.dm[rw, :].astype(F32)
        dx, gain, shift = norm_backward(
            r.mid[rw, :], r.st[rw, 4:5], r.st[rw, 5:6], r.dn[rw, :], r.v24[3:4, :]
        )
        d = dy + dx
        low = d.astype(BF16)
        r.mid[rw, :] = d
        r.dm[rw, :] = low
        r.gv[3:4, :] += gain
        r.gv[4:5, :] += shift
        r.gv[5:6, :] += jnp.sum(dy, axis=0, keepdims=True)
        r.gv[2:3, :] += jnp.sum(low.astype(F32), axis=0, keepdims=True)

    def grad_proj(j):
        rw = rows_of(j)
        put_a(3, rw, dot_tn(r.att[:, rw], r.dm[...]).astype(BF16))

    def grad_att(f):
        rw = rows_of(f)
        w = jnp.concatenate(natural(wa_m, (3,), pl.ds(0, 768)), axis=1)
        r.n2[rw, :] = dot_nt(r.dm[rw, :], w).astype(BF16)

    def attention_backward(t, f, pair):
        rw = rows_of(f)
        q2 = r.packed[rw, part(t, 0, pair)] * jnp.asarray(0.125, BF16)
        k2 = r.packed[rw, part(t, 1, pair)]
        v2 = r.packed[rw, part(t, 2, pair)]
        qs, ds, ks = two_heads(q2), two_heads(r.n2[rw, head_cols(t, pair)]), two_heads(k2)
        at = f * 12 + 4 * t + 2 * pair
        log_total = jnp.concatenate([r.lse[pl.ds(at + h, 1), :] for h in range(2)], axis=1)
        probs = jnp.exp(dot_nt(k2, qs) - log_total)
        prod = probs * dot_nt(v2, ds)
        row_dot = jnp.sum(prod, axis=0, keepdims=True)
        d_scores = (prod - probs * row_dot).astype(BF16)
        r.packed[rw, part(t, 2, pair)] = dot_nn(probs.astype(BF16), ds).astype(BF16)
        r.packed[rw, part(t, 1, pair)] = dot_nn(d_scores, qs).astype(BF16)
        stacked = jnp.concatenate([d_scores[:, :WIN], d_scores[:, WIN:]], axis=0)
        r.packed[rw, part(t, 0, pair)] = (dot_tn(stacked, ks) * 0.125).astype(BF16)

    def heads_backward(t):
        def body(f):
            for pair in range(2):
                attention_backward(t, f, pair)

        return body

    def grad_qkv(t):
        cols = tile(t)
        d = r.packed[:, cols]
        put_a(t, slice(None), dot_nn(r.tr[...], d).astype(BF16))
        r.gbqkv[:, cols] = jnp.sum(d.astype(F32), axis=0, keepdims=True)

    def grad_norm_one(n):
        rw = rows_of(n)
        parts = []
        for t in range(3):
            parts += natural(wa_m, (t,), rw)
        w = jnp.concatenate(parts, axis=1)
        for i in range(4):
            s = slice(WIN * i, WIN * (i + 1))
            r.dn[s, rw] = dot_nt(r.packed[s, :], w)

    def grad_mixed(f):
        rw = rows_of(f)
        dx, gain, shift = norm_backward(
            mixed_in(f), r.st[rw, 2:3], r.st[rw, 3:4], r.dn[rw, :], r.v24[0:1, :]
        )
        d = r.mid[rw, :] + dx
        chosen = r.st[rw, 0:1] > 0
        r.dn[rw, :] = jnp.where(chosen, 0.0, d)
        r.gv[0:1, :] += gain
        r.gv[1:2, :] += shift
        r.gv[6:7, :] += jnp.sum(jnp.where(chosen, d, 0.0), axis=0, keepdims=True)

    loads = [
        pltpu.make_async_copy(r.og_in, r.dm, r.ld.at[0]),
        pltpu.make_async_copy(r.tok_in, r.tok, r.ld.at[1]),
    ]
    for q in range(2):
        loads.append(
            pltpu.make_async_copy(
                r.s2w.at[:, pl.ds(COLS * q, COLS)], w2_shard.at[q, zpos, xy, core], r.ld.at[2 + q]
            )
        )
    loads.append(pltpu.make_async_copy(r.small, r.sv.at[zpos, xy, core], r.ld.at[4]))
    for copy in loads:
        copy.start()

    for land in (r.lz, r.l3):
        for slot in range(land.shape[0]):
            land[slot, 0] = jnp.zeros_like(land[slot, 0])
            land[slot, 2] = jnp.zeros_like(land[slot, 2])

    barrier = pltpu.get_barrier_semaphore()
    peers = [sib, x_dev, y_dev, z_dev(1), z_dev(2), z_dev(3)]
    for dev in peers:
        pl.semaphore_signal(barrier, inc=1, device_id=(dev,), device_id_type=MESH_ID)

    def shard_half(t, half):
        ref, first = (r.sq, 0) if t < 3 else ((r.sp, 0) if t == 3 else (r.s1w, t - 4))
        parts = []
        for g in range(3):
            base = 768 * g + 256 * t if t < 3 else 768 * first + 256 * g
            a = ref[:, base : base + LANES].astype(F32)
            b = ref[:, base + LANES : base + 2 * LANES].astype(F32)
            parts.append(jnp.where(half == 0, a, b))
        return jnp.concatenate(parts, axis=1)

    for t in range(8):
        away = jnp.concatenate([shard_half(t, other), jnp.zeros((8, COLS), F32)], axis=0)
        r.l0[0, t // 4, t % 4, 0:32] = away.astype(BF16)
    pl.semaphore_wait(barrier, len(peers))
    away, came = [r.l0.at[i, pl.ds(0, 2), :, pl.ds(0, 32)] for i in range(2)]
    swap = remote(away, came, r.prep.at[0], r.prep.at[1], sib)
    swap.start()
    loads[4].wait()
    ag_a(0)
    swap.wait()
    for t in range(8):
        here = shard_half(t, core)
        there = r.l0[1, t // 4, t % 4, 0:32].astype(F32)[:24]
        block = jnp.concatenate(
            [jnp.where(core == 0, here, there), jnp.where(core == 0, there, here)], axis=0
        ).astype(BF16)
        if t < 4:
            wa_v[core, t, zpos, xy] = block
        else:
            w1_v[core, t - 4, zpos, xy] = block
        if t + 1 < ahead:
            ag_a(t + 1)
    ag_step(-1)
    loads[2].wait()
    loads[3].wait()
    def ag(*numbers):
        def go():
            for s in numbers:
                ag_step(s)

        return go

    def rs(*numbers):
        def go():
            for s in numbers:
                rs_tick(s)

        return go

    def arrive(p, *numbers):
        def go():
            ag(*numbers)()
            ag_e(p)

        return go

    ag_step(0)
    masks()
    ag_step(1)
    loads[0].wait()
    loop(4, mask_grad)
    ag_step(2)
    ag_e(0)
    ag_step(3)
    loads[1].wait()
    spread_small()
    loop(4, ln1)
    ag_e(1)
    loop(
        3,
        functools.partial(heads_forward, between=[ag(4), ag(6), ag(8)]),
        [arrive(2, 5), arrive(3, 7), arrive(4, 9)],
    )
    loop(4, project, [None, ag(10), None, None])
    keep_middle = pltpu.make_async_copy(r.mid, r.ig, r.ld.at[5])
    keep_middle.start()
    ag_e(5)
    loop(4, fc1, [arrive(6, 11), arrive(7), arrive(8, 12), ag(13)])
    loop(4, turn(1))
    for p in range(9):
        ag_f(p)
    loop(4, grad_fc2, [None, ag(14), None, None])
    rs_tick(0)
    for p in range(9, PIECES + 1):
        ag_e(p)
        ag_f(p)
    loop(4, grad_pre, [rs(1), rs(2), rs(3), rs(4)])
    loop(3, grad_norm_two, [rs(5), rs(6), rs(7)])
    loop(4, grad_fc1, [rs(8), rs(9), rs(10), rs(11)])
    keep_middle.wait()
    loop(4, grad_middle, [None, rs(12), None, rs(13)])
    loop(3, grad_proj)
    rs_tick(14)
    loop(4, grad_att)
    rs_tick(15)
    loop(4, turn(0))
    loop(4, heads_backward(0), [rs(16), rs(17), rs(18), rs(19)])
    grad_qkv(0)
    rs_tick(20)
    loop(4, heads_backward(1), [rs(21), rs(22), rs(23), rs(24)])
    grad_qkv(1)
    rs_tick(25)
    loop(4, heads_backward(2), [rs(26), rs(27), rs(28), rs(29)])
    grad_qkv(2)
    rs_tick(30)
    loop(3, grad_norm_one, [rs(31), rs(32), rs(33)])
    loop(4, grad_mixed, [None, rs(34), None, rs(35)])
    load_middle = pltpu.make_async_copy(r.ig, r.mid, r.ld.at[6])
    load_middle.start()
    collect_small()
    rs_tick(36)
    load_middle.wait()
    write_grad = pltpu.make_async_copy(r.dn, r.ig, r.ld.at[7])
    write_grad.start()
    rs_tick(37)
    loop(3, fc2, [rs(38, 39), rs(40, 41), rs(42, 43)])
    write_out = pltpu.make_async_copy(r.n2, r.bo, r.ld.at[0])
    write_out.start()
    last = max(at + (LONG_AT if n < SHORT else SHORT_AT)[-1] for n, at in enumerate(STARTS))
    for tick in range(44, last + 1):
        rs_tick(tick)
    write_grad.wait()
    write_out.wait()


HAND_PARTS = 4


def hand_over(*refs):
    arrays, small, outs = refs[:6], refs[6], refs[7:13]
    vectors, held, (in_sems, out_sems) = refs[13:-8], refs[-8:-2], refs[-2:]
    loads, stores = [], []
    for src, buf, dst in zip(arrays, held, outs):
        parts = HAND_PARTS if src.shape[0] == 1024 else 1
        rows = src.shape[0] // parts
        for i in range(parts):
            at, n = pl.ds(rows * i, rows), len(loads)
            loads.append(pltpu.make_async_copy(src.at[at], buf.at[at], in_sems.at[n]))
            stores.append(pltpu.make_async_copy(buf.at[at], dst.at[at], out_sems.at[n]))
    for copy in loads:
        copy.start()
    for ref, (_, row, lane0, width) in zip(vectors, SMALL_ROWS):
        ref[...] = small[row : row + 1, lane0 : lane0 + width]
    for load, store in zip(loads, stores):
        load.wait()
        store.start()
    for copy in stores:
        copy.wait()


def fused_device(
    tokens,
    mask_bits,
    pad_flags,
    ln1_gain,
    ln1_bias,
    qkv_weight,
    qkv_bias,
    proj_weight,
    proj_bias,
    ln2_gain,
    ln2_bias,
    fc1_weight,
    fc1_bias,
    fc2_weight,
    fc2_bias,
    mask_embed,
    out_grad,
):
    held = dict(
        ln1_gain=ln1_gain,
        ln1_bias=ln1_bias,
        proj_bias=proj_bias,
        ln2_gain=ln2_gain,
        ln2_bias=ln2_bias,
        fc2_bias=fc2_bias,
        mask_embed=mask_embed,
        qkv_bias=qkv_bias,
        fc1_bias=fc1_bias,
    )
    small = jnp.zeros((8 * LANES,), F32)
    for name, row, lane0, width in SMALL_ROWS:
        first = row * LANES + lane0
        small = small + jnp.pad(held[name].astype(F32), (first, 8 * LANES - first - width))
    small = small.reshape(8, LANES)
    any_spec = pl.BlockSpec(memory_space=pl.ANY)
    vmem = pl.BlockSpec(memory_space=pltpu.VMEM)
    smem = pl.BlockSpec(memory_space=pltpu.SMEM)
    shape = jax.ShapeDtypeStruct
    outs = pl.pallas_call(
        fused_kernel,
        out_shape=(
            shape((1024, 768), BF16),
            shape((1024, 768), F32),
            shape((24, 2304), F32),
            shape((24, 768), F32),
            shape((24, 3072), F32),
            shape((96, 768), F32),
            shape((8, LANES), F32),
        ),
        in_specs=[any_spec, any_spec, vmem, smem, any_spec, vmem, vmem, vmem, any_spec],
        out_specs=(any_spec, any_spec, vmem, vmem, vmem, vmem, vmem),
        scratch_shapes=[pltpu.VMEM(*spec) for spec in SCRATCH.values()] + list(SEMS.values()),
        compiler_params=pltpu.CompilerParams(
            collective_id=0, has_side_effects=True, vmem_limit_bytes=64 * 2**20
        ),
    )(
        tokens,
        out_grad,
        mask_bits.reshape(8, LANES),
        pad_flags,
        small,
        qkv_weight,
        proj_weight,
        fc1_weight,
        fc2_weight,
    )
    held = pl.pallas_call(
        hand_over,
        out_shape=tuple(shape(o.shape, o.dtype) for o in outs[:6])
        + tuple(shape((1, width), F32) for _, _, _, width in SMALL_ROWS),
        in_specs=[any_spec] * 6 + [vmem],
        out_specs=(any_spec,) * 6 + (vmem,) * len(SMALL_ROWS),
        scratch_shapes=[pltpu.VMEM(o.shape, o.dtype) for o in outs[:6]]
        + [pltpu.SemaphoreType.DMA((6 * HAND_PARTS,)), pltpu.SemaphoreType.DMA((6 * HAND_PARTS,))],
        compiler_params=pltpu.CompilerParams(vmem_limit_bytes=63 * 2**20),
    )(*outs)
    block_out, input_grad, gq, gpj, g1, g2 = held[:6]
    v = {entry[0]: vec.reshape(entry[3]) for entry, vec in zip(SMALL_ROWS, held[6:])}
    return (
        block_out,
        input_grad,
        v["ln1_gain"],
        v["ln1_bias"],
        gq,
        v["qkv_bias"],
        gpj,
        v["proj_bias"],
        v["ln2_gain"],
        v["ln2_bias"],
        g1,
        v["fc1_bias"],
        g2,
        v["fc2_bias"],
        v["mask_embed"],
    )


def solution(mesh):
    placed = (
        P("fsdp", None),
        P("fsdp"),
        P("fsdp"),
        P("fsdp"),
        P("fsdp"),
        P("fsdp", None),
        P("fsdp"),
        P("fsdp", None),
        P("fsdp"),
        P("fsdp"),
        P("fsdp"),
        P("fsdp", None),
        P("fsdp"),
        P("fsdp", None),
        P("fsdp"),
        P("fsdp"),
        P("fsdp", None),
    )
    return jax.shard_map(
        fused_device if mesh.shape["fsdp"] == 32 else per_device,
        mesh=mesh,
        in_specs=placed,
        out_specs=(
            P("fsdp", None),
            P("fsdp", None),
            P("fsdp"),
            P("fsdp"),
            P("fsdp", None),
            P("fsdp"),
            P("fsdp", None),
            P("fsdp"),
            P("fsdp"),
            P("fsdp"),
            P("fsdp", None),
            P("fsdp"),
            P("fsdp", None),
            P("fsdp"),
            P("fsdp"),
        ),
        check_vma=False,
    )
```
